32 devices in a mesh: gx: 8 (over z, core), gy: 4 (over y, x).
Axes of the slice: x: 2, y: 2, z: 4, core: 2. Of those that a mesh axis runs over, the one named last changes fastest.
Arguments:
- mean_field: float32 [128, 256, 128], P('gx', 'gy'), may hold values from -3 to 3
- log_scale: float32 [128, 256, 128], P('gx', 'gy'), may hold values from -2.5 to -0.7
- noise: float32 [128, 256, 128], P('gx', 'gy'), may hold values from -6 to 6
- wave_prev: float32 [128, 256, 128], P('gx', 'gy'), may hold values from -6 to 6
- wave_now: float32 [128, 256, 128], P('gx', 'gy'), may hold values from -6 to 6
- adjoint_next: float32 [128, 256, 128], P('gx', 'gy'), may hold values from -6 to 6
- adjoint_now: float32 [128, 256, 128], P('gx', 'gy'), may hold values from -6 to 6
- sources: int32 [16, 3], replicated, may hold values from 0 to 255, as said below
- receivers: int32 [256, 3], replicated, may hold values from 0 to 255, as said below
- observed: float32 [256], replicated, may hold values from -6 to 6
- step_index: int32 [1], replicated, may hold values from 0 to 47
- prior_scale: float32 [1], replicated, may hold values from 0.5 to 2
Outputs:
- wave_next: float32 [128, 256, 128], P('gx', 'gy')
- adjoint_prev: float32 [128, 256, 128], P('gx', 'gy')
- search: float32 [128, 256, 128], P('gx', 'gy')
- logscale_grad: float32 [128, 256, 128], P('gx', 'gy')
The draws below stay inside these ranges and needn't reach their ends.
Inputs may be any that keep to these rules, and one draw needn't show every extreme that they name: `sources`: each row gives the first, second and depth cell of a point, below 128, 256 and 128; points may coincide. `receivers`: each row gives the first, second and depth cell of a point, below 128, 256 and 128; points may coincide.
All inputs are finite; a program needn't handle non-finite values.
Results may differ from the reference program's by a relative error of at most 0.000075.
Values sent between devices are 32-bit elements; how exact they have to be, the bound alone decides.
A program may use at most 64 MiB of HBM per device.

```python
import math
import jax
import jax.numpy as jnp
from jax import lax

NZ = 128
NSRC = 16
NREC = 256
NSTEPS = 48
NX = 128
NY = 256


def scatter_points(key, number):
    pieces = jax.random.split(key, 3)
    across = jax.random.randint(pieces[0], (number,), 0, NX)
    lateral = jax.random.randint(pieces[1], (number,), 0, NY)
    levels = jax.random.randint(pieces[2], (number,), 0, NZ)
    ordinal = lax.iota(jnp.int32, number)
    across = jnp.where(ordinal == 0, NX - 1, across)
    lateral = jnp.where(ordinal == 1, NY - 1, lateral)
    levels = jnp.where(ordinal == 0, 0, levels)
    levels = jnp.where(ordinal == 1, NZ - 1, levels)
    return jnp.stack([across, lateral, levels], axis=1).astype(jnp.int32)


def draw_sources(key, part):
    return scatter_points(jax.random.fold_in(key, 11), NSRC)


def draw_receivers(key, part):
    return scatter_points(jax.random.fold_in(key, 23), NREC)


def block_scale(stream_key, extent, cuts, low, largest):
    loudness = 1.0
    for axis_at, shards_of in cuts:
        draws = jax.random.uniform(jax.random.fold_in(jax.random.fold_in(stream_key, 6), axis_at), (shards_of,), jnp.float32, low / len(cuts), largest / len(cuts))
        loudness = loudness * jnp.repeat(jnp.exp(draws), extent[axis_at] // shards_of).reshape((-1,) + (1,) * (len(extent) - 1 - axis_at))
    return loudness


def centred(rng, shape, scale, bound, cuts=(), held_as=jnp.bfloat16):
    loudness = block_scale(rng, shape, cuts, -0.22, 0.18) if cuts else 1.0
    array = jax.random.normal(rng, shape, jnp.float32) * scale * loudness
    return jnp.minimum(jnp.maximum(array, -bound), bound).astype(held_as)


def setup_inputs(seed: int = 0) -> dict:
    arg_keys = jax.random.split(jax.random.key(seed), 13)
    mean_field = centred(arg_keys[0], (NX, NY, NZ), 0.5, 3.0, ((0, 8), (1, 4)), jnp.float32)
    log_scale = jnp.clip(-2.5 + 1.8 * jax.random.uniform(arg_keys[1], (NX, NY, NZ), jnp.float32) ** block_scale(arg_keys[1], (NX, NY, NZ), ((0, 8), (1, 4)), -0.2, 0.2), -2.5, -0.7)
    noise = centred(arg_keys[2], (NX, NY, NZ), 1.0, 6.0, ((0, 8), (1, 4)), jnp.float32)
    wave_prev = centred(arg_keys[3], (NX, NY, NZ), 1.0, 6.0, ((0, 8), (1, 4)), jnp.float32)
    wave_now = centred(arg_keys[4], (NX, NY, NZ), 1.0, 6.0, ((0, 8), (1, 4)), jnp.float32)
    adjoint_next = centred(arg_keys[5], (NX, NY, NZ), 1.0, 6.0, ((0, 8), (1, 4)), jnp.float32)
    adjoint_now = centred(arg_keys[6], (NX, NY, NZ), 1.0, 6.0, ((0, 8), (1, 4)), jnp.float32)
    sources = draw_sources(jax.random.fold_in(arg_keys[12], 71), 0)
    receivers = draw_receivers(jax.random.fold_in(arg_keys[12], 71), 0)
    observed = centred(arg_keys[9], (NREC,), 1.0, 6.0, (), jnp.float32)
    step_index = jax.random.randint(arg_keys[10], (1,), 0, NSTEPS).astype(jnp.int32)
    prior_scale = jnp.clip(jnp.exp(jax.random.uniform(arg_keys[11], (1,), jnp.float32, math.log(0.5), math.log(2.0))), 0.5, 2.0)
    return dict(mean_field=mean_field, log_scale=log_scale, noise=noise, wave_prev=wave_prev, wave_now=wave_now, adjoint_next=adjoint_next, adjoint_now=adjoint_now, sources=sources, receivers=receivers, observed=observed, step_index=step_index, prior_scale=prior_scale)


STENCIL_WEIGHTS = (-205.0 / 72.0, 8.0 / 5.0, -1.0 / 5.0, 8.0 / 315.0, -1.0 / 560.0)
COURANT_SQUARED = 0.08
VELOCITY_GAIN = 0.2
PULSE_FREQUENCY = 0.05
PULSE_AMPLITUDE = 20.0

def shifted(padded, dimension, offset):
    result = padded
    for axis_number in range(3):
        anchor = 4 + offset if axis_number == dimension else 4
        length = padded.shape[axis_number] - 8
        result = lax.slice_in_dim(result, anchor, anchor + length, axis=axis_number)
    return result

def laplacian(field):
    padded = jnp.pad(field, 4)
    summed = 3.0 * STENCIL_WEIGHTS[0] * field
    for offset in range(1, 5):
        for dimension in range(3):
            summed = summed + STENCIL_WEIGHTS[offset] * (shifted(padded, dimension, offset) + shifted(padded, dimension, -offset))
    return summed

def inject(field, points, values):
    return field.at[points[:, 0], points[:, 1], points[:, 2]].add(values)

def wave_term(count, length):
    waves = jnp.arange(count, dtype=jnp.int32).astype(jnp.float32)
    sine = jnp.sin(waves * (math.pi / length))
    return (length / 8.0) ** 2 * 4.0 * sine * sine

def reference(mean_field, log_scale, noise, wave_prev, wave_now, adjoint_next, adjoint_now, sources, receivers, observed, step_index, prior_scale):
    spread = jnp.exp(log_scale)
    sample = mean_field + spread * noise
    speed = COURANT_SQUARED * jnp.exp(2.0 * VELOCITY_GAIN * sample)
    moment = (step_index[0] - NSTEPS // 2).astype(jnp.float32) * (math.pi * PULSE_FREQUENCY)
    pulse = PULSE_AMPLITUDE * (1.0 - 2.0 * moment * moment) * jnp.exp(-moment * moment)
    curved = laplacian(wave_now)
    wave_next = 2.0 * wave_now - wave_prev + speed * curved
    wave_next = inject(wave_next, sources, jnp.ones((NSRC,), jnp.float32) * pulse)
    misfit = wave_next[receivers[:, 0], receivers[:, 1], receivers[:, 2]] - observed
    adjoint_prev = 2.0 * adjoint_now - adjoint_next + laplacian(speed * adjoint_now)
    adjoint_prev = inject(adjoint_prev, receivers, misfit)
    data_grad = 2.0 * VELOCITY_GAIN * speed * adjoint_prev * curved
    half_depth = NZ // 2 + 1
    denominator = 1.0 + wave_term(NX, NX)[:, None, None] + wave_term(NY, NY)[None, :, None] + wave_term(half_depth, NZ)[None, None, :]
    gain = prior_scale[0] * (math.sqrt(NX * NY * NZ) / 8.0) / denominator
    spectrum = jnp.fft.rfftn(data_grad)
    smooth = jnp.fft.irfftn(spectrum * gain, s=(NX, NY, NZ))
    search = smooth.astype(jnp.float32) + sample
    logscale_grad = data_grad * spread * noise - 1.0
    return (wave_next, adjoint_prev, search, logscale_grad)
```

```python
import functools
import math

import jax
import jax.numpy as jnp
import ml_dtypes
import numpy as np
from jax import lax
from jax.experimental import pallas as pl
from jax.experimental.pallas import tpu as pltpu
from jax.sharding import PartitionSpec as P

NSTEPS = 48
STENCIL_WEIGHTS = (-205.0 / 72.0, 8.0 / 5.0, -1.0 / 5.0, 8.0 / 315.0, -1.0 / 560.0)
COURANT_SQUARED = 0.08
VELOCITY_GAIN = 0.2
PULSE_FREQUENCY = 0.05
PULSE_AMPLITUDE = 20.0

REACH = 4
PAD = 8
LANES = 128
CHUNKS = 1
MESH = pl.DeviceIdType.MESH
F32 = jnp.float32
BF16 = jnp.bfloat16
NN = (((1,), (0,)), ((), ()))
NT = (((1,), (1,)), ((), ()))


def halves(table):
    high = table.astype(ml_dtypes.bfloat16)
    low = (table - high.astype(np.float64)).astype(ml_dtypes.bfloat16)
    return np.stack([high, low])


def cas(length):
    index = np.arange(length)
    angle = (index[:, None] * index[None, :] % length) * (2.0 * math.pi / length)
    return np.cos(angle) + np.sin(angle)


def wave_term(length):
    return (length / 8.0) ** 2 * 4.0 * np.sin(np.arange(length) * (math.pi / length)) ** 2


def tables(bx, by, nz, nxp, nyp, chunks):
    total_x, total_y = bx * nxp, by * nyp
    along_z = np.zeros((nz, nz))
    for o in range(1, REACH + 1):
        along_z += STENCIL_WEIGHTS[o] * (np.eye(nz, k=o) + np.eye(nz, k=-o))
    face_low = np.zeros((REACH, REACH))
    face_high = np.zeros((REACH, REACH))
    for i in range(REACH):
        for h in range(REACH):
            if h >= i:
                face_low[i, h] = STENCIL_WEIGHTS[i + REACH - h]
            if h <= i:
                face_high[i, h] = STENCIL_WEIGHTS[REACH + h - i]
    faces = np.stack([np.kron(np.eye(bx), face_low), np.kron(np.eye(bx), face_high)])
    pair = LANES // by
    weights_y = cas(total_y).reshape(nyp, by, total_y)
    forward_y = np.zeros((nyp, pair, by, pair, total_y))
    for s in range(pair):
        forward_y[:, s, :, s, :] = weights_y
    forward_y = forward_y.reshape(nyp * LANES, pair * total_y)
    c = (total_x / 8.0) ** 2
    d = 1.0 + wave_term(nz)[:, None] + wave_term(total_y)[None, :]
    log_r = -2.0 * np.arcsinh(0.5 * np.sqrt(d / c))
    r = np.exp(log_r)
    scale = math.sqrt(total_x * total_y * nz) / 8.0 / (nz * total_y)
    scale = scale / (c * -2.0 * np.sinh(log_r))
    closure = 1.0 / -np.expm1(total_x * log_r)
    share = nz // nyp
    sub = share // chunks
    tiles = total_y // LANES
    rows = sub * tiles // nxp
    segment = np.stack([np.exp(bx * log_r), closure])
    segment = segment.reshape(2, nyp, chunks, nxp // tiles, rows, tiles, LANES)
    segment = segment.transpose(1, 2, 3, 5, 0, 4, 6).reshape(nyp, chunks, nxp, 2, rows, LANES)
    as32 = lambda a: np.ascontiguousarray(a).astype(np.float32)
    return (
        as32(along_z),
        as32(faces),
        halves(cas(nz)),
        halves(forward_y),
        halves(forward_y.T),
        as32(np.stack([r, scale]).reshape(2, nyp, share, total_y)),
        as32(segment),
    )


def split(x):
    high = x.astype(BF16)
    return high, (x - high.astype(F32)).astype(BF16)


def split3(x):
    high = x.astype(BF16)
    rest = x - high.astype(F32)
    mid = rest.astype(BF16)
    return high, mid, (rest - mid.astype(F32)).astype(BF16)


def dot(a, b, dims=NN):
    return lax.dot_general(a, b, dims, preferred_element_type=F32)


def dot3(x, w):
    high, low = split(x)
    return dot(high, w[0]) + dot(high, w[1]) + dot(low, w[0])


def exact(a, b):
    return lax.dot_general(a, b, NN, precision=lax.Precision.HIGHEST, preferred_element_type=F32)


def kernel(
    nxp,
    nyp,
    chunks,
    mean_h,
    scale_h,
    noise_h,
    prev_h,
    now_h,
    anext_h,
    anow_h,
    src_row,
    src_col,
    rec_row,
    rec_col,
    observed,
    step,
    prior,
    along_z,
    faces,
    cas_z,
    fwd_y,
    inv_y,
    line_tab,
    seg_tab,
    wave_o,
    adj_o,
    search_o,
    lgrad_o,
    mean,
    logs,
    noise,
    prev,
    anext,
    anow,
    wpad,
    bpad,
    curl,
    acurl,
    speed,
    xrecv,
    ysend,
    yrecv,
    zsend,
    zrecv,
    lines,
    isend,
    irecv,
    msend,
    mrecv,
    rsend,
    rrecv,
    lsem,
    osem,
    xs,
    xr,
    ys,
    yr,
    zs,
    zr,
    ms,
    mr,
    rs,
    rr,
    vs,
    vr,
):
    bx, by, nz = mean.shape
    gx, gy = lax.axis_index("gx"), lax.axis_index("gy")
    pairs = bx * by // LANES
    pair = LANES // by
    share = nz // nyp
    sub = share // chunks
    total_y = by * nyp
    tiles = total_y // LANES
    rows = sub * tiles // nxp
    cells = bx * by
    centre = pl.ds(PAD, by)

    loads = [
        pltpu.make_async_copy(now_h, wpad.at[:, centre, :], lsem.at[0]),
        pltpu.make_async_copy(scale_h, logs, lsem.at[1]),
        pltpu.make_async_copy(noise_h, noise, lsem.at[2]),
        pltpu.make_async_copy(mean_h, mean, lsem.at[3]),
        pltpu.make_async_copy(anow_h, anow, lsem.at[4]),
        pltpu.make_async_copy(prev_h, prev, lsem.at[5]),
        pltpu.make_async_copy(anext_h, anext, lsem.at[6]),
    ]
    for load in loads:
        load.start()

    for padded in (wpad, bpad):
        padded[:, 0:PAD, :] = jnp.zeros((bx, PAD, nz), F32)
        padded[:, PAD + by : by + 2 * PAD, :] = jnp.zeros((bx, PAD, nz), F32)
    outside = ((gx == 0, gx == nxp - 1), (gy == 0, gy == nyp - 1))
    for side in range(2):

        @pl.when(outside[0][side])
        def _():
            for field in range(2):
                xrecv[field, side] = jnp.zeros(xrecv.shape[2:], F32)

        @pl.when(outside[1][side])
        def _():
            for field in range(2):
                yrecv[field, side] = jnp.zeros(yrecv.shape[2:], F32)

    barrier = pltpu.get_barrier_semaphore()
    for i in range(1, nxp):
        pl.semaphore_signal(
            barrier, inc=1, device_id={"gx": lax.rem(gx + i, nxp)}, device_id_type=MESH
        )
    for i in range(1, nyp):
        pl.semaphore_signal(
            barrier, inc=1, device_id={"gy": lax.rem(gy + i, nyp)}, device_id_type=MESH
        )
    pl.semaphore_wait(barrier, nxp + nyp - 2)

    def rim_copy(axis, field, side, src):
        me, count = ((gx, nxp), (gy, nyp))[axis]
        target = lax.rem(me + (1 if side == 0 else count - 1), count)
        land, send, recv = ((xrecv, xs, xr), (yrecv, ys, yr))[axis]
        return pltpu.make_async_remote_copy(
            src_ref=src,
            dst_ref=land.at[field, side],
            send_sem=send.at[field, side],
            recv_sem=recv.at[field, side],
            device_id={("gx", "gy")[axis]: target},
            device_id_type=MESH,
        )

    def start_rim(axis, field, side, src):
        copy = rim_copy(axis, field, side, src)

        @pl.when(jnp.logical_not(outside[axis][1 - side]))
        def _():
            copy.start()

        return (axis, side, copy)

    rims = []
    rims.append(start_rim(0, 0, 0, now_h.at[pl.ds(bx - REACH, REACH)]))
    rims.append(start_rim(0, 0, 1, now_h.at[pl.ds(0, REACH)]))

    def pack_faces(field, padded):
        for x in range(bx):
            here = pl.ds(REACH * x, REACH)
            ysend[field, 0, here, :] = padded[x, PAD + by - REACH : PAD + by, :]
            ysend[field, 1, here, :] = padded[x, PAD : PAD + REACH, :]
        for side in range(2):
            rims.append(start_rim(1, field, side, ysend.at[field, side]))

    loads[0].wait()
    pack_faces(0, wpad)

    for load in loads[1:5]:
        load.wait()

    def pointwise(x):
        turned = jnp.exp(logs[x]) * noise[x]
        sample = mean[x] + turned
        logs[x] = turned
        mean[x] = sample
        fast = COURANT_SQUARED * jnp.exp(2.0 * VELOCITY_GAIN * sample)
        speed[x] = fast
        bpad[x, centre, :] = fast * anow[x]

    for x in range(REACH):
        pointwise(x)
    rims.append(start_rim(0, 1, 1, bpad.at[pl.ds(0, REACH), centre, :]))
    for x in range(bx - REACH, bx):
        pointwise(x)
    rims.append(start_rim(0, 1, 0, bpad.at[pl.ds(bx - REACH, REACH), centre, :]))
    for x in range(REACH, bx - REACH):
        pointwise(x)
    pack_faces(1, bpad)

    def inner_laplacian(padded, out):
        for x0 in range(0, bx, REACH):
            block = padded[x0 : x0 + REACH, PAD : PAD + by, :].reshape(REACH * by, nz)
            depthwise = exact(block, along_z[...]).reshape(REACH, by, nz)
            for x in range(x0, x0 + REACH):
                total = depthwise[x - x0] + 3.0 * STENCIL_WEIGHTS[0] * padded[x, centre, :]
                for o in range(1, REACH + 1):
                    near = padded[x, PAD + o : PAD + o + by, :] + padded[x, PAD - o : PAD - o + by, :]
                    if x + o < bx:
                        near = near + padded[x + o, centre, :]
                    if x - o >= 0:
                        near = near + padded[x - o, centre, :]
                    total = total + STENCIL_WEIGHTS[o] * near
                out[x] = total

    inner_laplacian(wpad, curl)

    def codes(points):
        across = points[0:1, :] - gx * bx
        lateral = points[1:2, :] - gy * by
        inside = (across >= 0) & (across < bx) & (lateral >= 0) & (lateral < by)
        return jnp.where(inside, across * by + lateral, -1)

    src_code = codes(src_row)
    rec_code = codes(rec_row)

    def rim_terms(field, out):
        for side in range(2):
            terms = exact(faces[side], yrecv[field, side])
            first = 0 if side == 0 else by - REACH
            for x in range(bx):
                here = out[x, first : first + REACH, :]
                out[x, first : first + REACH, :] = here + terms[REACH * x : REACH * (x + 1), :]

    def x_rim(field, x):
        total = None
        for o in range(1, REACH + 1):
            if x - o < 0:
                term = STENCIL_WEIGHTS[o] * xrecv[field, 0, REACH + x - o]
                total = term if total is None else total + term
            if x + o >= bx:
                term = STENCIL_WEIGHTS[o] * xrecv[field, 1, x + o - bx]
                total = term if total is None else total + term
        return total

    def wait_rims(field_rims):
        for axis, side, copy in field_rims:

            @pl.when(jnp.logical_not(outside[axis][side]))
            def _():
                copy.wait_recv()

    inner_laplacian(bpad, acurl)
    loads[5].wait()
    loads[6].wait()

    wave_rims = rims[0:4]
    adj_rims = rims[4:8]
    wait_rims(wave_rims)
    rim_terms(0, curl)
    for x in range(bx):
        curved = curl[x]
        extra = x_rim(0, x)
        if extra is not None:
            curved = curved + extra
            curl[x] = curved
        prev[x] = 2.0 * wpad[x, centre, :] - prev[x] + speed[x] * curved

    moment = (step[...] - NSTEPS // 2).astype(F32) * (math.pi * PULSE_FREQUENCY)
    pulse = PULSE_AMPLITUDE * (1.0 - 2.0 * moment * moment) * jnp.exp(-moment * moment)
    nsrc, nrec = src_row.shape[1], rec_row.shape[1]
    src_level = (src_col[:, 2:3] == lax.broadcasted_iota(jnp.int32, (nsrc, nz), 1)).astype(F32)
    src_level = src_level.astype(BF16)
    rec_level = (rec_col[:, 2:3] == lax.broadcasted_iota(jnp.int32, (nrec, nz), 1)).astype(F32)
    rec_level = rec_level.astype(BF16)
    step_x = 4
    block = step_x * by
    picked = jnp.zeros((1, nrec), F32)
    for x0 in range(0, bx, step_x):
        cell = lax.broadcasted_iota(jnp.int32, (block, nsrc), 0) + x0 * by
        hit = (cell == src_code).astype(F32).astype(BF16)
        wave = prev[x0 : x0 + step_x].reshape(block, nz) + pulse * dot(hit, src_level)
        prev[x0 : x0 + step_x] = wave.reshape(step_x, by, nz)
        traces = sum(dot(part, rec_level, NT) for part in split3(wave))
        cell = lax.broadcasted_iota(jnp.int32, (block, nrec), 0) + x0 * by
        picked = picked + jnp.sum(
            jnp.where(cell == rec_code, traces, 0.0), axis=0, keepdims=True
        )
    wave_out = pltpu.make_async_copy(prev, wave_o, osem.at[0])
    wave_out.start()
    misfit = picked - observed[...]

    wait_rims(adj_rims)
    rim_terms(1, acurl)
    misfit_parts = split3(misfit)
    for x0 in range(0, bx, step_x):
        cell = lax.broadcasted_iota(jnp.int32, (block, nrec), 0) + x0 * by
        hit = cell == rec_code
        added = sum(
            dot(jnp.where(hit, part.astype(F32), 0.0).astype(BF16), rec_level)
            for part in misfit_parts
        ).reshape(step_x, by, nz)
        for x in range(x0, x0 + step_x):
            total = acurl[x]
            extra = x_rim(1, x)
            if extra is not None:
                total = total + extra
            adjoint = 2.0 * anow[x] - anext[x] + total + added[x - x0]
            anext[x] = adjoint
            grad = (2.0 * VELOCITY_GAIN) * speed[x] * adjoint * curl[x]
            acurl[x] = grad
            anow[x] = grad * logs[x] - 1.0

        high, low = split(acurl[x0 : x0 + step_x].reshape(block, nz))
        zsend[:, x0 * by : x0 * by + block] = (
            dot(cas_z[0], high, NT) + dot(cas_z[1], high, NT) + dot(cas_z[0], low, NT)
        )

    def z_copy(c, i):
        to = lax.rem(gy + i, nyp)
        return pltpu.make_async_remote_copy(
            src_ref=zsend.at[pl.ds(pl.multiple_of(to * share + c * sub, sub), sub), :],
            dst_ref=zrecv.at[c, gy],
            send_sem=zs.at[c, i],
            recv_sem=zr.at[c, i],
            device_id={"gy": to},
            device_id_type=MESH,
        )

    def own_z(c):
        zrecv[c, gy] = zsend[pl.ds(pl.multiple_of(gy * share + c * sub, sub), sub), :]

    z_copies = [[z_copy(c, i) for i in range(1, nyp)] for c in range(chunks)]
    for c in range(chunks):
        for copy in z_copies[c]:
            copy.start()
    adj_out = pltpu.make_async_copy(anext, adj_o, osem.at[1])
    adj_out.start()
    lgrad_out = pltpu.make_async_copy(anow, lgrad_o, osem.at[2])
    lgrad_out.start()
    for c in range(chunks):
        own_z(c)

    def ratio(c):
        return line_tab[0, gy, c * sub : (c + 1) * sub, :]

    def at(c, x):
        first = (x // pair) * sub
        left = (x % pair) * total_y
        return lines[c, first : first + sub, left : left + total_y]

    def segment(o):
        return (
            slice((o // tiles) * rows, (o // tiles + 1) * rows),
            slice((o % tiles) * LANES, (o % tiles + 1) * LANES),
        )

    def small_copy(src, dst, send, recv, c, i):
        to = lax.rem(gx + i, nxp)
        return pltpu.make_async_remote_copy(
            src_ref=src.at[c, to],
            dst_ref=dst.at[c, gx],
            send_sem=send.at[c, i],
            recv_sem=recv.at[c, i],
            device_id={"gx": to},
            device_id_type=MESH,
        )

    m_copies, r_copies, v_copies = [], [], []

    def lateral(c):
        for copy in z_copies[c]:
            copy.wait_recv()
        block = jnp.concatenate(
            [
                jnp.concatenate(
                    [zrecv[c, p, :, LANES * j : LANES * (j + 1)] for p in range(nyp)], axis=1
                )
                for j in range(pairs)
            ],
            axis=0,
        )
        lines[c] = dot3(block, fwd_y)
        r = ratio(c)
        up = at(c, 0)
        down = at(c, bx - 1)
        for x in range(1, bx):
            up = at(c, x) + r * up
            down = at(c, bx - 1 - x) + r * down
        for o in range(nxp):
            here = segment(o)
            msend[c, o, 0:rows, :] = up[here]
            msend[c, o, rows : 2 * rows, :] = down[here]
        copies = [small_copy(msend, mrecv, ms, mr, c, i) for i in range(1, nxp)]
        for copy in copies:
            copy.start()
        mrecv[c, gx] = msend[c, gx]
        m_copies.append(copies)

    def close(c):
        for copy in m_copies[c]:
            copy.wait_recv()
        decay = seg_tab[gy, c, gx, 0]
        closure = seg_tab[gy, c, gx, 1]
        ups = [mrecv[c, d, 0:rows, :] for d in range(nxp)]
        downs = [mrecv[c, d, rows : 2 * rows, :] for d in range(nxp)]
        up, down = ups[0], downs[nxp - 1]
        for d in range(1, nxp):
            up = ups[d] + decay * up
            down = downs[nxp - 1 - d] + decay * down
        up = up * closure
        down = down * closure
        for d in range(nxp):
            rsend[c, d, 0:rows, :] = up
            up = ups[d] + decay * up
        for d in range(nxp - 1, -1, -1):
            rsend[c, d, rows : 2 * rows, :] = down
            down = downs[d] + decay * down
        copies = [small_copy(rsend, rrecv, rs, rr, c, i) for i in range(1, nxp)]
        for copy in copies:
            copy.start()
        rrecv[c, gx] = rsend[c, gx]
        r_copies.append(copies)

    def back(c):
        for copy in r_copies[c]:
            copy.wait_recv()

        def whole(first):
            return jnp.concatenate(
                [
                    jnp.concatenate(
                        [rrecv[c, i * tiles + t, first : first + rows, :] for t in range(tiles)],
                        axis=1,
                    )
                    for i in range(nxp // tiles)
                ],
                axis=0,
            )

        r = ratio(c)
        gain = line_tab[1, gy, c * sub : (c + 1) * sub, :] * prior[...]
        up, down = whole(0), whole(rows)
        ups = []
        for x in range(bx):
            up = at(c, x) + r * up
            ups.append(up)
        for x in range(bx - 1, -1, -1):
            ahead = r * down
            here = at(c, x)
            down = here + ahead
            first = (x // pair) * sub
            left = (x % pair) * total_y
            lines[c, first : first + sub, left : left + total_y] = gain * (ups[x] + ahead)
        field = dot3(lines[c], inv_y)
        for p in range(nyp):
            isend[c, p] = field[:, LANES * p : LANES * (p + 1)]
        copies = []
        for i in range(1, nyp):
            to = lax.rem(gy + i, nyp)
            copies.append(
                pltpu.make_async_remote_copy(
                    src_ref=isend.at[c, to],
                    dst_ref=irecv.at[c, gy],
                    send_sem=vs.at[c, i],
                    recv_sem=vr.at[c, i],
                    device_id={"gy": to},
                    device_id_type=MESH,
                )
            )
        for copy in copies:
            copy.start()
        irecv[c, gy] = isend[c, gy]
        v_copies.append(copies)

    for stage in range(chunks + 2):
        if stage >= 2:
            back(stage - 2)
        if 1 <= stage <= chunks:
            close(stage - 1)
        if stage < chunks:
            lateral(stage)

    for c in range(chunks):
        for copy in v_copies[c]:
            copy.wait_recv()
    for j in range(pairs):
        spectrum = jnp.concatenate(
            [irecv[c, p, sub * j : sub * (j + 1), :] for p in range(nyp) for c in range(chunks)],
            axis=0,
        )
        smooth = dot3(spectrum.T, cas_z).reshape(pair, by, nz)
        for s in range(pair):
            x = pair * j + s
            mean[x] = mean[x] + smooth[s]
    search_out = pltpu.make_async_copy(mean, search_o, osem.at[3])
    search_out.start()

    for axis, side, copy in rims:

        @pl.when(jnp.logical_not(outside[axis][1 - side]))
        def _():
            copy.wait_send()

    for group in (z_copies, m_copies, r_copies, v_copies):
        for copies in group:
            for copy in copies:
                copy.wait_send()
    wave_out.wait()
    adj_out.wait()
    lgrad_out.wait()
    search_out.wait()


def per_device(
    nxp,
    nyp,
    mean_field,
    log_scale,
    noise,
    wave_prev,
    wave_now,
    adjoint_next,
    adjoint_now,
    sources,
    receivers,
    observed,
    step_index,
    prior_scale,
):
    bx, by, nz = wave_now.shape
    chunks = CHUNKS
    constants = tables(bx, by, nz, nxp, nyp, chunks)
    pairs = bx * by // LANES
    share = nz // nyp
    sub = share // chunks
    total_y = by * nyp
    rows = sub * (total_y // LANES) // nxp
    field = jax.ShapeDtypeStruct((bx, by, nz), F32)
    vmem = pl.BlockSpec(memory_space=pltpu.VMEM)
    hbm = pl.BlockSpec(memory_space=pl.ANY)
    dma = pltpu.SemaphoreType.DMA
    whole = pltpu.VMEM((bx, by, nz), F32)
    padded = pltpu.VMEM((bx, by + 2 * PAD, nz), F32)
    scratch = [whole] * 6 + [padded] * 2 + [whole] * 3
    scratch += [
        pltpu.VMEM((2, 2, REACH, by, nz), F32),
        pltpu.VMEM((2, 2, REACH * bx, nz), F32),
        pltpu.VMEM((2, 2, REACH * bx, nz), F32),
        pltpu.VMEM((nz, bx * by), F32),
        pltpu.VMEM((chunks, nyp, sub, bx * by), F32),
        pltpu.VMEM((chunks, pairs * sub, nyp * LANES), F32),
        pltpu.VMEM((chunks, nyp, pairs * sub, LANES), F32),
        pltpu.VMEM((chunks, nyp, pairs * sub, LANES), F32),
        pltpu.VMEM((chunks, nxp, 2 * rows, LANES), F32),
        pltpu.VMEM((chunks, nxp, 2 * rows, LANES), F32),
        pltpu.VMEM((chunks, nxp, 2 * rows, LANES), F32),
        pltpu.VMEM((chunks, nxp, 2 * rows, LANES), F32),
        dma((7,)),
        dma((4,)),
        dma((2, 2)),
        dma((2, 2)),
        dma((2, 2)),
        dma((2, 2)),
    ]
    scratch += [dma((chunks, nyp))] * 2 + [dma((chunks, nxp))] * 4 + [dma((chunks, nyp))] * 2
    filled = (-sources.shape[0]) % LANES
    src = jnp.pad(sources, ((0, filled), (0, 0)), constant_values=-1)
    return pl.pallas_call(
        functools.partial(kernel, nxp, nyp, chunks),
        out_shape=(field,) * 4,
        in_specs=[hbm] * 7 + [vmem] * (7 + len(constants)),
        out_specs=(hbm,) * 4,
        scratch_shapes=scratch,
        compiler_params=pltpu.CompilerParams(
            collective_id=0, has_side_effects=True, vmem_limit_bytes=50 * 2**20
        ),
    )(
        mean_field,
        log_scale,
        noise,
        wave_prev,
        wave_now,
        adjoint_next,
        adjoint_now,
        src.T,
        src,
        receivers.T,
        receivers,
        observed.reshape(1, -1),
        step_index.reshape(1, 1),
        prior_scale.reshape(1, 1),
        *[jnp.asarray(table) for table in constants],
    )


def solution(mesh):
    grid = P("gx", "gy", None)
    return jax.shard_map(
        functools.partial(per_device, mesh.shape["gx"], mesh.shape["gy"]),
        mesh=mesh,
        in_specs=(grid,) * 7 + (P(),) * 5,
        out_specs=(grid,) * 4,
        check_vma=False,
    )
```

```python
import functools
import math

import jax
import jax.numpy as jnp
import ml_dtypes
import numpy as np
from jax import lax
from jax.experimental import pallas as pl
from jax.experimental.pallas import tpu as pltpu
from jax.sharding import PartitionSpec as P

NSTEPS = 48
STENCIL_WEIGHTS = (-205.0 / 72.0, 8.0 / 5.0, -1.0 / 5.0, 8.0 / 315.0, -1.0 / 560.0)
COURANT_SQUARED = 0.08
VELOCITY_GAIN = 0.2
PULSE_FREQUENCY = 0.05
PULSE_AMPLITUDE = 20.0

REACH = 4
PAD = 8
LANES = 128
CHUNKS = 2
SMALL = 12
MESH = pl.DeviceIdType.MESH
F32 = jnp.float32
BF16 = jnp.bfloat16
NN = (((1,), (0,)), ((), ()))
NT = (((1,), (1,)), ((), ()))


def halves(table):
    high = table.astype(ml_dtypes.bfloat16)
    low = (table - high.astype(np.float64)).astype(ml_dtypes.bfloat16)
    return np.stack([high, low])


def cas(length):
    index = np.arange(length)
    angle = (index[:, None] * index[None, :] % length) * (2.0 * math.pi / length)
    return np.cos(angle) + np.sin(angle)


def wave_term(length):
    return (length / 8.0) ** 2 * 4.0 * np.sin(np.arange(length) * (math.pi / length)) ** 2


def tables(bx, by, nz, nxp, nyp, chunks):
    total_x, total_y = bx * nxp, by * nyp
    along_z = np.zeros((nz, nz))
    for o in range(1, REACH + 1):
        along_z += STENCIL_WEIGHTS[o] * (np.eye(nz, k=o) + np.eye(nz, k=-o))
    face_low = np.zeros((REACH, REACH))
    face_high = np.zeros((REACH, REACH))
    for i in range(REACH):
        for h in range(REACH):
            if h >= i:
                face_low[i, h] = STENCIL_WEIGHTS[i + REACH - h]
            if h <= i:
                face_high[i, h] = STENCIL_WEIGHTS[REACH + h - i]
    faces = np.stack([np.kron(np.eye(bx), face_low), np.kron(np.eye(bx), face_high)])
    pair = LANES // by
    weights_y = cas(total_y).reshape(nyp, by, total_y)
    forward_y = np.zeros((nyp, pair, by, pair, total_y))
    for s in range(pair):
        forward_y[:, s, :, s, :] = weights_y
    forward_y = forward_y.reshape(nyp * LANES, pair * total_y)
    c = (total_x / 8.0) ** 2
    d = 1.0 + wave_term(nz)[:, None] + wave_term(total_y)[None, :]
    log_r = -2.0 * np.arcsinh(0.5 * np.sqrt(d / c))
    r = np.exp(log_r)
    scale = math.sqrt(total_x * total_y * nz) / 8.0 / (nz * total_y)
    scale = scale / (c * -2.0 * np.sinh(log_r))
    closure = 1.0 / -np.expm1(total_x * log_r)
    share = nz // nyp
    sub = share // chunks
    tiles = total_y // LANES
    rows = sub * tiles // nxp
    segment = np.stack([np.exp(bx * log_r), closure])
    segment = segment.reshape(2, nyp, chunks, nxp // tiles, rows, tiles, LANES)
    segment = segment.transpose(1, 2, 3, 5, 0, 4, 6).reshape(nyp, chunks, nxp, 2, rows, LANES)
    as32 = lambda a: np.ascontiguousarray(a).astype(np.float32)
    return (
        as32(along_z),
        as32(faces),
        halves(cas(nz)),
        halves(forward_y),
        halves(forward_y.T),
        as32(np.stack([r, scale]).reshape(2, nyp, share, total_y)),
        as32(segment),
    )


def split(x):
    high = x.astype(BF16)
    return high, (x - high.astype(F32)).astype(BF16)


def split3(x):
    high = x.astype(BF16)
    rest = x - high.astype(F32)
    mid = rest.astype(BF16)
    return high, mid, (rest - mid.astype(F32)).astype(BF16)


def dot(a, b, dims=NN):
    return lax.dot_general(a, b, dims, preferred_element_type=F32)


def dot3(x, w):
    high, low = split(x)
    return dot(high, w[0]) + dot(high, w[1]) + dot(low, w[0])


def exact(a, b):
    return lax.dot_general(a, b, NN, precision=lax.Precision.HIGHEST, preferred_element_type=F32)


def kernel(
    nxp,
    nyp,
    chunks,
    mean_h,
    scale_h,
    noise_h,
    prev_h,
    now_h,
    anext_h,
    anow_h,
    *rest,
):
    small_h, rest = rest[:SMALL], rest[SMALL:]
    (wave_o, adj_o, sample_o, lgrad_o, irecv), rest = rest[:5], rest[5:]
    small, rest = rest[:SMALL], rest[SMALL:]
    (src_row, rec_row, observed, step, prior) = small[:5]
    (along_z, faces, cas_z, fwd_y, inv_y, line_tab, seg_tab) = small[5:]
    (
        mean,
        logs,
        noise,
        prev,
        anext,
        anow,
        wpad,
        bpad,
        curl,
        acurl,
        speed,
        xrecv,
        ysend,
        yrecv,
        zsend,
        zrecv,
        lines,
        isend,
        msend,
        mrecv,
        rsend,
        rrecv,
        lsem,
        tsem,
        osem,
        xs,
        xr,
        ys,
        yr,
        zs,
        zr,
        ms,
        mr,
        rs,
        rr,
        vs,
        vr,
        vsem,
    ) = rest
    bx, by, nz = mean.shape
    gx, gy = lax.axis_index("gx"), lax.axis_index("gy")
    pairs = bx * by // LANES
    pair = LANES // by
    share = nz // nyp
    sub = share // chunks
    total_y = by * nyp
    tiles = total_y // LANES
    rows = sub * tiles // nxp
    cells = bx * by
    centre = pl.ds(PAD, by)

    loads = [
        pltpu.make_async_copy(now_h, wpad.at[:, centre, :], lsem.at[0]),
        pltpu.make_async_copy(scale_h, logs, lsem.at[1]),
        pltpu.make_async_copy(noise_h, noise, lsem.at[2]),
        pltpu.make_async_copy(mean_h, mean, lsem.at[3]),
        pltpu.make_async_copy(anow_h, anow, lsem.at[4]),
        pltpu.make_async_copy(prev_h, prev, lsem.at[5]),
        pltpu.make_async_copy(anext_h, anext, lsem.at[6]),
    ]
    for load in loads:
        load.start()
    small_loads = [
        pltpu.make_async_copy(small_h[i], small[i], tsem.at[i]) for i in range(SMALL)
    ]
    for load in small_loads:
        load.start()

    for padded in (wpad, bpad):
        padded[:, 0:PAD, :] = jnp.zeros((bx, PAD, nz), F32)
        padded[:, PAD + by : by + 2 * PAD, :] = jnp.zeros((bx, PAD, nz), F32)
    outside = ((gx == 0, gx == nxp - 1), (gy == 0, gy == nyp - 1))
    for side in range(2):

        @pl.when(outside[0][side])
        def _():
            for field in range(2):
                xrecv[field, side] = jnp.zeros(xrecv.shape[2:], F32)

        @pl.when(outside[1][side])
        def _():
            for field in range(2):
                yrecv[field, side] = jnp.zeros(yrecv.shape[2:], F32)

    barrier = pltpu.get_barrier_semaphore()
    for i in range(1, nxp):
        pl.semaphore_signal(
            barrier, inc=1, device_id={"gx": lax.rem(gx + i, nxp)}, device_id_type=MESH
        )
    for i in range(1, nyp):
        pl.semaphore_signal(
            barrier, inc=1, device_id={"gy": lax.rem(gy + i, nyp)}, device_id_type=MESH
        )
    pl.semaphore_wait(barrier, nxp + nyp - 2)

    def rim_copy(axis, field, side, src):
        me, count = ((gx, nxp), (gy, nyp))[axis]
        target = lax.rem(me + (1 if side == 0 else count - 1), count)
        land, send, recv = ((xrecv, xs, xr), (yrecv, ys, yr))[axis]
        return pltpu.make_async_remote_copy(
            src_ref=src,
            dst_ref=land.at[field, side],
            send_sem=send.at[field, side],
            recv_sem=recv.at[field, side],
            device_id={("gx", "gy")[axis]: target},
            device_id_type=MESH,
        )

    def start_rim(axis, field, side, src):
        copy = rim_copy(axis, field, side, src)

        @pl.when(jnp.logical_not(outside[axis][1 - side]))
        def _():
            copy.start()

        return (axis, side, copy)

    rims = []
    rims.append(start_rim(0, 0, 0, now_h.at[pl.ds(bx - REACH, REACH)]))
    rims.append(start_rim(0, 0, 1, now_h.at[pl.ds(0, REACH)]))

    def pack_faces(field, padded):
        for x in range(bx):
            here = pl.ds(REACH * x, REACH)
            ysend[field, 0, here, :] = padded[x, PAD + by - REACH : PAD + by, :]
            ysend[field, 1, here, :] = padded[x, PAD : PAD + REACH, :]
        for side in range(2):
            rims.append(start_rim(1, field, side, ysend.at[field, side]))

    loads[0].wait()
    pack_faces(0, wpad)

    for load in loads[1:5]:
        load.wait()

    def pointwise(x):
        turned = jnp.exp(logs[x]) * noise[x]
        sample = mean[x] + turned
        logs[x] = turned
        mean[x] = sample
        fast = COURANT_SQUARED * jnp.exp(2.0 * VELOCITY_GAIN * sample)
        speed[x] = fast
        bpad[x, centre, :] = fast * anow[x]

    for x in range(REACH):
        pointwise(x)
    rims.append(start_rim(0, 1, 1, bpad.at[pl.ds(0, REACH), centre, :]))
    for x in range(bx - REACH, bx):
        pointwise(x)
    rims.append(start_rim(0, 1, 0, bpad.at[pl.ds(bx - REACH, REACH), centre, :]))
    for x in range(REACH, bx - REACH):
        pointwise(x)
    pack_faces(1, bpad)

    def inner_laplacian(padded, out):
        for x0 in range(0, bx, REACH):
            block = padded[x0 : x0 + REACH, PAD : PAD + by, :].reshape(REACH * by, nz)
            depthwise = exact(block, along_z[...]).reshape(REACH, by, nz)
            for x in range(x0, x0 + REACH):
                total = depthwise[x - x0] + 3.0 * STENCIL_WEIGHTS[0] * padded[x, centre, :]
                for o in range(1, REACH + 1):
                    near = padded[x, PAD + o : PAD + o + by, :] + padded[x, PAD - o : PAD - o + by, :]
                    if x + o < bx:
                        near = near + padded[x + o, centre, :]
                    if x - o >= 0:
                        near = near + padded[x - o, centre, :]
                    total = total + STENCIL_WEIGHTS[o] * near
                out[x] = total

    for load in small_loads:
        load.wait()
    inner_laplacian(wpad, curl)

    def codes(points):
        across = points[0:1, :] - gx * bx
        lateral = points[1:2, :] - gy * by
        inside = (across >= 0) & (across < bx) & (lateral >= 0) & (lateral < by)
        return jnp.where(inside, across * by + lateral, -1)

    src_code = codes(src_row)
    rec_code = codes(rec_row)

    def rim_terms(field, out):
        for side in range(2):
            terms = exact(faces[side], yrecv[field, side])
            first = 0 if side == 0 else by - REACH
            for x in range(bx):
                here = out[x, first : first + REACH, :]
                out[x, first : first + REACH, :] = here + terms[REACH * x : REACH * (x + 1), :]

    def x_rim(field, x):
        total = None
        for o in range(1, REACH + 1):
            if x - o < 0:
                term = STENCIL_WEIGHTS[o] * xrecv[field, 0, REACH + x - o]
                total = term if total is None else total + term
            if x + o >= bx:
                term = STENCIL_WEIGHTS[o] * xrecv[field, 1, x + o - bx]
                total = term if total is None else total + term
        return total

    def wait_rims(field_rims):
        for axis, side, copy in field_rims:

            @pl.when(jnp.logical_not(outside[axis][side]))
            def _():
                copy.wait_recv()

    inner_laplacian(bpad, acurl)
    loads[5].wait()
    loads[6].wait()

    wave_rims = rims[0:4]
    adj_rims = rims[4:8]
    wait_rims(wave_rims)
    rim_terms(0, curl)
    for x in range(bx):
        curved = curl[x]
        extra = x_rim(0, x)
        if extra is not None:
            curved = curved + extra
            curl[x] = curved
        prev[x] = 2.0 * wpad[x, centre, :] - prev[x] + speed[x] * curved

    moment = (step[...] - NSTEPS // 2).astype(F32) * (math.pi * PULSE_FREQUENCY)
    pulse = PULSE_AMPLITUDE * (1.0 - 2.0 * moment * moment) * jnp.exp(-moment * moment)
    nsrc, nrec = src_row.shape[1], rec_row.shape[1]
    src_level = lax.broadcasted_iota(jnp.int32, (nz, nsrc), 0) == src_row[2:3, :]
    src_level = src_level.astype(F32).astype(BF16)
    rec_level = lax.broadcasted_iota(jnp.int32, (nz, nrec), 0) == rec_row[2:3, :]
    rec_level = rec_level.astype(F32).astype(BF16)
    step_x = 4
    block = step_x * by
    picked = jnp.zeros((1, nrec), F32)
    for x0 in range(0, bx, step_x):
        cell = lax.broadcasted_iota(jnp.int32, (block, nsrc), 0) + x0 * by
        hit = (cell == src_code).astype(F32).astype(BF16)
        wave = prev[x0 : x0 + step_x].reshape(block, nz) + pulse * dot(hit, src_level, NT)
        prev[x0 : x0 + step_x] = wave.reshape(step_x, by, nz)
        traces = sum(dot(part, rec_level) for part in split3(wave))
        cell = lax.broadcasted_iota(jnp.int32, (block, nrec), 0) + x0 * by
        picked = picked + jnp.sum(
            jnp.where(cell == rec_code, traces, 0.0), axis=0, keepdims=True
        )
    wave_out = pltpu.make_async_copy(prev, wave_o, osem.at[0])
    wave_out.start()
    misfit = picked - observed[...]

    wait_rims(adj_rims)
    rim_terms(1, acurl)
    misfit_parts = split3(misfit)
    for x0 in range(0, bx, step_x):
        cell = lax.broadcasted_iota(jnp.int32, (block, nrec), 0) + x0 * by
        hit = cell == rec_code
        added = sum(
            dot(jnp.where(hit, part.astype(F32), 0.0).astype(BF16), rec_level, NT)
            for part in misfit_parts
        ).reshape(step_x, by, nz)
        for x in range(x0, x0 + step_x):
            total = acurl[x]
            extra = x_rim(1, x)
            if extra is not None:
                total = total + extra
            adjoint = 2.0 * anow[x] - anext[x] + total + added[x - x0]
            anext[x] = adjoint
            grad = (2.0 * VELOCITY_GAIN) * speed[x] * adjoint * curl[x]
            acurl[x] = grad
            anow[x] = grad * logs[x] - 1.0

        high, low = split(acurl[x0 : x0 + step_x].reshape(block, nz))
        zsend[:, x0 * by : x0 * by + block] = (
            dot(cas_z[0], high, NT) + dot(cas_z[1], high, NT) + dot(cas_z[0], low, NT)
        )

    def z_copy(c, i):
        to = lax.rem(gy + i, nyp)
        return pltpu.make_async_remote_copy(
            src_ref=zsend.at[pl.ds(pl.multiple_of(to * share + c * sub, sub), sub), :],
            dst_ref=zrecv.at[c, gy],
            send_sem=zs.at[c, i],
            recv_sem=zr.at[c, i],
            device_id={"gy": to},
            device_id_type=MESH,
        )

    def own_z(c):
        zrecv[c, gy] = zsend[pl.ds(pl.multiple_of(gy * share + c * sub, sub), sub), :]

    z_copies = [[z_copy(c, i) for i in range(1, nyp)] for c in range(chunks)]
    for c in range(chunks):
        for copy in z_copies[c]:
            copy.start()
    adj_out = pltpu.make_async_copy(anext, adj_o, osem.at[1])
    adj_out.start()
    lgrad_out = pltpu.make_async_copy(anow, lgrad_o, osem.at[2])
    lgrad_out.start()
    sample_out = pltpu.make_async_copy(mean, sample_o, osem.at[3])
    sample_out.start()
    for c in range(chunks):
        own_z(c)

    def ratio(c):
        return line_tab[0, gy, c * sub : (c + 1) * sub, :]

    def at(c, x):
        first = (x // pair) * sub
        left = (x % pair) * total_y
        return lines[c, first : first + sub, left : left + total_y]

    def segment(o):
        return (
            slice((o // tiles) * rows, (o // tiles + 1) * rows),
            slice((o % tiles) * LANES, (o % tiles + 1) * LANES),
        )

    def small_copy(src, dst, send, recv, c, i):
        to = lax.rem(gx + i, nxp)
        return pltpu.make_async_remote_copy(
            src_ref=src.at[c, to],
            dst_ref=dst.at[c, gx],
            send_sem=send.at[c, i],
            recv_sem=recv.at[c, i],
            device_id={"gx": to},
            device_id_type=MESH,
        )

    m_copies, r_copies, v_copies, own_fields = [], [], [], []

    def lateral(c):
        for copy in z_copies[c]:
            copy.wait_recv()
        block = jnp.concatenate(
            [
                jnp.concatenate(
                    [zrecv[c, p, :, LANES * j : LANES * (j + 1)] for p in range(nyp)], axis=1
                )
                for j in range(pairs)
            ],
            axis=0,
        )
        lines[c] = dot3(block, fwd_y)
        r = ratio(c)
        up = at(c, 0)
        down = at(c, bx - 1)
        for x in range(1, bx):
            up = at(c, x) + r * up
            down = at(c, bx - 1 - x) + r * down
        for o in range(nxp):
            here = segment(o)
            msend[c, o, 0:rows, :] = up[here]
            msend[c, o, rows : 2 * rows, :] = down[here]
        copies = [small_copy(msend, mrecv, ms, mr, c, i) for i in range(1, nxp)]
        for copy in copies:
            copy.start()
        mrecv[c, gx] = msend[c, gx]
        m_copies.append(copies)

    def close(c):
        for copy in m_copies[c]:
            copy.wait_recv()
        decay = seg_tab[gy, c, gx, 0]
        closure = seg_tab[gy, c, gx, 1]
        ups = [mrecv[c, d, 0:rows, :] for d in range(nxp)]
        downs = [mrecv[c, d, rows : 2 * rows, :] for d in range(nxp)]
        up, down = ups[0], downs[nxp - 1]
        for d in range(1, nxp):
            up = ups[d] + decay * up
            down = downs[nxp - 1 - d] + decay * down
        up = up * closure
        down = down * closure
        for d in range(nxp):
            rsend[c, d, 0:rows, :] = up
            up = ups[d] + decay * up
        for d in range(nxp - 1, -1, -1):
            rsend[c, d, rows : 2 * rows, :] = down
            down = downs[d] + decay * down
        copies = [small_copy(rsend, rrecv, rs, rr, c, i) for i in range(1, nxp)]
        for copy in copies:
            copy.start()
        rrecv[c, gx] = rsend[c, gx]
        r_copies.append(copies)

    def back(c):
        for copy in r_copies[c]:
            copy.wait_recv()

        def whole(first):
            return jnp.concatenate(
                [
                    jnp.concatenate(
                        [rrecv[c, i * tiles + t, first : first + rows, :] for t in range(tiles)],
                        axis=1,
                    )
                    for i in range(nxp // tiles)
                ],
                axis=0,
            )

        r = ratio(c)
        gain = line_tab[1, gy, c * sub : (c + 1) * sub, :] * prior[...]
        up, down = whole(0), whole(rows)
        ups = []
        for x in range(bx):
            up = at(c, x) + r * up
            ups.append(up)
        for x in range(bx - 1, -1, -1):
            ahead = r * down
            here = at(c, x)
            down = here + ahead
            first = (x // pair) * sub
            left = (x % pair) * total_y
            lines[c, first : first + sub, left : left + total_y] = gain * (ups[x] + ahead)
        field = dot3(lines[c], inv_y)
        for p in range(nyp):
            isend[c, p] = field[:, LANES * p : LANES * (p + 1)]
        copies = []
        for i in range(1, nyp):
            to = lax.rem(gy + i, nyp)
            copies.append(
                pltpu.make_async_remote_copy(
                    src_ref=isend.at[c, to],
                    dst_ref=irecv.at[c, gy],
                    send_sem=vs.at[c, i],
                    recv_sem=vr.at[c, i],
                    device_id={"gy": to},
                    device_id_type=MESH,
                )
            )
        for copy in copies:
            copy.start()
        own = pltpu.make_async_copy(isend.at[c, gy], irecv.at[c, gy], vsem.at[c])
        own.start()
        own_fields.append(own)
        v_copies.append(copies)

    for stage in range(chunks + 2):
        if stage >= 2:
            back(stage - 2)
        if 1 <= stage <= chunks:
            close(stage - 1)
        if stage < chunks:
            lateral(stage)

    for c in range(chunks):
        for copy in v_copies[c]:
            copy.wait_recv()
    for own in own_fields:
        own.wait()
    for axis, side, copy in rims:

        @pl.when(jnp.logical_not(outside[axis][1 - side]))
        def _():
            copy.wait_send()

    for group in (z_copies, m_copies, r_copies, v_copies):
        for copies in group:
            for copy in copies:
                copy.wait_send()
    wave_out.wait()
    adj_out.wait()
    lgrad_out.wait()
    sample_out.wait()


def finish(
    wave,
    adjoint,
    sample_h,
    lgrad,
    field_h,
    cas_h,
    wave_o,
    adj_o,
    search_o,
    lgrad_o,
    sample,
    field,
    cas_z,
    search,
    sem,
    out_sem,
):
    bx, by, nz = sample.shape
    pair = LANES // by
    pairs = bx // pair
    chunks, nyp, height, _ = field.shape
    sub = height // pairs
    copies = [
        pltpu.make_async_copy(field_h, field, sem.at[0]),
        pltpu.make_async_copy(cas_h, cas_z, sem.at[1]),
        pltpu.make_async_copy(sample_h, sample, sem.at[2]),
        pltpu.make_async_copy(wave, wave_o, sem.at[3]),
        pltpu.make_async_copy(adjoint, adj_o, sem.at[4]),
        pltpu.make_async_copy(lgrad, lgrad_o, sem.at[5]),
    ]
    for copy in copies:
        copy.start()
    for copy in copies[:3]:
        copy.wait()
    outs = []
    for j in range(pairs):
        spectrum = jnp.concatenate(
            [field[c, p, sub * j : sub * (j + 1), :] for p in range(nyp) for c in range(chunks)],
            axis=0,
        )
        smooth = dot3(spectrum.T, cas_z).reshape(pair, by, nz)
        here = pl.ds(pair * j, pair)
        search[here] = sample[here] + smooth
        out = pltpu.make_async_copy(search.at[here], search_o.at[here], out_sem.at[j])
        out.start()
        outs.append(out)
    for copy in copies[3:] + outs:
        copy.wait()


def per_device(
    nxp,
    nyp,
    mean_field,
    log_scale,
    noise,
    wave_prev,
    wave_now,
    adjoint_next,
    adjoint_now,
    sources,
    receivers,
    observed,
    step_index,
    prior_scale,
):
    bx, by, nz = wave_now.shape
    chunks = CHUNKS
    constants = tables(bx, by, nz, nxp, nyp, chunks)
    small = [
        sources.T,
        receivers.T,
        observed.reshape(1, -1),
        step_index.reshape(1, 1),
        prior_scale.reshape(1, 1),
    ] + [jnp.asarray(table) for table in constants]
    pairs = bx * by // LANES
    share = nz // nyp
    sub = share // chunks
    total_y = by * nyp
    rows = sub * (total_y // LANES) // nxp
    field = jax.ShapeDtypeStruct((bx, by, nz), F32)
    hbm = pl.BlockSpec(memory_space=pltpu.HBM)
    anywhere = pl.BlockSpec(memory_space=pl.ANY)
    dma = pltpu.SemaphoreType.DMA
    whole = pltpu.VMEM((bx, by, nz), F32)
    padded = pltpu.VMEM((bx, by + 2 * PAD, nz), F32)
    scratch = [pltpu.VMEM(a.shape, a.dtype) for a in small]
    scratch += [whole] * 6 + [padded] * 2 + [whole] * 3
    scratch += [
        pltpu.VMEM((2, 2, REACH, by, nz), F32),
        pltpu.VMEM((2, 2, REACH * bx, nz), F32),
        pltpu.VMEM((2, 2, REACH * bx, nz), F32),
        pltpu.VMEM((nz, bx * by), F32),
        pltpu.VMEM((chunks, nyp, sub, bx * by), F32),
        pltpu.VMEM((chunks, pairs * sub, nyp * LANES), F32),
        pltpu.VMEM((chunks, nyp, pairs * sub, LANES), F32),
        pltpu.VMEM((chunks, nxp, 2 * rows, LANES), F32),
        pltpu.VMEM((chunks, nxp, 2 * rows, LANES), F32),
        pltpu.VMEM((chunks, nxp, 2 * rows, LANES), F32),
        pltpu.VMEM((chunks, nxp, 2 * rows, LANES), F32),
        dma((7,)),
        dma((SMALL,)),
        dma((4,)),
        dma((2, 2)),
        dma((2, 2)),
        dma((2, 2)),
        dma((2, 2)),
    ]
    scratch += [dma((chunks, nyp))] * 2 + [dma((chunks, nxp))] * 4 + [dma((chunks, nyp))] * 2
    scratch += [dma((chunks,))]
    spread = jax.ShapeDtypeStruct((chunks, nyp, pairs * sub, LANES), F32)
    wave, adjoint, sample, lgrad, spectrum = pl.pallas_call(
        functools.partial(kernel, nxp, nyp, chunks),
        out_shape=(field,) * 4 + (spread,),
        in_specs=[hbm] * (7 + len(small)),
        out_specs=(anywhere,) * 5,
        scratch_shapes=scratch,
        compiler_params=pltpu.CompilerParams(
            collective_id=0, has_side_effects=True, vmem_limit_bytes=63 * 2**20
        ),
    )(
        mean_field, log_scale, noise, wave_prev, wave_now, adjoint_next, adjoint_now, *small
    )
    return pl.pallas_call(
        finish,
        out_shape=(field,) * 4,
        in_specs=[anywhere] * 5 + [hbm],
        out_specs=(hbm,) * 4,
        scratch_shapes=[
            whole,
            pltpu.VMEM(spread.shape, F32),
            pltpu.VMEM((2, nz, nz), BF16),
            whole,
            dma((6,)),
            dma((pairs,)),
        ],
        compiler_params=pltpu.CompilerParams(vmem_limit_bytes=63 * 2**20),
    )(wave, adjoint, sample, lgrad, spectrum, small[7])


def solution(mesh):
    grid = P("gx", "gy", None)
    return jax.shard_map(
        functools.partial(per_device, mesh.shape["gx"], mesh.shape["gy"]),
        mesh=mesh,
        in_specs=(grid,) * 7 + (P(),) * 5,
        out_specs=(grid,) * 4,
        check_vma=False,
    )
```

```python
import functools
import math

import jax
import jax.numpy as jnp
import ml_dtypes
import numpy as np
from jax import lax
from jax.experimental import pallas as pl
from jax.experimental.pallas import tpu as pltpu
from jax.sharding import PartitionSpec as P

NSTEPS = 48
STENCIL_WEIGHTS = (-205.0 / 72.0, 8.0 / 5.0, -1.0 / 5.0, 8.0 / 315.0, -1.0 / 560.0)
COURANT_SQUARED = 0.08
VELOCITY_GAIN = 0.2
PULSE_FREQUENCY = 0.05
PULSE_AMPLITUDE = 20.0

REACH = 4
PAD = 8
LANES = 128
CHUNKS = 2
SMALL = 12
MESH = pl.DeviceIdType.MESH
F32 = jnp.float32
BF16 = jnp.bfloat16
NN = (((1,), (0,)), ((), ()))
NT = (((1,), (1,)), ((), ()))


def halves(table):
    high = table.astype(ml_dtypes.bfloat16)
    low = (table - high.astype(np.float64)).astype(ml_dtypes.bfloat16)
    return np.stack([high, low])


def cas(length):
    index = np.arange(length)
    angle = (index[:, None] * index[None, :] % length) * (2.0 * math.pi / length)
    return np.cos(angle) + np.sin(angle)


def wave_term(length):
    return (length / 8.0) ** 2 * 4.0 * np.sin(np.arange(length) * (math.pi / length)) ** 2


def tables(bx, by, nz, nxp, nyp, chunks):
    total_x, total_y = bx * nxp, by * nyp
    along_z = np.zeros((nz, nz))
    for o in range(1, REACH + 1):
        along_z += STENCIL_WEIGHTS[o] * (np.eye(nz, k=o) + np.eye(nz, k=-o))
    face_low = np.zeros((REACH, REACH))
    face_high = np.zeros((REACH, REACH))
    for i in range(REACH):
        for h in range(REACH):
            if h >= i:
                face_low[i, h] = STENCIL_WEIGHTS[i + REACH - h]
            if h <= i:
                face_high[i, h] = STENCIL_WEIGHTS[REACH + h - i]
    faces = np.stack([np.kron(np.eye(bx), face_low), np.kron(np.eye(bx), face_high)])
    pair = LANES // by
    weights_y = cas(total_y).reshape(nyp, by, total_y)
    forward_y = np.zeros((nyp, pair, by, pair, total_y))
    for s in range(pair):
        forward_y[:, s, :, s, :] = weights_y
    forward_y = forward_y.reshape(nyp * LANES, pair * total_y)
    c = (total_x / 8.0) ** 2
    d = 1.0 + wave_term(nz)[:, None] + wave_term(total_y)[None, :]
    log_r = -2.0 * np.arcsinh(0.5 * np.sqrt(d / c))
    r = np.exp(log_r)
    scale = math.sqrt(total_x * total_y * nz) / 8.0 / (nz * total_y)
    scale = scale / (c * -2.0 * np.sinh(log_r))
    closure = 1.0 / -np.expm1(total_x * log_r)
    share = nz // nyp
    sub = share // chunks
    tiles = total_y // LANES
    rows = sub * tiles // nxp
    segment = np.stack([np.exp(bx * log_r), closure])
    segment = segment.reshape(2, nyp, chunks, nxp // tiles, rows, tiles, LANES)
    segment = segment.transpose(1, 2, 3, 5, 0, 4, 6).reshape(nyp, chunks, nxp, 2, rows, LANES)
    as32 = lambda a: np.ascontiguousarray(a).astype(np.float32)
    return (
        as32(along_z),
        as32(faces),
        halves(cas(nz)),
        halves(forward_y),
        halves(forward_y.T),
        as32(np.stack([r, scale]).reshape(2, nyp, share, total_y)),
        as32(segment),
    )


def split(x):
    high = x.astype(BF16)
    return high, (x - high.astype(F32)).astype(BF16)


def split3(x):
    high = x.astype(BF16)
    rest = x - high.astype(F32)
    mid = rest.astype(BF16)
    return high, mid, (rest - mid.astype(F32)).astype(BF16)


def dot(a, b, dims=NN):
    return lax.dot_general(a, b, dims, preferred_element_type=F32)


def dot3(x, w):
    high, low = split(x)
    return dot(high, w[0]) + dot(high, w[1]) + dot(low, w[0])


def exact(a, b):
    return lax.dot_general(a, b, NN, precision=lax.Precision.HIGHEST, preferred_element_type=F32)


def kernel(
    nxp,
    nyp,
    chunks,
    mean_h,
    scale_h,
    noise_h,
    prev_h,
    now_h,
    anext_h,
    anow_h,
    *rest,
):
    small_h, rest = rest[:SMALL], rest[SMALL:]
    (wave_o, adj_o, sample_o, lgrad_o, irecv), rest = rest[:5], rest[5:]
    small, rest = rest[:SMALL], rest[SMALL:]
    (src_row, rec_row, observed, step, prior) = small[:5]
    (along_z, faces, cas_z, fwd_y, inv_y, line_tab, seg_tab) = small[5:]
    (
        mean,
        logs,
        noise,
        prev,
        anext,
        anow,
        wpad,
        bpad,
        curl,
        acurl,
        speed,
        xrecv,
        ysend,
        yrecv,
        zsend,
        zrecv,
        lines,
        isend,
        msend,
        mrecv,
        rsend,
        rrecv,
        lsem,
        tsem,
        osem,
        xs,
        xr,
        ys,
        yr,
        zs,
        zr,
        ms,
        mr,
        rs,
        rr,
        vs,
        vr,
        vsem,
    ) = rest
    bx, by, nz = mean.shape
    gx, gy = lax.axis_index("gx"), lax.axis_index("gy")
    pairs = bx * by // LANES
    pair = LANES // by
    share = nz // nyp
    sub = share // chunks
    total_y = by * nyp
    tiles = total_y // LANES
    rows = sub * tiles // nxp
    cells = bx * by
    centre = pl.ds(PAD, by)

    loads = [
        pltpu.make_async_copy(now_h, wpad.at[:, centre, :], lsem.at[0]),
        pltpu.make_async_copy(scale_h, logs, lsem.at[1]),
        pltpu.make_async_copy(noise_h, noise, lsem.at[2]),
        pltpu.make_async_copy(mean_h, mean, lsem.at[3]),
        pltpu.make_async_copy(anow_h, anow, lsem.at[4]),
        pltpu.make_async_copy(prev_h, prev, lsem.at[5]),
        pltpu.make_async_copy(anext_h, anext, lsem.at[6]),
    ]
    for load in loads:
        load.start()
    small_loads = [
        pltpu.make_async_copy(small_h[i], small[i], tsem.at[i]) for i in range(SMALL)
    ]
    for load in small_loads:
        load.start()

    for padded in (wpad, bpad):
        padded[:, 0:PAD, :] = jnp.zeros((bx, PAD, nz), F32)
        padded[:, PAD + by : by + 2 * PAD, :] = jnp.zeros((bx, PAD, nz), F32)
    outside = ((gx == 0, gx == nxp - 1), (gy == 0, gy == nyp - 1))
    for side in range(2):

        @pl.when(outside[0][side])
        def _():
            for field in range(2):
                xrecv[field, side] = jnp.zeros(xrecv.shape[2:], F32)

        @pl.when(outside[1][side])
        def _():
            for field in range(2):
                yrecv[field, side] = jnp.zeros(yrecv.shape[2:], F32)

    barrier = pltpu.get_barrier_semaphore()
    for i in range(1, nxp):
        pl.semaphore_signal(
            barrier, inc=1, device_id={"gx": lax.rem(gx + i, nxp)}, device_id_type=MESH
        )
    for i in range(1, nyp):
        pl.semaphore_signal(
            barrier, inc=1, device_id={"gy": lax.rem(gy + i, nyp)}, device_id_type=MESH
        )
    pl.semaphore_wait(barrier, nxp + nyp - 2)

    def rim_copy(axis, field, side, src):
        me, count = ((gx, nxp), (gy, nyp))[axis]
        target = lax.rem(me + (1 if side == 0 else count - 1), count)
        land, send, recv = ((xrecv, xs, xr), (yrecv, ys, yr))[axis]
        return pltpu.make_async_remote_copy(
            src_ref=src,
            dst_ref=land.at[field, side],
            send_sem=send.at[field, side],
            recv_sem=recv.at[field, side],
            device_id={("gx", "gy")[axis]: target},
            device_id_type=MESH,
        )

    def start_rim(axis, field, side, src):
        copy = rim_copy(axis, field, side, src)

        @pl.when(jnp.logical_not(outside[axis][1 - side]))
        def _():
            copy.start()

        return (axis, side, copy)

    rims = []
    rims.append(start_rim(0, 0, 0, now_h.at[pl.ds(bx - REACH, REACH)]))
    rims.append(start_rim(0, 0, 1, now_h.at[pl.ds(0, REACH)]))

    def pack_faces(field, padded):
        for x in range(bx):
            here = pl.ds(REACH * x, REACH)
            ysend[field, 0, here, :] = padded[x, PAD + by - REACH : PAD + by, :]
            ysend[field, 1, here, :] = padded[x, PAD : PAD + REACH, :]
        for side in range(2):
            rims.append(start_rim(1, field, side, ysend.at[field, side]))

    loads[0].wait()
    pack_faces(0, wpad)

    for load in loads[1:5]:
        load.wait()

    def pointwise(x):
        turned = jnp.exp(logs[x]) * noise[x]
        sample = mean[x] + turned
        logs[x] = turned
        mean[x] = sample
        fast = COURANT_SQUARED * jnp.exp(2.0 * VELOCITY_GAIN * sample)
        speed[x] = fast
        bpad[x, centre, :] = fast * anow[x]

    for x in range(REACH):
        pointwise(x)
    rims.append(start_rim(0, 1, 1, bpad.at[pl.ds(0, REACH), centre, :]))
    for x in range(bx - REACH, bx):
        pointwise(x)
    rims.append(start_rim(0, 1, 0, bpad.at[pl.ds(bx - REACH, REACH), centre, :]))
    for x in range(REACH, bx - REACH):
        pointwise(x)
    pack_faces(1, bpad)

    def inner_laplacian(padded, out):
        for x0 in range(0, bx, REACH):
            block = padded[x0 : x0 + REACH, PAD : PAD + by, :].reshape(REACH * by, nz)
            depthwise = exact(block, along_z[...]).reshape(REACH, by, nz)
            for x in range(x0, x0 + REACH):
                total = depthwise[x - x0] + 3.0 * STENCIL_WEIGHTS[0] * padded[x, centre, :]
                for o in range(1, REACH + 1):
                    near = padded[x, PAD + o : PAD + o + by, :] + padded[x, PAD - o : PAD - o + by, :]
                    if x + o < bx:
                        near = near + padded[x + o, centre, :]
                    if x - o >= 0:
                        near = near + padded[x - o, centre, :]
                    total = total + STENCIL_WEIGHTS[o] * near
                out[x] = total

    for load in small_loads:
        load.wait()
    inner_laplacian(wpad, curl)

    def codes(points):
        across = points[0:1, :] - gx * bx
        lateral = points[1:2, :] - gy * by
        inside = (across >= 0) & (across < bx) & (lateral >= 0) & (lateral < by)
        return jnp.where(inside, across * by + lateral, -1)

    src_code = codes(src_row)
    rec_code = codes(rec_row)

    def rim_terms(field, out):
        for side in range(2):
            terms = exact(faces[side], yrecv[field, side])
            first = 0 if side == 0 else by - REACH
            for x in range(bx):
                here = out[x, first : first + REACH, :]
                out[x, first : first + REACH, :] = here + terms[REACH * x : REACH * (x + 1), :]

    def x_rim(field, x):
        total = None
        for o in range(1, REACH + 1):
            if x - o < 0:
                term = STENCIL_WEIGHTS[o] * xrecv[field, 0, REACH + x - o]
                total = term if total is None else total + term
            if x + o >= bx:
                term = STENCIL_WEIGHTS[o] * xrecv[field, 1, x + o - bx]
                total = term if total is None else total + term
        return total

    def wait_rims(field_rims):
        for axis, side, copy in field_rims:

            @pl.when(jnp.logical_not(outside[axis][side]))
            def _():
                copy.wait_recv()

    inner_laplacian(bpad, acurl)
    loads[5].wait()
    loads[6].wait()

    wave_rims = rims[0:4]
    adj_rims = rims[4:8]
    wait_rims(wave_rims)
    rim_terms(0, curl)
    for x in range(bx):
        curved = curl[x]
        extra = x_rim(0, x)
        if extra is not None:
            curved = curved + extra
            curl[x] = curved
        prev[x] = 2.0 * wpad[x, centre, :] - prev[x] + speed[x] * curved

    moment = (step[...] - NSTEPS // 2).astype(F32) * (math.pi * PULSE_FREQUENCY)
    pulse = PULSE_AMPLITUDE * (1.0 - 2.0 * moment * moment) * jnp.exp(-moment * moment)
    nsrc, nrec = src_row.shape[1], rec_row.shape[1]
    src_level = lax.broadcasted_iota(jnp.int32, (nz, nsrc), 0) == src_row[2:3, :]
    src_level = src_level.astype(F32).astype(BF16)
    rec_level = lax.broadcasted_iota(jnp.int32, (nz, nrec), 0) == rec_row[2:3, :]
    rec_level = rec_level.astype(F32).astype(BF16)
    step_x = 4
    block = step_x * by
    picked = jnp.zeros((1, nrec), F32)
    for x0 in range(0, bx, step_x):
        cell = lax.broadcasted_iota(jnp.int32, (block, nsrc), 0) + x0 * by
        hit = (cell == src_code).astype(F32).astype(BF16)
        wave = prev[x0 : x0 + step_x].reshape(block, nz) + pulse * dot(hit, src_level, NT)
        prev[x0 : x0 + step_x] = wave.reshape(step_x, by, nz)
        traces = sum(dot(part, rec_level) for part in split3(wave))
        cell = lax.broadcasted_iota(jnp.int32, (block, nrec), 0) + x0 * by
        picked = picked + jnp.sum(
            jnp.where(cell == rec_code, traces, 0.0), axis=0, keepdims=True
        )
    wave_out = pltpu.make_async_copy(prev, wave_o, osem.at[0])
    wave_out.start()
    misfit = picked - observed[...]

    wait_rims(adj_rims)
    rim_terms(1, acurl)
    misfit_parts = split3(misfit)

    parts = bx // step_x

    def z_copy(c, i, part):
        to = lax.rem(gy + i, nyp)
        first = pl.multiple_of(to * share + c * sub, sub)
        across = pl.ds(0, cells) if part is None else pl.ds(part * block, block)
        slot = 0 if part is None else part
        return pltpu.make_async_remote_copy(
            src_ref=zsend.at[pl.ds(first, sub), across],
            dst_ref=zrecv.at[c, gy, :, across],
            send_sem=zs.at[c, slot, i],
            recv_sem=zr.at[c, slot, i],
            device_id={"gy": to},
            device_id_type=MESH,
        )

    def own_z(c):
        zrecv[c, gy] = zsend[pl.ds(pl.multiple_of(gy * share + c * sub, sub), sub), :]

    z_copies = [
        [z_copy(c, i, part) for part in (range(parts) if c == 0 else (None,)) for i in range(1, nyp)]
        for c in range(chunks)
    ]
    for x0 in range(0, bx, step_x):
        cell = lax.broadcasted_iota(jnp.int32, (block, nrec), 0) + x0 * by
        hit = cell == rec_code
        added = sum(
            dot(jnp.where(hit, part.astype(F32), 0.0).astype(BF16), rec_level, NT)
            for part in misfit_parts
        ).reshape(step_x, by, nz)
        for x in range(x0, x0 + step_x):
            total = acurl[x]
            extra = x_rim(1, x)
            if extra is not None:
                total = total + extra
            adjoint = 2.0 * anow[x] - anext[x] + total + added[x - x0]
            anext[x] = adjoint
            grad = (2.0 * VELOCITY_GAIN) * speed[x] * adjoint * curl[x]
            acurl[x] = grad
            anow[x] = grad * logs[x] - 1.0

        high, low = split(acurl[x0 : x0 + step_x].reshape(block, nz))
        zsend[:, x0 * by : x0 * by + block] = (
            dot(cas_z[0], high, NT) + dot(cas_z[1], high, NT) + dot(cas_z[0], low, NT)
        )
        part = x0 // step_x
        for copy in z_copies[0][part * (nyp - 1) : (part + 1) * (nyp - 1)]:
            copy.start()

    for copies in z_copies[1:]:
        for copy in copies:
            copy.start()

    adj_out = pltpu.make_async_copy(anext, adj_o, osem.at[1])
    adj_out.start()
    lgrad_out = pltpu.make_async_copy(anow, lgrad_o, osem.at[2])
    lgrad_out.start()
    sample_out = pltpu.make_async_copy(mean, sample_o, osem.at[3])
    sample_out.start()
    for c in range(chunks):
        own_z(c)

    def ratio(c):
        return line_tab[0, gy, c * sub : (c + 1) * sub, :]

    def at(c, x):
        first = (x // pair) * sub
        left = (x % pair) * total_y
        return lines[c, first : first + sub, left : left + total_y]

    def segment(o):
        return (
            slice((o // tiles) * rows, (o // tiles + 1) * rows),
            slice((o % tiles) * LANES, (o % tiles + 1) * LANES),
        )

    def small_copy(src, dst, send, recv, c, i):
        to = lax.rem(gx + i, nxp)
        return pltpu.make_async_remote_copy(
            src_ref=src.at[c, to],
            dst_ref=dst.at[c, gx],
            send_sem=send.at[c, i],
            recv_sem=recv.at[c, i],
            device_id={"gx": to},
            device_id_type=MESH,
        )

    m_copies, r_copies, v_copies, own_fields = [], [], [], []

    def lateral(c):
        for copy in z_copies[c]:
            copy.wait_recv()
        block = jnp.concatenate(
            [
                jnp.concatenate(
                    [zrecv[c, p, :, LANES * j : LANES * (j + 1)] for p in range(nyp)], axis=1
                )
                for j in range(pairs)
            ],
            axis=0,
        )
        lines[c] = dot3(block, fwd_y)
        r = ratio(c)
        up = at(c, 0)
        down = at(c, bx - 1)
        for x in range(1, bx):
            up = at(c, x) + r * up
            down = at(c, bx - 1 - x) + r * down
        for o in range(nxp):
            here = segment(o)
            msend[c, o, 0:rows, :] = up[here]
            msend[c, o, rows : 2 * rows, :] = down[here]
        copies = [small_copy(msend, mrecv, ms, mr, c, i) for i in range(1, nxp)]
        for copy in copies:
            copy.start()
        mrecv[c, gx] = msend[c, gx]
        m_copies.append(copies)

    def close(c):
        for copy in m_copies[c]:
            copy.wait_recv()
        decay = seg_tab[gy, c, gx, 0]
        closure = seg_tab[gy, c, gx, 1]
        ups = [mrecv[c, d, 0:rows, :] for d in range(nxp)]
        downs = [mrecv[c, d, rows : 2 * rows, :] for d in range(nxp)]
        up, down = ups[0], downs[nxp - 1]
        for d in range(1, nxp):
            up = ups[d] + decay * up
            down = downs[nxp - 1 - d] + decay * down
        up = up * closure
        down = down * closure
        for d in range(nxp):
            rsend[c, d, 0:rows, :] = up
            up = ups[d] + decay * up
        for d in range(nxp - 1, -1, -1):
            rsend[c, d, rows : 2 * rows, :] = down
            down = downs[d] + decay * down
        copies = [small_copy(rsend, rrecv, rs, rr, c, i) for i in range(1, nxp)]
        for copy in copies:
            copy.start()
        rrecv[c, gx] = rsend[c, gx]
        r_copies.append(copies)

    def back(c):
        for copy in r_copies[c]:
            copy.wait_recv()

        def whole(first):
            return jnp.concatenate(
                [
                    jnp.concatenate(
                        [rrecv[c, i * tiles + t, first : first + rows, :] for t in range(tiles)],
                        axis=1,
                    )
                    for i in range(nxp // tiles)
                ],
                axis=0,
            )

        r = ratio(c)
        gain = line_tab[1, gy, c * sub : (c + 1) * sub, :] * prior[...]
        up, down = whole(0), whole(rows)
        ups = []
        for x in range(bx):
            up = at(c, x) + r * up
            ups.append(up)
        for x in range(bx - 1, -1, -1):
            ahead = r * down
            here = at(c, x)
            down = here + ahead
            first = (x // pair) * sub
            left = (x % pair) * total_y
            lines[c, first : first + sub, left : left + total_y] = gain * (ups[x] + ahead)
        field = dot3(lines[c], inv_y)
        for p in range(nyp):
            isend[c, p] = field[:, LANES * p : LANES * (p + 1)]
        copies = []
        for i in range(1, nyp):
            to = lax.rem(gy + i, nyp)
            copies.append(
                pltpu.make_async_remote_copy(
                    src_ref=isend.at[c, to],
                    dst_ref=irecv.at[c, gy],
                    send_sem=vs.at[c, i],
                    recv_sem=vr.at[c, i],
                    device_id={"gy": to},
                    device_id_type=MESH,
                )
            )
        for copy in copies:
            copy.start()
        own = pltpu.make_async_copy(isend.at[c, gy], irecv.at[c, gy], vsem.at[c])
        own.start()
        own_fields.append(own)
        v_copies.append(copies)

    for stage in range(chunks + 2):
        if stage >= 2:
            back(stage - 2)
        if 1 <= stage <= chunks:
            close(stage - 1)
        if stage < chunks:
            lateral(stage)

    for c in range(chunks):
        for copy in v_copies[c]:
            copy.wait_recv()
    for own in own_fields:
        own.wait()
    for axis, side, copy in rims:

        @pl.when(jnp.logical_not(outside[axis][1 - side]))
        def _():
            copy.wait_send()

    for group in (z_copies, m_copies, r_copies, v_copies):
        for copies in group:
            for copy in copies:
                copy.wait_send()
    wave_out.wait()
    adj_out.wait()
    lgrad_out.wait()
    sample_out.wait()


def finish(
    wave,
    adjoint,
    sample_h,
    lgrad,
    field_h,
    cas_h,
    wave_o,
    adj_o,
    search_o,
    lgrad_o,
    sample,
    field,
    cas_z,
    search,
    kept,
    sem,
    out_sem,
):
    bx, by, nz = sample.shape
    pair = LANES // by
    pairs = bx // pair
    chunks, nyp, height, _ = field.shape
    sub = height // pairs
    copies = [
        pltpu.make_async_copy(field_h, field, sem.at[0]),
        pltpu.make_async_copy(cas_h, cas_z, sem.at[1]),
        pltpu.make_async_copy(sample_h, sample, sem.at[2]),
        pltpu.make_async_copy(wave, kept.at[0], sem.at[3]),
        pltpu.make_async_copy(adjoint, kept.at[1], sem.at[4]),
        pltpu.make_async_copy(lgrad, kept.at[2], sem.at[5]),
    ]
    for copy in copies[3:] + copies[:3]:
        copy.start()
    outs = []
    for i, kept_o in enumerate((wave_o, adj_o, lgrad_o)):
        copies[3 + i].wait()
        out = pltpu.make_async_copy(kept.at[i], kept_o, out_sem.at[pairs + i])
        out.start()
        outs.append(out)
    for copy in copies[:3]:
        copy.wait()
    for j in range(pairs):
        spectrum = jnp.concatenate(
            [field[c, p, sub * j : sub * (j + 1), :] for p in range(nyp) for c in range(chunks)],
            axis=0,
        )
        smooth = dot3(spectrum.T, cas_z).reshape(pair, by, nz)
        here = pl.ds(pair * j, pair)
        search[here] = sample[here] + smooth
        out = pltpu.make_async_copy(search.at[here], search_o.at[here], out_sem.at[j])
        out.start()
        outs.append(out)
    for out in outs:
        out.wait()


def per_device(
    nxp,
    nyp,
    mean_field,
    log_scale,
    noise,
    wave_prev,
    wave_now,
    adjoint_next,
    adjoint_now,
    sources,
    receivers,
    observed,
    step_index,
    prior_scale,
):
    bx, by, nz = wave_now.shape
    chunks = CHUNKS
    constants = tables(bx, by, nz, nxp, nyp, chunks)
    small = [
        sources.T,
        receivers.T,
        observed.reshape(1, -1),
        step_index.reshape(1, 1),
        prior_scale.reshape(1, 1),
    ] + [jnp.asarray(table) for table in constants]
    pairs = bx * by // LANES
    share = nz // nyp
    sub = share // chunks
    total_y = by * nyp
    rows = sub * (total_y // LANES) // nxp
    field = jax.ShapeDtypeStruct((bx, by, nz), F32)
    hbm = pl.BlockSpec(memory_space=pltpu.HBM)
    anywhere = pl.BlockSpec(memory_space=pl.ANY)
    dma = pltpu.SemaphoreType.DMA
    whole = pltpu.VMEM((bx, by, nz), F32)
    padded = pltpu.VMEM((bx, by + 2 * PAD, nz), F32)
    scratch = [pltpu.VMEM(a.shape, a.dtype) for a in small]
    scratch += [whole] * 6 + [padded] * 2 + [whole] * 3
    scratch += [
        pltpu.VMEM((2, 2, REACH, by, nz), F32),
        pltpu.VMEM((2, 2, REACH * bx, nz), F32),
        pltpu.VMEM((2, 2, REACH * bx, nz), F32),
        pltpu.VMEM((nz, bx * by), F32),
        pltpu.VMEM((chunks, nyp, sub, bx * by), F32),
        pltpu.VMEM((chunks, pairs * sub, nyp * LANES), F32),
        pltpu.VMEM((chunks, nyp, pairs * sub, LANES), F32),
        pltpu.VMEM((chunks, nxp, 2 * rows, LANES), F32),
        pltpu.VMEM((chunks, nxp, 2 * rows, LANES), F32),
        pltpu.VMEM((chunks, nxp, 2 * rows, LANES), F32),
        pltpu.VMEM((chunks, nxp, 2 * rows, LANES), F32),
        dma((7,)),
        dma((SMALL,)),
        dma((4,)),
        dma((2, 2)),
        dma((2, 2)),
        dma((2, 2)),
        dma((2, 2)),
    ]
    scratch += [dma((chunks, bx // 4, nyp))] * 2 + [dma((chunks, nxp))] * 4 + [dma((chunks, nyp))] * 2
    scratch += [dma((chunks,))]
    spread = jax.ShapeDtypeStruct((chunks, nyp, pairs * sub, LANES), F32)
    wave, adjoint, sample, lgrad, spectrum = pl.pallas_call(
        functools.partial(kernel, nxp, nyp, chunks),
        out_shape=(field,) * 4 + (spread,),
        in_specs=[hbm] * (7 + len(small)),
        out_specs=(anywhere,) * 5,
        scratch_shapes=scratch,
        compiler_params=pltpu.CompilerParams(
            collective_id=0, has_side_effects=True, vmem_limit_bytes=63 * 2**20
        ),
    )(
        mean_field, log_scale, noise, wave_prev, wave_now, adjoint_next, adjoint_now, *small
    )
    return pl.pallas_call(
        finish,
        out_shape=(field,) * 4,
        in_specs=[anywhere] * 5 + [hbm],
        out_specs=(hbm,) * 4,
        scratch_shapes=[
            whole,
            pltpu.VMEM(spread.shape, F32),
            pltpu.VMEM((2, nz, nz), BF16),
            whole,
            pltpu.VMEM((3, bx, by, nz), F32),
            dma((6,)),
            dma((pairs + 3,)),
        ],
        compiler_params=pltpu.CompilerParams(vmem_limit_bytes=63 * 2**20),
    )(wave, adjoint, sample, lgrad, spectrum, small[7])


def solution(mesh):
    grid = P("gx", "gy", None)
    return jax.shard_map(
        functools.partial(per_device, mesh.shape["gx"], mesh.shape["gy"]),
        mesh=mesh,
        in_specs=(grid,) * 7 + (P(),) * 5,
        out_specs=(grid,) * 4,
        check_vma=False,
    )
```

```python
import functools
import math

import jax
import jax.numpy as jnp
import ml_dtypes
import numpy as np
from jax import lax
from jax.experimental import pallas as pl
from jax.experimental.pallas import tpu as pltpu
from jax.sharding import PartitionSpec as P

NSTEPS = 48
STENCIL_WEIGHTS = (-205.0 / 72.0, 8.0 / 5.0, -1.0 / 5.0, 8.0 / 315.0, -1.0 / 560.0)
COURANT_SQUARED = 0.08
VELOCITY_GAIN = 0.2
PULSE_FREQUENCY = 0.05
PULSE_AMPLITUDE = 20.0

REACH = 4
PAD = 8
LANES = 128
CHUNKS = 4
SMALL = 12
MESH = pl.DeviceIdType.MESH
F32 = jnp.float32
BF16 = jnp.bfloat16
NN = (((1,), (0,)), ((), ()))
NT = (((1,), (1,)), ((), ()))


def halves(table):
    high = table.astype(ml_dtypes.bfloat16)
    low = (table - high.astype(np.float64)).astype(ml_dtypes.bfloat16)
    return np.stack([high, low])


def cas(length):
    index = np.arange(length)
    angle = (index[:, None] * index[None, :] % length) * (2.0 * math.pi / length)
    return np.cos(angle) + np.sin(angle)


def wave_term(length):
    return (length / 8.0) ** 2 * 4.0 * np.sin(np.arange(length) * (math.pi / length)) ** 2


def tables(bx, by, nz, nxp, nyp, chunks):
    total_x, total_y = bx * nxp, by * nyp
    along_z = np.zeros((nz, nz))
    for o in range(1, REACH + 1):
        along_z += STENCIL_WEIGHTS[o] * (np.eye(nz, k=o) + np.eye(nz, k=-o))
    face_low = np.zeros((REACH, REACH))
    face_high = np.zeros((REACH, REACH))
    for i in range(REACH):
        for h in range(REACH):
            if h >= i:
                face_low[i, h] = STENCIL_WEIGHTS[i + REACH - h]
            if h <= i:
                face_high[i, h] = STENCIL_WEIGHTS[REACH + h - i]
    faces = np.stack([np.kron(np.eye(bx), face_low), np.kron(np.eye(bx), face_high)])
    pair = LANES // by
    weights_y = cas(total_y).reshape(nyp, by, total_y)
    forward_y = np.zeros((nyp, pair, by, pair, total_y))
    for s in range(pair):
        forward_y[:, s, :, s, :] = weights_y
    forward_y = forward_y.reshape(nyp * LANES, pair * total_y)
    c = (total_x / 8.0) ** 2
    d = 1.0 + wave_term(nz)[:, None] + wave_term(total_y)[None, :]
    log_r = -2.0 * np.arcsinh(0.5 * np.sqrt(d / c))
    r = np.exp(log_r)
    scale = math.sqrt(total_x * total_y * nz) / 8.0 / (nz * total_y)
    scale = scale / (c * -2.0 * np.sinh(log_r))
    closure = 1.0 / -np.expm1(total_x * log_r)
    share = nz // nyp
    sub = share // chunks
    tiles = total_y // LANES
    rows = sub * tiles // nxp
    segment = np.stack([np.exp(bx * log_r), closure])
    segment = segment.reshape(2, nyp, chunks, nxp // tiles, rows, tiles, LANES)
    segment = segment.transpose(1, 2, 3, 5, 0, 4, 6).reshape(nyp, chunks, nxp, 2, rows, LANES)
    as32 = lambda a: np.ascontiguousarray(a).astype(np.float32)
    return (
        as32(along_z),
        as32(faces),
        halves(cas(nz)),
        halves(forward_y),
        halves(forward_y.T),
        as32(np.stack([r, scale]).reshape(2, nyp, share, total_y)),
        as32(segment),
    )


def split(x):
    high = x.astype(BF16)
    return high, (x - high.astype(F32)).astype(BF16)


def split3(x):
    high = x.astype(BF16)
    rest = x - high.astype(F32)
    mid = rest.astype(BF16)
    return high, mid, (rest - mid.astype(F32)).astype(BF16)


def dot(a, b, dims=NN):
    return lax.dot_general(a, b, dims, preferred_element_type=F32)


def dot3(x, w):
    high, low = split(x)
    return dot(high, w[0]) + dot(high, w[1]) + dot(low, w[0])


def exact(a, b):
    return lax.dot_general(a, b, NN, precision=lax.Precision.HIGHEST, preferred_element_type=F32)


def kernel(
    nxp,
    nyp,
    chunks,
    mean_h,
    scale_h,
    noise_h,
    prev_h,
    now_h,
    anext_h,
    anow_h,
    *rest,
):
    small_h, rest = rest[:SMALL], rest[SMALL:]
    (wave_o, adj_o, sample_o, lgrad_o, irecv), rest = rest[:5], rest[5:]
    small, rest = rest[:SMALL], rest[SMALL:]
    (src_row, rec_row, observed, step, prior) = small[:5]
    (along_z, faces, cas_z, fwd_y, inv_y, line_tab, seg_tab) = small[5:]
    (
        mean,
        logs,
        noise,
        prev,
        anext,
        anow,
        wpad,
        bpad,
        curl,
        acurl,
        speed,
        xrecv,
        ysend,
        yrecv,
        zsend,
        zrecv,
        lines,
        isend,
        msend,
        mrecv,
        rsend,
        rrecv,
        lsem,
        tsem,
        osem,
        xs,
        xr,
        ys,
        yr,
        zs,
        zr,
        ms,
        mr,
        rs,
        rr,
        vs,
        vr,
        vsem,
    ) = rest
    bx, by, nz = mean.shape
    gx, gy = lax.axis_index("gx"), lax.axis_index("gy")
    pairs = bx * by // LANES
    pair = LANES // by
    share = nz // nyp
    sub = share // chunks
    total_y = by * nyp
    tiles = total_y // LANES
    rows = sub * tiles // nxp
    cells = bx * by
    centre = pl.ds(PAD, by)

    loads = [
        pltpu.make_async_copy(now_h, wpad.at[:, centre, :], lsem.at[0]),
        pltpu.make_async_copy(scale_h, logs, lsem.at[1]),
        pltpu.make_async_copy(noise_h, noise, lsem.at[2]),
        pltpu.make_async_copy(mean_h, mean, lsem.at[3]),
        pltpu.make_async_copy(anow_h, anow, lsem.at[4]),
        pltpu.make_async_copy(prev_h, prev, lsem.at[5]),
        pltpu.make_async_copy(anext_h, anext, lsem.at[6]),
    ]
    for load in loads:
        load.start()
    small_loads = [
        pltpu.make_async_copy(small_h[i], small[i], tsem.at[i]) for i in range(SMALL)
    ]
    for load in small_loads:
        load.start()

    for padded in (wpad, bpad):
        padded[:, 0:PAD, :] = jnp.zeros((bx, PAD, nz), F32)
        padded[:, PAD + by : by + 2 * PAD, :] = jnp.zeros((bx, PAD, nz), F32)
    outside = ((gx == 0, gx == nxp - 1), (gy == 0, gy == nyp - 1))
    for side in range(2):

        @pl.when(outside[0][side])
        def _():
            for field in range(2):
                xrecv[field, side] = jnp.zeros(xrecv.shape[2:], F32)

        @pl.when(outside[1][side])
        def _():
            for field in range(2):
                yrecv[field, side] = jnp.zeros(yrecv.shape[2:], F32)

    barrier = pltpu.get_barrier_semaphore()
    for i in range(1, nxp):
        pl.semaphore_signal(
            barrier, inc=1, device_id={"gx": lax.rem(gx + i, nxp)}, device_id_type=MESH
        )
    for i in range(1, nyp):
        pl.semaphore_signal(
            barrier, inc=1, device_id={"gy": lax.rem(gy + i, nyp)}, device_id_type=MESH
        )
    pl.semaphore_wait(barrier, nxp + nyp - 2)

    def rim_copy(axis, field, side, src):
        me, count = ((gx, nxp), (gy, nyp))[axis]
        target = lax.rem(me + (1 if side == 0 else count - 1), count)
        land, send, recv = ((xrecv, xs, xr), (yrecv, ys, yr))[axis]
        return pltpu.make_async_remote_copy(
            src_ref=src,
            dst_ref=land.at[field, side],
            send_sem=send.at[field, side],
            recv_sem=recv.at[field, side],
            device_id={("gx", "gy")[axis]: target},
            device_id_type=MESH,
        )

    def start_rim(axis, field, side, src):
        copy = rim_copy(axis, field, side, src)

        @pl.when(jnp.logical_not(outside[axis][1 - side]))
        def _():
            copy.start()

        return (axis, side, copy)

    rims = []
    rims.append(start_rim(0, 0, 0, now_h.at[pl.ds(bx - REACH, REACH)]))
    rims.append(start_rim(0, 0, 1, now_h.at[pl.ds(0, REACH)]))

    def pack_faces(field, padded):
        for x in range(bx):
            here = pl.ds(REACH * x, REACH)
            ysend[field, 0, here, :] = padded[x, PAD + by - REACH : PAD + by, :]
            ysend[field, 1, here, :] = padded[x, PAD : PAD + REACH, :]
        for side in range(2):
            rims.append(start_rim(1, field, side, ysend.at[field, side]))

    loads[0].wait()
    pack_faces(0, wpad)

    for load in loads[1:5]:
        load.wait()

    def pointwise(x):
        turned = jnp.exp(logs[x]) * noise[x]
        sample = mean[x] + turned
        logs[x] = turned
        mean[x] = sample
        fast = COURANT_SQUARED * jnp.exp(2.0 * VELOCITY_GAIN * sample)
        speed[x] = fast
        bpad[x, centre, :] = fast * anow[x]

    for x in range(REACH):
        pointwise(x)
    rims.append(start_rim(0, 1, 1, bpad.at[pl.ds(0, REACH), centre, :]))
    for x in range(bx - REACH, bx):
        pointwise(x)
    rims.append(start_rim(0, 1, 0, bpad.at[pl.ds(bx - REACH, REACH), centre, :]))
    for x in range(REACH, bx - REACH):
        pointwise(x)
    pack_faces(1, bpad)

    def inner_laplacian(padded, out):
        for x0 in range(0, bx, REACH):
            block = padded[x0 : x0 + REACH, PAD : PAD + by, :].reshape(REACH * by, nz)
            depthwise = exact(block, along_z[...]).reshape(REACH, by, nz)
            for x in range(x0, x0 + REACH):
                total = depthwise[x - x0] + 3.0 * STENCIL_WEIGHTS[0] * padded[x, centre, :]
                for o in range(1, REACH + 1):
                    near = padded[x, PAD + o : PAD + o + by, :] + padded[x, PAD - o : PAD - o + by, :]
                    if x + o < bx:
                        near = near + padded[x + o, centre, :]
                    if x - o >= 0:
                        near = near + padded[x - o, centre, :]
                    total = total + STENCIL_WEIGHTS[o] * near
                out[x] = total

    for load in small_loads:
        load.wait()
    inner_laplacian(wpad, curl)

    def codes(points):
        across = points[0:1, :] - gx * bx
        lateral = points[1:2, :] - gy * by
        inside = (across >= 0) & (across < bx) & (lateral >= 0) & (lateral < by)
        return jnp.where(inside, across * by + lateral, -1)

    src_code = codes(src_row)
    rec_code = codes(rec_row)

    def rim_terms(field, out):
        for side in range(2):
            terms = exact(faces[side], yrecv[field, side])
            first = 0 if side == 0 else by - REACH
            for x in range(bx):
                here = out[x, first : first + REACH, :]
                out[x, first : first + REACH, :] = here + terms[REACH * x : REACH * (x + 1), :]

    def x_rim(field, x):
        total = None
        for o in range(1, REACH + 1):
            if x - o < 0:
                term = STENCIL_WEIGHTS[o] * xrecv[field, 0, REACH + x - o]
                total = term if total is None else total + term
            if x + o >= bx:
                term = STENCIL_WEIGHTS[o] * xrecv[field, 1, x + o - bx]
                total = term if total is None else total + term
        return total

    def wait_rims(field_rims):
        for axis, side, copy in field_rims:

            @pl.when(jnp.logical_not(outside[axis][side]))
            def _():
                copy.wait_recv()

    inner_laplacian(bpad, acurl)
    loads[5].wait()
    loads[6].wait()

    wave_rims = rims[0:4]
    adj_rims = rims[4:8]
    wait_rims(wave_rims)
    rim_terms(0, curl)
    for x in range(bx):
        curved = curl[x]
        extra = x_rim(0, x)
        if extra is not None:
            curved = curved + extra
            curl[x] = curved
        prev[x] = 2.0 * wpad[x, centre, :] - prev[x] + speed[x] * curved

    moment = (step[...] - NSTEPS // 2).astype(F32) * (math.pi * PULSE_FREQUENCY)
    pulse = PULSE_AMPLITUDE * (1.0 - 2.0 * moment * moment) * jnp.exp(-moment * moment)
    nsrc, nrec = src_row.shape[1], rec_row.shape[1]
    src_level = lax.broadcasted_iota(jnp.int32, (nz, nsrc), 0) == src_row[2:3, :]
    src_level = src_level.astype(F32).astype(BF16)
    rec_level = lax.broadcasted_iota(jnp.int32, (nz, nrec), 0) == rec_row[2:3, :]
    rec_level = rec_level.astype(F32).astype(BF16)
    step_x = 4
    block = step_x * by
    picked = jnp.zeros((1, nrec), F32)
    for x0 in range(0, bx, step_x):
        cell = lax.broadcasted_iota(jnp.int32, (block, nsrc), 0) + x0 * by
        hit = (cell == src_code).astype(F32).astype(BF16)
        wave = prev[x0 : x0 + step_x].reshape(block, nz) + pulse * dot(hit, src_level, NT)
        prev[x0 : x0 + step_x] = wave.reshape(step_x, by, nz)
        traces = sum(dot(part, rec_level) for part in split3(wave))
        cell = lax.broadcasted_iota(jnp.int32, (block, nrec), 0) + x0 * by
        picked = picked + jnp.sum(
            jnp.where(cell == rec_code, traces, 0.0), axis=0, keepdims=True
        )
    wave_out = pltpu.make_async_copy(prev, wave_o, osem.at[0])
    wave_out.start()
    misfit = picked - observed[...]

    wait_rims(adj_rims)
    rim_terms(1, acurl)
    misfit_parts = split3(misfit)

    parts = bx // step_x

    def z_copy(c, i, part):
        to = lax.rem(gy + i, nyp)
        first = pl.multiple_of(to * share + c * sub, sub)
        across = pl.ds(0, cells) if part is None else pl.ds(part * block, block)
        slot = 0 if part is None else part
        return pltpu.make_async_remote_copy(
            src_ref=zsend.at[pl.ds(first, sub), across],
            dst_ref=zrecv.at[c, gy, :, across],
            send_sem=zs.at[c, slot, i],
            recv_sem=zr.at[c, slot, i],
            device_id={"gy": to},
            device_id_type=MESH,
        )

    def own_z(c):
        zrecv[c, gy] = zsend[pl.ds(pl.multiple_of(gy * share + c * sub, sub), sub), :]

    z_copies = [
        [z_copy(c, i, part) for part in (range(parts) if c == 0 else (None,)) for i in range(1, nyp)]
        for c in range(chunks)
    ]
    for x0 in range(0, bx, step_x):
        cell = lax.broadcasted_iota(jnp.int32, (block, nrec), 0) + x0 * by
        hit = cell == rec_code
        added = sum(
            dot(jnp.where(hit, part.astype(F32), 0.0).astype(BF16), rec_level, NT)
            for part in misfit_parts
        ).reshape(step_x, by, nz)
        for x in range(x0, x0 + step_x):
            total = acurl[x]
            extra = x_rim(1, x)
            if extra is not None:
                total = total + extra
            adjoint = 2.0 * anow[x] - anext[x] + total + added[x - x0]
            anext[x] = adjoint
            grad = (2.0 * VELOCITY_GAIN) * speed[x] * adjoint * curl[x]
            acurl[x] = grad
            anow[x] = grad * logs[x] - 1.0

        high, low = split(acurl[x0 : x0 + step_x].reshape(block, nz))
        zsend[:, x0 * by : x0 * by + block] = (
            dot(cas_z[0], high, NT) + dot(cas_z[1], high, NT) + dot(cas_z[0], low, NT)
        )
        part = x0 // step_x
        for copy in z_copies[0][part * (nyp - 1) : (part + 1) * (nyp - 1)]:
            copy.start()

    for copies in z_copies[1:]:
        for copy in copies:
            copy.start()

    adj_out = pltpu.make_async_copy(anext, adj_o, osem.at[1])
    adj_out.start()
    lgrad_out = pltpu.make_async_copy(anow, lgrad_o, osem.at[2])
    lgrad_out.start()
    sample_out = pltpu.make_async_copy(mean, sample_o, osem.at[3])
    sample_out.start()
    for c in range(chunks):
        own_z(c)

    def ratio(c):
        return line_tab[0, gy, c * sub : (c + 1) * sub, :]

    def at(c, x):
        first = (x // pair) * sub
        left = (x % pair) * total_y
        return lines[c, first : first + sub, left : left + total_y]

    def segment(o):
        return (
            slice((o // tiles) * rows, (o // tiles + 1) * rows),
            slice((o % tiles) * LANES, (o % tiles + 1) * LANES),
        )

    def small_copy(src, dst, send, recv, c, i):
        to = lax.rem(gx + i, nxp)
        return pltpu.make_async_remote_copy(
            src_ref=src.at[c, to],
            dst_ref=dst.at[c, gx],
            send_sem=send.at[c, i],
            recv_sem=recv.at[c, i],
            device_id={"gx": to},
            device_id_type=MESH,
        )

    m_copies, r_copies, v_copies, own_fields = [], [], [], []

    def lateral(c):
        for copy in z_copies[c]:
            copy.wait_recv()
        block = jnp.concatenate(
            [
                jnp.concatenate(
                    [zrecv[c, p, :, LANES * j : LANES * (j + 1)] for p in range(nyp)], axis=1
                )
                for j in range(pairs)
            ],
            axis=0,
        )
        lines[c] = dot3(block, fwd_y)
        r = ratio(c)
        up = at(c, 0)
        down = at(c, bx - 1)
        for x in range(1, bx):
            up = at(c, x) + r * up
            down = at(c, bx - 1 - x) + r * down
        for o in range(nxp):
            here = segment(o)
            msend[c, o, 0:rows, :] = up[here]
            msend[c, o, rows : 2 * rows, :] = down[here]
        copies = [small_copy(msend, mrecv, ms, mr, c, i) for i in range(1, nxp)]
        for copy in copies:
            copy.start()
        mrecv[c, gx] = msend[c, gx]
        m_copies.append(copies)

    def close(c):
        for copy in m_copies[c]:
            copy.wait_recv()
        decay = seg_tab[gy, c, gx, 0]
        closure = seg_tab[gy, c, gx, 1]
        ups = [mrecv[c, d, 0:rows, :] for d in range(nxp)]
        downs = [mrecv[c, d, rows : 2 * rows, :] for d in range(nxp)]
        up, down = ups[0], downs[nxp - 1]
        for d in range(1, nxp):
            up = ups[d] + decay * up
            down = downs[nxp - 1 - d] + decay * down
        up = up * closure
        down = down * closure
        for d in range(nxp):
            rsend[c, d, 0:rows, :] = up
            up = ups[d] + decay * up
        for d in range(nxp - 1, -1, -1):
            rsend[c, d, rows : 2 * rows, :] = down
            down = downs[d] + decay * down
        copies = [small_copy(rsend, rrecv, rs, rr, c, i) for i in range(1, nxp)]
        for copy in copies:
            copy.start()
        rrecv[c, gx] = rsend[c, gx]
        r_copies.append(copies)

    def back(c):
        for copy in r_copies[c]:
            copy.wait_recv()

        def whole(first):
            return jnp.concatenate(
                [
                    jnp.concatenate(
                        [rrecv[c, i * tiles + t, first : first + rows, :] for t in range(tiles)],
                        axis=1,
                    )
                    for i in range(nxp // tiles)
                ],
                axis=0,
            )

        r = ratio(c)
        gain = line_tab[1, gy, c * sub : (c + 1) * sub, :] * prior[...]
        up, down = whole(0), whole(rows)
        ups = []
        for x in range(bx):
            up = at(c, x) + r * up
            ups.append(up)
        for x in range(bx - 1, -1, -1):
            ahead = r * down
            here = at(c, x)
            down = here + ahead
            first = (x // pair) * sub
            left = (x % pair) * total_y
            lines[c, first : first + sub, left : left + total_y] = gain * (ups[x] + ahead)
        field = dot3(lines[c], inv_y)
        for p in range(nyp):
            isend[c, p] = field[:, LANES * p : LANES * (p + 1)]
        copies = []
        for i in range(1, nyp):
            to = lax.rem(gy + i, nyp)
            copies.append(
                pltpu.make_async_remote_copy(
                    src_ref=isend.at[c, to],
                    dst_ref=irecv.at[c, gy],
                    send_sem=vs.at[c, i],
                    recv_sem=vr.at[c, i],
                    device_id={"gy": to},
                    device_id_type=MESH,
                )
            )
        for copy in copies:
            copy.start()
        own = pltpu.make_async_copy(isend.at[c, gy], irecv.at[c, gy], vsem.at[c])
        own.start()
        own_fields.append(own)
        v_copies.append(copies)

    for stage in range(chunks + 2):
        if stage >= 2:
            back(stage - 2)
        if 1 <= stage <= chunks:
            close(stage - 1)
        if stage < chunks:
            lateral(stage)

    for c in range(chunks):
        for copy in v_copies[c]:
            copy.wait_recv()
    for own in own_fields:
        own.wait()
    for axis, side, copy in rims:

        @pl.when(jnp.logical_not(outside[axis][1 - side]))
        def _():
            copy.wait_send()

    for group in (z_copies, m_copies, r_copies, v_copies):
        for copies in group:
            for copy in copies:
                copy.wait_send()
    wave_out.wait()
    adj_out.wait()
    lgrad_out.wait()
    sample_out.wait()


def finish(
    wave,
    adjoint,
    sample_h,
    lgrad,
    field_h,
    cas_h,
    wave_o,
    adj_o,
    search_o,
    lgrad_o,
    sample,
    field,
    cas_z,
    search,
    kept,
    sem,
    out_sem,
):
    bx, by, nz = sample.shape
    pair = LANES // by
    pairs = bx // pair
    chunks, nyp, height, _ = field.shape
    sub = height // pairs
    copies = [
        pltpu.make_async_copy(field_h, field, sem.at[0]),
        pltpu.make_async_copy(cas_h, cas_z, sem.at[1]),
        pltpu.make_async_copy(sample_h, sample, sem.at[2]),
        pltpu.make_async_copy(wave, kept.at[0], sem.at[3]),
        pltpu.make_async_copy(adjoint, kept.at[1], sem.at[4]),
        pltpu.make_async_copy(lgrad, kept.at[2], sem.at[5]),
    ]
    for copy in copies[3:] + copies[:3]:
        copy.start()
    outs = []
    for i, kept_o in enumerate((wave_o, adj_o, lgrad_o)):
        copies[3 + i].wait()
        out = pltpu.make_async_copy(kept.at[i], kept_o, out_sem.at[pairs + i])
        out.start()
        outs.append(out)
    for copy in copies[:3]:
        copy.wait()
    for j in range(pairs):
        spectrum = jnp.concatenate(
            [field[c, p, sub * j : sub * (j + 1), :] for p in range(nyp) for c in range(chunks)],
            axis=0,
        )
        smooth = dot3(spectrum.T, cas_z).reshape(pair, by, nz)
        here = pl.ds(pair * j, pair)
        search[here] = sample[here] + smooth
        out = pltpu.make_async_copy(search.at[here], search_o.at[here], out_sem.at[j])
        out.start()
        outs.append(out)
    for out in outs:
        out.wait()


def per_device(
    nxp,
    nyp,
    mean_field,
    log_scale,
    noise,
    wave_prev,
    wave_now,
    adjoint_next,
    adjoint_now,
    sources,
    receivers,
    observed,
    step_index,
    prior_scale,
):
    bx, by, nz = wave_now.shape
    chunks = max(1, min(CHUNKS, nz // nyp // 8))
    constants = tables(bx, by, nz, nxp, nyp, chunks)
    small = [
        sources.T,
        receivers.T,
        observed.reshape(1, -1),
        step_index.reshape(1, 1),
        prior_scale.reshape(1, 1),
    ] + [jnp.asarray(table) for table in constants]
    pairs = bx * by // LANES
    share = nz // nyp
    sub = share // chunks
    total_y = by * nyp
    rows = sub * (total_y // LANES) // nxp
    field = jax.ShapeDtypeStruct((bx, by, nz), F32)
    hbm = pl.BlockSpec(memory_space=pltpu.HBM)
    anywhere = pl.BlockSpec(memory_space=pl.ANY)
    dma = pltpu.SemaphoreType.DMA
    whole = pltpu.VMEM((bx, by, nz), F32)
    padded = pltpu.VMEM((bx, by + 2 * PAD, nz), F32)
    scratch = [pltpu.VMEM(a.shape, a.dtype) for a in small]
    scratch += [whole] * 6 + [padded] * 2 + [whole] * 3
    scratch += [
        pltpu.VMEM((2, 2, REACH, by, nz), F32),
        pltpu.VMEM((2, 2, REACH * bx, nz), F32),
        pltpu.VMEM((2, 2, REACH * bx, nz), F32),
        pltpu.VMEM((nz, bx * by), F32),
        pltpu.VMEM((chunks, nyp, sub, bx * by), F32),
        pltpu.VMEM((chunks, pairs * sub, nyp * LANES), F32),
        pltpu.VMEM((chunks, nyp, pairs * sub, LANES), F32),
        pltpu.VMEM((chunks, nxp, 2 * rows, LANES), F32),
        pltpu.VMEM((chunks, nxp, 2 * rows, LANES), F32),
        pltpu.VMEM((chunks, nxp, 2 * rows, LANES), F32),
        pltpu.VMEM((chunks, nxp, 2 * rows, LANES), F32),
        dma((7,)),
        dma((SMALL,)),
        dma((4,)),
        dma((2, 2)),
        dma((2, 2)),
        dma((2, 2)),
        dma((2, 2)),
    ]
    scratch += [dma((chunks, bx // 4, nyp))] * 2 + [dma((chunks, nxp))] * 4 + [dma((chunks, nyp))] * 2
    scratch += [dma((chunks,))]
    spread = jax.ShapeDtypeStruct((chunks, nyp, pairs * sub, LANES), F32)
    wave, adjoint, sample, lgrad, spectrum = pl.pallas_call(
        functools.partial(kernel, nxp, nyp, chunks),
        out_shape=(field,) * 4 + (spread,),
        in_specs=[hbm] * (7 + len(small)),
        out_specs=(anywhere,) * 5,
        scratch_shapes=scratch,
        compiler_params=pltpu.CompilerParams(
            collective_id=0, has_side_effects=True, vmem_limit_bytes=63 * 2**20
        ),
    )(
        mean_field, log_scale, noise, wave_prev, wave_now, adjoint_next, adjoint_now, *small
    )
    return pl.pallas_call(
        finish,
        out_shape=(field,) * 4,
        in_specs=[anywhere] * 5 + [hbm],
        out_specs=(hbm,) * 4,
        scratch_shapes=[
            whole,
            pltpu.VMEM(spread.shape, F32),
            pltpu.VMEM((2, nz, nz), BF16),
            whole,
            pltpu.VMEM((3, bx, by, nz), F32),
            dma((6,)),
            dma((pairs + 3,)),
        ],
        compiler_params=pltpu.CompilerParams(vmem_limit_bytes=63 * 2**20),
    )(wave, adjoint, sample, lgrad, spectrum, small[7])


def solution(mesh):
    grid = P("gx", "gy", None)
    return jax.shard_map(
        functools.partial(per_device, mesh.shape["gx"], mesh.shape["gy"]),
        mesh=mesh,
        in_specs=(grid,) * 7 + (P(),) * 5,
        out_specs=(grid,) * 4,
        check_vma=False,
    )
```

```python
import functools
import math

import jax
import jax.numpy as jnp
import ml_dtypes
import numpy as np
from jax import lax
from jax.experimental import pallas as pl
from jax.experimental.pallas import tpu as pltpu
from jax.sharding import PartitionSpec as P

NSTEPS = 48
STENCIL_WEIGHTS = (-205.0 / 72.0, 8.0 / 5.0, -1.0 / 5.0, 8.0 / 315.0, -1.0 / 560.0)
COURANT_SQUARED = 0.08
VELOCITY_GAIN = 0.2
PULSE_FREQUENCY = 0.05
PULSE_AMPLITUDE = 20.0

REACH = 4
PAD = 8
LANES = 128
CHUNKS = 2
SMALL = 11
MESH = pl.DeviceIdType.MESH
F32 = jnp.float32
BF16 = jnp.bfloat16
NN = (((1,), (0,)), ((), ()))
NT = (((1,), (1,)), ((), ()))


def halves(table):
    high = table.astype(ml_dtypes.bfloat16)
    low = (table - high.astype(np.float64)).astype(ml_dtypes.bfloat16)
    return np.concatenate([high, low, high])


def cas(length):
    index = np.arange(length)
    angle = (index[:, None] * index[None, :] % length) * (2.0 * math.pi / length)
    return np.cos(angle) + np.sin(angle)


def wave_term(length):
    return (length / 8.0) ** 2 * 4.0 * np.sin(np.arange(length) * (math.pi / length)) ** 2


def tables(bx, by, nz, nxp, nyp, chunks):
    total_x, total_y = bx * nxp, by * nyp
    along_z = np.zeros((nz, nz))
    for o in range(1, REACH + 1):
        along_z += STENCIL_WEIGHTS[o] * (np.eye(nz, k=o) + np.eye(nz, k=-o))
    face_low = np.zeros((REACH, REACH))
    face_high = np.zeros((REACH, REACH))
    for i in range(REACH):
        for h in range(REACH):
            if h >= i:
                face_low[i, h] = STENCIL_WEIGHTS[i + REACH - h]
            if h <= i:
                face_high[i, h] = STENCIL_WEIGHTS[REACH + h - i]
    faces = np.stack([np.kron(np.eye(bx), face_low), np.kron(np.eye(bx), face_high)])
    c = (total_x / 8.0) ** 2
    d = 1.0 + wave_term(nz)[:, None] + wave_term(total_y)[None, :]
    log_r = -2.0 * np.arcsinh(0.5 * np.sqrt(d / c))
    r = np.exp(log_r)
    scale = math.sqrt(total_x * total_y * nz) / 8.0 / (nz * total_y)
    scale = scale / (c * -2.0 * np.sinh(log_r))
    closure = 1.0 / -np.expm1(total_x * log_r)
    share = nz // nyp
    sub = share // chunks
    tiles = total_y // LANES
    rows = sub * tiles // nxp
    segment = np.stack([np.exp(bx * log_r), closure])
    segment = segment.reshape(2, nyp, chunks, nxp // tiles, rows, tiles, LANES)
    segment = segment.transpose(1, 2, 3, 5, 0, 4, 6).reshape(nyp, chunks, nxp, 2, rows, LANES)
    as32 = lambda a: np.ascontiguousarray(a).astype(np.float32)
    return (
        as32(along_z),
        as32(faces),
        halves(cas(nz)),
        halves(cas(total_y)),
        as32(np.stack([r, scale]).reshape(2, nyp, share, total_y)),
        as32(segment),
    )


def split(x):
    high = x.astype(BF16)
    return high, (x - high.astype(F32)).astype(BF16)


def split3(x):
    high = x.astype(BF16)
    rest = x - high.astype(F32)
    mid = rest.astype(BF16)
    return high, mid, (rest - mid.astype(F32)).astype(BF16)


def dot(a, b, dims=NN):
    return lax.dot_general(a, b, dims, preferred_element_type=F32)


def parts3(x):
    high, low = split(x)
    return jnp.concatenate([high, high, low], axis=1)


def dot3(x, w):
    return dot(parts3(x), w[...])


def trade(left, right):
    half = LANES // 2
    low = lax.broadcasted_iota(jnp.int32, left.shape, 1) < half
    first = jnp.where(low, left, pltpu.roll(right, half, 1))
    second = jnp.where(low, pltpu.roll(left, half, 1), right)
    return first, second


def exact(a, b):
    return lax.dot_general(a, b, NN, precision=lax.Precision.HIGHEST, preferred_element_type=F32)


def kernel(
    nxp,
    nyp,
    chunks,
    mean_h,
    scale_h,
    noise_h,
    prev_h,
    now_h,
    anext_h,
    anow_h,
    *rest,
):
    small_h, rest = rest[:SMALL], rest[SMALL:]
    (wave_o, adj_o, sample_o, lgrad_o, irecv), rest = rest[:5], rest[5:]
    small, rest = rest[:SMALL], rest[SMALL:]
    (src_row, rec_row, observed, step, prior) = small[:5]
    (along_z, faces, cas_z, cas_y, line_tab, seg_tab) = small[5:]
    (
        mean,
        logs,
        noise,
        prev,
        anext,
        anow,
        wpad,
        bpad,
        curl,
        acurl,
        speed,
        xrecv,
        ysend,
        yrecv,
        zsend,
        zrecv,
        lines,
        isend,
        msend,
        mrecv,
        rsend,
        rrecv,
        hits,
        lsem,
        tsem,
        osem,
        xs,
        xr,
        ys,
        yr,
        zs,
        zr,
        ms,
        mr,
        rs,
        rr,
        vs,
        vr,
        vsem,
    ) = rest
    bx, by, nz = mean.shape
    gx, gy = lax.axis_index("gx"), lax.axis_index("gy")
    pairs = bx * by // LANES
    pair = LANES // by
    share = nz // nyp
    sub = share // chunks
    total_y = by * nyp
    tiles = total_y // LANES
    rows = sub * tiles // nxp
    cells = bx * by
    centre = pl.ds(PAD, by)

    loads = [
        pltpu.make_async_copy(now_h, wpad.at[:, centre, :], lsem.at[0]),
        pltpu.make_async_copy(scale_h, logs, lsem.at[1]),
        pltpu.make_async_copy(noise_h, noise, lsem.at[2]),
        pltpu.make_async_copy(mean_h, mean, lsem.at[3]),
        pltpu.make_async_copy(anow_h, anow, lsem.at[4]),
        pltpu.make_async_copy(prev_h, prev, lsem.at[5]),
        pltpu.make_async_copy(anext_h, anext, lsem.at[6]),
    ]
    for load in loads:
        load.start()
    small_loads = [
        pltpu.make_async_copy(small_h[i], small[i], tsem.at[i]) for i in range(SMALL)
    ]
    for load in small_loads:
        load.start()

    for padded in (wpad, bpad):
        padded[:, 0:PAD, :] = jnp.zeros((bx, PAD, nz), F32)
        padded[:, PAD + by : by + 2 * PAD, :] = jnp.zeros((bx, PAD, nz), F32)
    outside = ((gx == 0, gx == nxp - 1), (gy == 0, gy == nyp - 1))
    for side in range(2):

        @pl.when(outside[0][side])
        def _():
            for field in range(2):
                xrecv[field, side] = jnp.zeros(xrecv.shape[2:], F32)

        @pl.when(outside[1][side])
        def _():
            for field in range(2):
                yrecv[field, side] = jnp.zeros(yrecv.shape[2:], F32)

    barrier = pltpu.get_barrier_semaphore()
    for i in range(1, nxp):
        pl.semaphore_signal(
            barrier, inc=1, device_id={"gx": lax.rem(gx + i, nxp)}, device_id_type=MESH
        )
    for i in range(1, nyp):
        pl.semaphore_signal(
            barrier, inc=1, device_id={"gy": lax.rem(gy + i, nyp)}, device_id_type=MESH
        )
    pl.semaphore_wait(barrier, nxp + nyp - 2)

    def rim_copy(axis, field, side, src):
        me, count = ((gx, nxp), (gy, nyp))[axis]
        target = lax.rem(me + (1 if side == 0 else count - 1), count)
        land, send, recv = ((xrecv, xs, xr), (yrecv, ys, yr))[axis]
        return pltpu.make_async_remote_copy(
            src_ref=src,
            dst_ref=land.at[field, side],
            send_sem=send.at[field, side],
            recv_sem=recv.at[field, side],
            device_id={("gx", "gy")[axis]: target},
            device_id_type=MESH,
        )

    def start_rim(axis, field, side, src):
        copy = rim_copy(axis, field, side, src)

        @pl.when(jnp.logical_not(outside[axis][1 - side]))
        def _():
            copy.start()

        return (axis, side, copy)

    rims = []
    rims.append(start_rim(0, 0, 0, now_h.at[pl.ds(bx - REACH, REACH)]))
    rims.append(start_rim(0, 0, 1, now_h.at[pl.ds(0, REACH)]))

    def pack_faces(field, padded):
        for x in range(bx):
            here = pl.ds(REACH * x, REACH)
            ysend[field, 0, here, :] = padded[x, PAD + by - REACH : PAD + by, :]
            ysend[field, 1, here, :] = padded[x, PAD : PAD + REACH, :]
        for side in range(2):
            rims.append(start_rim(1, field, side, ysend.at[field, side]))

    loads[0].wait()
    pack_faces(0, wpad)

    for load in loads[1:5]:
        load.wait()

    def pointwise(x):
        turned = jnp.exp(logs[x]) * noise[x]
        sample = mean[x] + turned
        logs[x] = turned
        mean[x] = sample
        fast = COURANT_SQUARED * jnp.exp(2.0 * VELOCITY_GAIN * sample)
        speed[x] = fast
        bpad[x, centre, :] = fast * anow[x]

    for x in range(REACH):
        pointwise(x)
    rims.append(start_rim(0, 1, 1, bpad.at[pl.ds(0, REACH), centre, :]))
    for x in range(bx - REACH, bx):
        pointwise(x)
    rims.append(start_rim(0, 1, 0, bpad.at[pl.ds(bx - REACH, REACH), centre, :]))
    for x in range(REACH, bx - REACH):
        pointwise(x)
    pack_faces(1, bpad)

    def inner_laplacian(padded, out):
        for x0 in range(0, bx, REACH):
            block = padded[x0 : x0 + REACH, PAD : PAD + by, :].reshape(REACH * by, nz)
            depthwise = exact(block, along_z[...]).reshape(REACH, by, nz)
            for x in range(x0, x0 + REACH):
                total = depthwise[x - x0] + 3.0 * STENCIL_WEIGHTS[0] * padded[x, centre, :]
                for o in range(1, REACH + 1):
                    near = padded[x, PAD + o : PAD + o + by, :] + padded[x, PAD - o : PAD - o + by, :]
                    if x + o < bx:
                        near = near + padded[x + o, centre, :]
                    if x - o >= 0:
                        near = near + padded[x - o, centre, :]
                    total = total + STENCIL_WEIGHTS[o] * near
                out[x] = total

    for load in small_loads:
        load.wait()
    inner_laplacian(wpad, curl)

    def codes(points):
        across = points[0:1, :] - gx * bx
        lateral = points[1:2, :] - gy * by
        inside = (across >= 0) & (across < bx) & (lateral >= 0) & (lateral < by)
        return jnp.where(inside, across * by + lateral, -1)

    src_code = codes(src_row)
    rec_code = codes(rec_row)

    def rim_terms(field, out):
        for side in range(2):
            terms = exact(faces[side], yrecv[field, side])
            first = 0 if side == 0 else by - REACH
            for x in range(bx):
                here = out[x, first : first + REACH, :]
                out[x, first : first + REACH, :] = here + terms[REACH * x : REACH * (x + 1), :]

    def x_rim(field, x):
        total = None
        for o in range(1, REACH + 1):
            if x - o < 0:
                term = STENCIL_WEIGHTS[o] * xrecv[field, 0, REACH + x - o]
                total = term if total is None else total + term
            if x + o >= bx:
                term = STENCIL_WEIGHTS[o] * xrecv[field, 1, x + o - bx]
                total = term if total is None else total + term
        return total

    def wait_rims(field_rims):
        for axis, side, copy in field_rims:

            @pl.when(jnp.logical_not(outside[axis][side]))
            def _():
                copy.wait_recv()

    inner_laplacian(bpad, acurl)
    loads[5].wait()
    loads[6].wait()

    wave_rims = rims[0:4]
    adj_rims = rims[4:8]
    wait_rims(wave_rims)
    rim_terms(0, curl)
    for x in range(bx):
        curved = curl[x]
        extra = x_rim(0, x)
        if extra is not None:
            curved = curved + extra
            curl[x] = curved
        prev[x] = 2.0 * wpad[x, centre, :] - prev[x] + speed[x] * curved

    moment = (step[...] - NSTEPS // 2).astype(F32) * (math.pi * PULSE_FREQUENCY)
    pulse = PULSE_AMPLITUDE * (1.0 - 2.0 * moment * moment) * jnp.exp(-moment * moment)
    nsrc, nrec = src_row.shape[1], rec_row.shape[1]
    src_level = lax.broadcasted_iota(jnp.int32, (nz, nsrc), 0) == src_row[2:3, :]
    src_level = src_level.astype(F32).astype(BF16)
    rec_level = lax.broadcasted_iota(jnp.int32, (nz, nrec), 0) == rec_row[2:3, :]
    rec_level = rec_level.astype(F32)
    level3 = jnp.concatenate([rec_level.astype(BF16)] * 3, axis=0)
    step_x = 4
    block = step_x * by
    picked = jnp.zeros((1, nrec), F32)
    for x0 in range(0, bx, step_x):
        cell = lax.broadcasted_iota(jnp.int32, (block, nsrc), 0) + x0 * by
        hit = (cell == src_code).astype(F32).astype(BF16)
        wave = prev[x0 : x0 + step_x].reshape(block, nz) + pulse * dot(hit, src_level, NT)
        prev[x0 : x0 + step_x] = wave.reshape(step_x, by, nz)
        traces = dot(jnp.concatenate(split3(wave), axis=1), level3)
        cell = lax.broadcasted_iota(jnp.int32, (block, nrec), 0) + x0 * by
        hit = cell == rec_code
        hits[x0 * by : x0 * by + block, :] = hit.astype(F32).astype(BF16)
        picked = picked + jnp.sum(
            jnp.where(hit, traces, 0.0), axis=0, keepdims=True
        )
    wave_out = pltpu.make_async_copy(prev, wave_o, osem.at[0])
    wave_out.start()
    misfit = picked - observed[...]

    wait_rims(adj_rims)
    rim_terms(1, acurl)
    misfit3 = jnp.concatenate(split3(rec_level * misfit), axis=1)

    cas_side = jnp.concatenate([cas_z[nz * i : nz * (i + 1), :] for i in range(3)], axis=1)

    parts = bx // step_x

    def z_copy(c, i, part):
        to = lax.rem(gy + i, nyp)
        first = pl.multiple_of(to * share + c * sub, sub)
        across = pl.ds(0, cells) if part is None else pl.ds(part * block, block)
        slot = 0 if part is None else part
        return pltpu.make_async_remote_copy(
            src_ref=zsend.at[pl.ds(first, sub), across],
            dst_ref=zrecv.at[c, gy, :, across],
            send_sem=zs.at[c, slot, i],
            recv_sem=zr.at[c, slot, i],
            device_id={"gy": to},
            device_id_type=MESH,
        )

    def own_z(c):
        zrecv[c, gy] = zsend[pl.ds(pl.multiple_of(gy * share + c * sub, sub), sub), :]

    z_copies = [
        [z_copy(c, i, part) for part in (range(parts) if c == 0 else (None,)) for i in range(1, nyp)]
        for c in range(chunks)
    ]
    for x0 in range(0, bx, step_x):
        hit = hits[x0 * by : x0 * by + block, :]
        added = dot(jnp.concatenate([hit] * 3, axis=1), misfit3, NT).reshape(step_x, by, nz)
        for x in range(x0, x0 + step_x):
            total = acurl[x]
            extra = x_rim(1, x)
            if extra is not None:
                total = total + extra
            adjoint = 2.0 * anow[x] - anext[x] + total + added[x - x0]
            anext[x] = adjoint
            grad = (2.0 * VELOCITY_GAIN) * speed[x] * adjoint * curl[x]
            acurl[x] = grad
            anow[x] = grad * logs[x] - 1.0

        zsend[:, x0 * by : x0 * by + block] = dot(
            cas_side, parts3(acurl[x0 : x0 + step_x].reshape(block, nz)), NT
        )
        part = x0 // step_x
        for copy in z_copies[0][part * (nyp - 1) : (part + 1) * (nyp - 1)]:
            copy.start()

    for copies in z_copies[1:]:
        for copy in copies:
            copy.start()

    adj_out = pltpu.make_async_copy(anext, adj_o, osem.at[1])
    adj_out.start()
    lgrad_out = pltpu.make_async_copy(anow, lgrad_o, osem.at[2])
    lgrad_out.start()
    sample_out = pltpu.make_async_copy(mean, sample_o, osem.at[3])
    sample_out.start()
    for c in range(chunks):
        own_z(c)

    def ratio(c):
        return line_tab[0, gy, c * sub : (c + 1) * sub, :]

    def at(c, x):
        return lines[c, x * sub : (x + 1) * sub, :]

    def segment(o):
        return (
            slice((o // tiles) * rows, (o // tiles + 1) * rows),
            slice((o % tiles) * LANES, (o % tiles + 1) * LANES),
        )

    def small_copy(src, dst, send, recv, c, i):
        to = lax.rem(gx + i, nxp)
        return pltpu.make_async_remote_copy(
            src_ref=src.at[c, to],
            dst_ref=dst.at[c, gx],
            send_sem=send.at[c, i],
            recv_sem=recv.at[c, i],
            device_id={"gx": to},
            device_id_type=MESH,
        )

    m_copies, r_copies, v_copies, own_fields = [], [], [], []

    def lateral(c):
        for copy in z_copies[c]:
            copy.wait_recv()
        rows_of = [[] for _ in range(bx)]
        for j in range(pairs):
            here = [zrecv[c, p, :, LANES * j : LANES * (j + 1)] for p in range(nyp)]
            for p in range(0, nyp, 2):
                first, second = trade(here[p], here[p + 1])
                rows_of[2 * j].append(first)
                rows_of[2 * j + 1].append(second)
        block = jnp.concatenate([jnp.concatenate(row, axis=1) for row in rows_of], axis=0)
        lines[c] = dot3(block, cas_y)
        r = ratio(c)
        up = at(c, 0)
        down = at(c, bx - 1)
        for x in range(1, bx):
            up = at(c, x) + r * up
            down = at(c, bx - 1 - x) + r * down
        for o in range(nxp):
            here = segment(o)
            msend[c, o, 0:rows, :] = up[here]
            msend[c, o, rows : 2 * rows, :] = down[here]
        copies = [small_copy(msend, mrecv, ms, mr, c, i) for i in range(1, nxp)]
        for copy in copies:
            copy.start()
        mrecv[c, gx] = msend[c, gx]
        m_copies.append(copies)

    def close(c):
        for copy in m_copies[c]:
            copy.wait_recv()
        decay = seg_tab[gy, c, gx, 0]
        closure = seg_tab[gy, c, gx, 1]
        ups = [mrecv[c, d, 0:rows, :] for d in range(nxp)]
        downs = [mrecv[c, d, rows : 2 * rows, :] for d in range(nxp)]
        up, down = ups[0], downs[nxp - 1]
        for d in range(1, nxp):
            up = ups[d] + decay * up
            down = downs[nxp - 1 - d] + decay * down
        up = up * closure
        down = down * closure
        for d in range(nxp):
            rsend[c, d, 0:rows, :] = up
            up = ups[d] + decay * up
        for d in range(nxp - 1, -1, -1):
            rsend[c, d, rows : 2 * rows, :] = down
            down = downs[d] + decay * down
        copies = [small_copy(rsend, rrecv, rs, rr, c, i) for i in range(1, nxp)]
        for copy in copies:
            copy.start()
        rrecv[c, gx] = rsend[c, gx]
        r_copies.append(copies)

    def back(c):
        for copy in r_copies[c]:
            copy.wait_recv()

        def whole(first):
            return jnp.concatenate(
                [
                    jnp.concatenate(
                        [rrecv[c, i * tiles + t, first : first + rows, :] for t in range(tiles)],
                        axis=1,
                    )
                    for i in range(nxp // tiles)
                ],
                axis=0,
            )

        r = ratio(c)
        gain = line_tab[1, gy, c * sub : (c + 1) * sub, :] * prior[...]
        up, down = whole(0), whole(rows)
        ups = []
        for x in range(bx):
            up = at(c, x) + r * up
            ups.append(up)
        for x in range(bx - 1, -1, -1):
            ahead = r * down
            here = at(c, x)
            down = here + ahead
            lines[c, x * sub : (x + 1) * sub, :] = gain * (ups[x] + ahead)
        out = dot3(lines[c], cas_y)
        for j in range(pairs):
            one = out[2 * j * sub : (2 * j + 1) * sub, :]
            two = out[(2 * j + 1) * sub : (2 * j + 2) * sub, :]
            for p in range(0, nyp, 2):
                here = slice(p * by, (p + 2) * by)
                first, second = trade(one[:, here], two[:, here])
                isend[c, p, sub * j : sub * (j + 1), :] = first
                isend[c, p + 1, sub * j : sub * (j + 1), :] = second
        copies = []
        for i in range(1, nyp):
            to = lax.rem(gy + i, nyp)
            copies.append(
                pltpu.make_async_remote_copy(
                    src_ref=isend.at[c, to],
                    dst_ref=irecv.at[c, gy],
                    send_sem=vs.at[c, i],
                    recv_sem=vr.at[c, i],
                    device_id={"gy": to},
                    device_id_type=MESH,
                )
            )
        for copy in copies:
            copy.start()
        own = pltpu.make_async_copy(isend.at[c, gy], irecv.at[c, gy], vsem.at[c])
        own.start()
        own_fields.append(own)
        v_copies.append(copies)

    for stage in range(chunks + 2):
        if stage >= 2:
            back(stage - 2)
        if 1 <= stage <= chunks:
            close(stage - 1)
        if stage < chunks:
            lateral(stage)

    for c in range(chunks):
        for copy in v_copies[c]:
            copy.wait_recv()
    for own in own_fields:
        own.wait()
    for axis, side, copy in rims:

        @pl.when(jnp.logical_not(outside[axis][1 - side]))
        def _():
            copy.wait_send()

    for group in (z_copies, m_copies, r_copies, v_copies):
        for copies in group:
            for copy in copies:
                copy.wait_send()
    wave_out.wait()
    adj_out.wait()
    lgrad_out.wait()
    sample_out.wait()


def finish(
    wave,
    adjoint,
    sample_h,
    lgrad,
    field_h,
    cas_h,
    wave_o,
    adj_o,
    search_o,
    lgrad_o,
    sample,
    field,
    cas_z,
    search,
    kept,
    sem,
    out_sem,
):
    bx, by, nz = sample.shape
    pair = LANES // by
    pairs = bx // pair
    chunks, nyp, height, _ = field.shape
    sub = height // pairs
    copies = [
        pltpu.make_async_copy(field_h, field, sem.at[0]),
        pltpu.make_async_copy(cas_h, cas_z, sem.at[1]),
        pltpu.make_async_copy(sample_h, sample, sem.at[2]),
        pltpu.make_async_copy(wave, kept.at[0], sem.at[3]),
        pltpu.make_async_copy(adjoint, kept.at[1], sem.at[4]),
        pltpu.make_async_copy(lgrad, kept.at[2], sem.at[5]),
    ]
    for copy in copies[3:] + copies[:3]:
        copy.start()
    outs = []
    for i, kept_o in enumerate((wave_o, adj_o, lgrad_o)):
        copies[3 + i].wait()
        out = pltpu.make_async_copy(kept.at[i], kept_o, out_sem.at[pairs + i])
        out.start()
        outs.append(out)
    for copy in copies[:3]:
        copy.wait()
    for j in range(pairs):
        spectrum = jnp.concatenate(
            [field[c, p, sub * j : sub * (j + 1), :] for p in range(nyp) for c in range(chunks)],
            axis=0,
        )
        smooth = dot3(spectrum.T, cas_z).reshape(pair, by, nz)
        here = pl.ds(pair * j, pair)
        search[here] = sample[here] + smooth
        out = pltpu.make_async_copy(search.at[here], search_o.at[here], out_sem.at[j])
        out.start()
        outs.append(out)
    for out in outs:
        out.wait()


def per_device(
    nxp,
    nyp,
    mean_field,
    log_scale,
    noise,
    wave_prev,
    wave_now,
    adjoint_next,
    adjoint_now,
    sources,
    receivers,
    observed,
    step_index,
    prior_scale,
):
    bx, by, nz = wave_now.shape
    chunks = max(1, min(CHUNKS, nz // nyp // 8))
    constants = tables(bx, by, nz, nxp, nyp, chunks)
    small = [
        sources.T,
        receivers.T,
        observed.reshape(1, -1),
        step_index.reshape(1, 1),
        prior_scale.reshape(1, 1),
    ] + [jnp.asarray(table) for table in constants]
    pairs = bx * by // LANES
    share = nz // nyp
    sub = share // chunks
    total_y = by * nyp
    rows = sub * (total_y // LANES) // nxp
    field = jax.ShapeDtypeStruct((bx, by, nz), F32)
    hbm = pl.BlockSpec(memory_space=pltpu.HBM)
    anywhere = pl.BlockSpec(memory_space=pl.ANY)
    dma = pltpu.SemaphoreType.DMA
    whole = pltpu.VMEM((bx, by, nz), F32)
    padded = pltpu.VMEM((bx, by + 2 * PAD, nz), F32)
    scratch = [pltpu.VMEM(a.shape, a.dtype) for a in small]
    scratch += [whole] * 6 + [padded] * 2 + [whole] * 3
    scratch += [
        pltpu.VMEM((2, 2, REACH, by, nz), F32),
        pltpu.VMEM((2, 2, REACH * bx, nz), F32),
        pltpu.VMEM((2, 2, REACH * bx, nz), F32),
        pltpu.VMEM((nz, bx * by), F32),
        pltpu.VMEM((chunks, nyp, sub, bx * by), F32),
        pltpu.VMEM((chunks, bx * sub, total_y), F32),
        pltpu.VMEM((chunks, nyp, pairs * sub, LANES), F32),
        pltpu.VMEM((chunks, nxp, 2 * rows, LANES), F32),
        pltpu.VMEM((chunks, nxp, 2 * rows, LANES), F32),
        pltpu.VMEM((chunks, nxp, 2 * rows, LANES), F32),
        pltpu.VMEM((chunks, nxp, 2 * rows, LANES), F32),
        pltpu.VMEM((bx * by, receivers.shape[0]), BF16),
        dma((7,)),
        dma((SMALL,)),
        dma((4,)),
        dma((2, 2)),
        dma((2, 2)),
        dma((2, 2)),
        dma((2, 2)),
    ]
    scratch += [dma((chunks, bx // 4, nyp))] * 2 + [dma((chunks, nxp))] * 4 + [dma((chunks, nyp))] * 2
    scratch += [dma((chunks,))]
    spread = jax.ShapeDtypeStruct((chunks, nyp, pairs * sub, LANES), F32)
    wave, adjoint, sample, lgrad, spectrum = pl.pallas_call(
        functools.partial(kernel, nxp, nyp, chunks),
        out_shape=(field,) * 4 + (spread,),
        in_specs=[hbm] * (7 + len(small)),
        out_specs=(anywhere,) * 5,
        scratch_shapes=scratch,
        compiler_params=pltpu.CompilerParams(
            collective_id=0, has_side_effects=True, vmem_limit_bytes=63 * 2**20
        ),
    )(
        mean_field, log_scale, noise, wave_prev, wave_now, adjoint_next, adjoint_now, *small
    )
    return pl.pallas_call(
        finish,
        out_shape=(field,) * 4,
        in_specs=[anywhere] * 5 + [hbm],
        out_specs=(hbm,) * 4,
        scratch_shapes=[
            whole,
            pltpu.VMEM(spread.shape, F32),
            pltpu.VMEM(small[7].shape, BF16),
            whole,
            pltpu.VMEM((3, bx, by, nz), F32),
            dma((6,)),
            dma((pairs + 3,)),
        ],
        compiler_params=pltpu.CompilerParams(vmem_limit_bytes=63 * 2**20),
    )(wave, adjoint, sample, lgrad, spectrum, small[7])


def solution(mesh):
    grid = P("gx", "gy", None)
    return jax.shard_map(
        functools.partial(per_device, mesh.shape["gx"], mesh.shape["gy"]),
        mesh=mesh,
        in_specs=(grid,) * 7 + (P(),) * 5,
        out_specs=(grid,) * 4,
        check_vma=False,
    )
```

```python
import functools
import math

import jax
import jax.numpy as jnp
import ml_dtypes
import numpy as np
from jax import lax
from jax.experimental import pallas as pl
from jax.experimental.pallas import tpu as pltpu
from jax.sharding import PartitionSpec as P

NSTEPS = 48
STENCIL_WEIGHTS = (-205.0 / 72.0, 8.0 / 5.0, -1.0 / 5.0, 8.0 / 315.0, -1.0 / 560.0)
COURANT_SQUARED = 0.08
VELOCITY_GAIN = 0.2
PULSE_FREQUENCY = 0.05
PULSE_AMPLITUDE = 20.0

REACH = 4
PAD = 8
LANES = 128
CHUNKS = 2
SMALL = 11
MESH = pl.DeviceIdType.MESH
F32 = jnp.float32
BF16 = jnp.bfloat16
NN = (((1,), (0,)), ((), ()))
NT = (((1,), (1,)), ((), ()))


def halves(table):
    high = table.astype(ml_dtypes.bfloat16)
    low = (table - high.astype(np.float64)).astype(ml_dtypes.bfloat16)
    return np.concatenate([high, low, high])


def thirds(table):
    parts = []
    for _ in range(3):
        part = table.astype(ml_dtypes.bfloat16)
        table = table - part.astype(np.float64)
        parts.append(part)
    high, mid, low = parts
    return np.concatenate([high, mid, low, high, mid, high])


def cas(length):
    index = np.arange(length)
    angle = (index[:, None] * index[None, :] % length) * (2.0 * math.pi / length)
    return np.cos(angle) + np.sin(angle)


def wave_term(length):
    return (length / 8.0) ** 2 * 4.0 * np.sin(np.arange(length) * (math.pi / length)) ** 2


def tables(bx, by, nz, nxp, nyp, chunks):
    total_x, total_y = bx * nxp, by * nyp
    along_z = np.zeros((nz, nz))
    for o in range(1, REACH + 1):
        along_z += STENCIL_WEIGHTS[o] * (np.eye(nz, k=o) + np.eye(nz, k=-o))
    face_low = np.zeros((REACH, REACH))
    face_high = np.zeros((REACH, REACH))
    for i in range(REACH):
        for h in range(REACH):
            if h >= i:
                face_low[i, h] = STENCIL_WEIGHTS[i + REACH - h]
            if h <= i:
                face_high[i, h] = STENCIL_WEIGHTS[REACH + h - i]
    faces = np.stack([np.kron(np.eye(bx), face_low), np.kron(np.eye(bx), face_high)])
    c = (total_x / 8.0) ** 2
    d = 1.0 + wave_term(nz)[:, None] + wave_term(total_y)[None, :]
    log_r = -2.0 * np.arcsinh(0.5 * np.sqrt(d / c))
    r = np.exp(log_r)
    scale = math.sqrt(total_x * total_y * nz) / 8.0 / (nz * total_y)
    scale = scale / (c * -2.0 * np.sinh(log_r))
    closure = 1.0 / -np.expm1(total_x * log_r)
    share = nz // nyp
    sub = share // chunks
    tiles = total_y // LANES
    rows = sub * tiles // nxp
    segment = np.stack([np.exp(bx * log_r), closure])
    segment = segment.reshape(2, nyp, chunks, nxp // tiles, rows, tiles, LANES)
    segment = segment.transpose(1, 2, 3, 5, 0, 4, 6).reshape(nyp, chunks, nxp, 2, rows, LANES)
    as32 = lambda a: np.ascontiguousarray(a).astype(np.float32)
    return (
        thirds(along_z),
        as32(faces),
        halves(cas(nz)),
        halves(cas(total_y)),
        as32(np.stack([r, scale]).reshape(2, nyp, share, total_y)),
        as32(segment),
    )


def split(x):
    high = x.astype(BF16)
    return high, (x - high.astype(F32)).astype(BF16)


def split3(x):
    high = x.astype(BF16)
    rest = x - high.astype(F32)
    mid = rest.astype(BF16)
    return high, mid, (rest - mid.astype(F32)).astype(BF16)


def dot(a, b, dims=NN):
    return lax.dot_general(a, b, dims, preferred_element_type=F32)


def parts6(x):
    high, mid, low = split3(x)
    return jnp.concatenate([high, high, high, mid, mid, low], axis=1)


def parts3(x):
    high, low = split(x)
    return jnp.concatenate([high, high, low], axis=1)


def dot3(x, w):
    return dot(parts3(x), w[...])


def trade(left, right):
    half = LANES // 2
    low = lax.broadcasted_iota(jnp.int32, left.shape, 1) < half
    first = jnp.where(low, left, pltpu.roll(right, half, 1))
    second = jnp.where(low, pltpu.roll(left, half, 1), right)
    return first, second


def exact(a, b):
    return lax.dot_general(a, b, NN, precision=lax.Precision.HIGHEST, preferred_element_type=F32)


def kernel(
    nxp,
    nyp,
    chunks,
    mean_h,
    scale_h,
    noise_h,
    prev_h,
    now_h,
    anext_h,
    anow_h,
    *rest,
):
    small_h, rest = rest[:SMALL], rest[SMALL:]
    (wave_o, adj_o, sample_o, lgrad_o, irecv), rest = rest[:5], rest[5:]
    small, rest = rest[:SMALL], rest[SMALL:]
    (src_row, rec_row, observed, step, prior) = small[:5]
    (along_z, faces, cas_z, cas_y, line_tab, seg_tab) = small[5:]
    (
        mean,
        logs,
        noise,
        prev,
        anext,
        anow,
        wpad,
        bpad,
        curl,
        acurl,
        speed,
        xrecv,
        ysend,
        yrecv,
        zsend,
        zrecv,
        lines,
        isend,
        msend,
        mrecv,
        rsend,
        rrecv,
        hits,
        lsem,
        tsem,
        osem,
        xs,
        xr,
        ys,
        yr,
        zs,
        zr,
        ms,
        mr,
        rs,
        rr,
        vs,
        vr,
        vsem,
    ) = rest
    bx, by, nz = mean.shape
    gx, gy = lax.axis_index("gx"), lax.axis_index("gy")
    pairs = bx * by // LANES
    pair = LANES // by
    share = nz // nyp
    sub = share // chunks
    total_y = by * nyp
    tiles = total_y // LANES
    rows = sub * tiles // nxp
    cells = bx * by
    centre = pl.ds(PAD, by)

    loads = [
        pltpu.make_async_copy(now_h, wpad.at[:, centre, :], lsem.at[0]),
        pltpu.make_async_copy(scale_h, logs, lsem.at[1]),
        pltpu.make_async_copy(noise_h, noise, lsem.at[2]),
        pltpu.make_async_copy(mean_h, mean, lsem.at[3]),
        pltpu.make_async_copy(anow_h, anow, lsem.at[4]),
        pltpu.make_async_copy(prev_h, prev, lsem.at[5]),
        pltpu.make_async_copy(anext_h, anext, lsem.at[6]),
    ]
    for load in loads:
        load.start()
    small_loads = [
        pltpu.make_async_copy(small_h[i], small[i], tsem.at[i]) for i in range(SMALL)
    ]
    for load in small_loads:
        load.start()

    for padded in (wpad, bpad):
        padded[:, 0:PAD, :] = jnp.zeros((bx, PAD, nz), F32)
        padded[:, PAD + by : by + 2 * PAD, :] = jnp.zeros((bx, PAD, nz), F32)
    outside = ((gx == 0, gx == nxp - 1), (gy == 0, gy == nyp - 1))
    for side in range(2):

        @pl.when(outside[0][side])
        def _():
            for field in range(2):
                xrecv[field, side] = jnp.zeros(xrecv.shape[2:], F32)

        @pl.when(outside[1][side])
        def _():
            for field in range(2):
                yrecv[field, side] = jnp.zeros(yrecv.shape[2:], F32)

    barrier = pltpu.get_barrier_semaphore()
    for i in range(1, nxp):
        pl.semaphore_signal(
            barrier, inc=1, device_id={"gx": lax.rem(gx + i, nxp)}, device_id_type=MESH
        )
    for i in range(1, nyp):
        pl.semaphore_signal(
            barrier, inc=1, device_id={"gy": lax.rem(gy + i, nyp)}, device_id_type=MESH
        )
    pl.semaphore_wait(barrier, nxp + nyp - 2)

    def rim_copy(axis, field, side, src):
        me, count = ((gx, nxp), (gy, nyp))[axis]
        target = lax.rem(me + (1 if side == 0 else count - 1), count)
        land, send, recv = ((xrecv, xs, xr), (yrecv, ys, yr))[axis]
        return pltpu.make_async_remote_copy(
            src_ref=src,
            dst_ref=land.at[field, side],
            send_sem=send.at[field, side],
            recv_sem=recv.at[field, side],
            device_id={("gx", "gy")[axis]: target},
            device_id_type=MESH,
        )

    def start_rim(axis, field, side, src):
        copy = rim_copy(axis, field, side, src)

        @pl.when(jnp.logical_not(outside[axis][1 - side]))
        def _():
            copy.start()

        return (axis, side, copy)

    rims = []
    rims.append(start_rim(0, 0, 0, now_h.at[pl.ds(bx - REACH, REACH)]))
    rims.append(start_rim(0, 0, 1, now_h.at[pl.ds(0, REACH)]))

    def pack_faces(field, padded):
        for x in range(bx):
            here = pl.ds(REACH * x, REACH)
            ysend[field, 0, here, :] = padded[x, PAD + by - REACH : PAD + by, :]
            ysend[field, 1, here, :] = padded[x, PAD : PAD + REACH, :]
        for side in range(2):
            rims.append(start_rim(1, field, side, ysend.at[field, side]))

    loads[0].wait()
    pack_faces(0, wpad)
    small_loads[0].wait()
    small_loads[1].wait()

    def codes(points):
        across = points[0:1, :] - gx * bx
        lateral = points[1:2, :] - gy * by
        inside = (across >= 0) & (across < bx) & (lateral >= 0) & (lateral < by)
        return jnp.where(inside, across * by + lateral, -1)

    src_code = codes(src_row)
    rec_code = codes(rec_row)

    nsrc, nrec = src_row.shape[1], rec_row.shape[1]
    src_level = lax.broadcasted_iota(jnp.int32, (nz, nsrc), 0) == src_row[2:3, :]
    src_level = src_level.astype(F32).astype(BF16)
    rec_level = lax.broadcasted_iota(jnp.int32, (nz, nrec), 0) == rec_row[2:3, :]
    rec_level = rec_level.astype(F32)
    level3 = jnp.concatenate([rec_level.astype(BF16)] * 3, axis=0)
    step_x = 4
    block = step_x * by
    for x0 in range(0, bx, step_x):
        cell = lax.broadcasted_iota(jnp.int32, (block, nrec), 0) + x0 * by
        hits[x0 * by : x0 * by + block, :] = (cell == rec_code).astype(F32).astype(BF16)

    for load in loads[1:5]:
        load.wait()

    def pointwise(x):
        turned = jnp.exp(logs[x]) * noise[x]
        sample = mean[x] + turned
        logs[x] = turned
        mean[x] = sample
        fast = COURANT_SQUARED * jnp.exp(2.0 * VELOCITY_GAIN * sample)
        speed[x] = fast
        bpad[x, centre, :] = fast * anow[x]

    for x in range(REACH):
        pointwise(x)
    rims.append(start_rim(0, 1, 1, bpad.at[pl.ds(0, REACH), centre, :]))
    for x in range(bx - REACH, bx):
        pointwise(x)
    rims.append(start_rim(0, 1, 0, bpad.at[pl.ds(bx - REACH, REACH), centre, :]))
    for x in range(REACH, bx - REACH):
        pointwise(x)
    pack_faces(1, bpad)

    def inner_laplacian(padded, out):
        for x0 in range(0, bx, REACH):
            block = padded[x0 : x0 + REACH, PAD : PAD + by, :].reshape(REACH * by, nz)
            depthwise = dot(parts6(block), along_z[...]).reshape(REACH, by, nz)
            for x in range(x0, x0 + REACH):
                total = depthwise[x - x0] + 3.0 * STENCIL_WEIGHTS[0] * padded[x, centre, :]
                for o in range(1, REACH + 1):
                    near = padded[x, PAD + o : PAD + o + by, :] + padded[x, PAD - o : PAD - o + by, :]
                    if x + o < bx:
                        near = near + padded[x + o, centre, :]
                    if x - o >= 0:
                        near = near + padded[x - o, centre, :]
                    total = total + STENCIL_WEIGHTS[o] * near
                out[x] = total

    for load in small_loads[2:]:
        load.wait()
    inner_laplacian(wpad, curl)

    def rim_terms(field, out):
        for side in range(2):
            terms = exact(faces[side], yrecv[field, side])
            first = 0 if side == 0 else by - REACH
            for x in range(bx):
                here = out[x, first : first + REACH, :]
                out[x, first : first + REACH, :] = here + terms[REACH * x : REACH * (x + 1), :]

    def x_rim(field, x):
        total = None
        for o in range(1, REACH + 1):
            if x - o < 0:
                term = STENCIL_WEIGHTS[o] * xrecv[field, 0, REACH + x - o]
                total = term if total is None else total + term
            if x + o >= bx:
                term = STENCIL_WEIGHTS[o] * xrecv[field, 1, x + o - bx]
                total = term if total is None else total + term
        return total

    def wait_rims(field_rims):
        for axis, side, copy in field_rims:

            @pl.when(jnp.logical_not(outside[axis][side]))
            def _():
                copy.wait_recv()

    inner_laplacian(bpad, acurl)
    loads[5].wait()
    loads[6].wait()

    wave_rims = rims[0:4]
    adj_rims = rims[4:8]
    wait_rims(wave_rims)
    rim_terms(0, curl)
    for x in range(bx):
        curved = curl[x]
        extra = x_rim(0, x)
        if extra is not None:
            curved = curved + extra
            curl[x] = curved
        prev[x] = 2.0 * wpad[x, centre, :] - prev[x] + speed[x] * curved

    moment = (step[...] - NSTEPS // 2).astype(F32) * (math.pi * PULSE_FREQUENCY)
    pulse = PULSE_AMPLITUDE * (1.0 - 2.0 * moment * moment) * jnp.exp(-moment * moment)
    picked = jnp.zeros((1, nrec), F32)
    for x0 in range(0, bx, step_x):
        cell = lax.broadcasted_iota(jnp.int32, (block, nsrc), 0) + x0 * by
        hit = (cell == src_code).astype(F32).astype(BF16)
        wave = prev[x0 : x0 + step_x].reshape(block, nz) + pulse * dot(hit, src_level, NT)
        prev[x0 : x0 + step_x] = wave.reshape(step_x, by, nz)
        traces = dot(jnp.concatenate(split3(wave), axis=1), level3)
        hit = hits[x0 * by : x0 * by + block, :].astype(F32)
        picked = picked + jnp.sum(
            hit * traces, axis=0, keepdims=True
        )
    wave_out = pltpu.make_async_copy(prev, wave_o, osem.at[0])
    wave_out.start()
    misfit = picked - observed[...]

    wait_rims(adj_rims)
    rim_terms(1, acurl)
    misfit3 = jnp.concatenate(split3(rec_level * misfit), axis=1)

    cas_side = jnp.concatenate([cas_z[nz * i : nz * (i + 1), :] for i in range(3)], axis=1)

    parts = bx // step_x

    def z_copy(c, i, part):
        to = lax.rem(gy + i, nyp)
        first = pl.multiple_of(to * share + c * sub, sub)
        across = pl.ds(0, cells) if part is None else pl.ds(part * block, block)
        slot = 0 if part is None else part
        return pltpu.make_async_remote_copy(
            src_ref=zsend.at[pl.ds(first, sub), across],
            dst_ref=zrecv.at[c, gy, :, across],
            send_sem=zs.at[c, slot, i],
            recv_sem=zr.at[c, slot, i],
            device_id={"gy": to},
            device_id_type=MESH,
        )

    def own_z(c):
        zrecv[c, gy] = zsend[pl.ds(pl.multiple_of(gy * share + c * sub, sub), sub), :]

    z_copies = [
        [z_copy(c, i, part) for part in (range(parts) if c == 0 else (None,)) for i in range(1, nyp)]
        for c in range(chunks)
    ]
    for x0 in range(0, bx, step_x):
        hit = hits[x0 * by : x0 * by + block, :]
        added = dot(jnp.concatenate([hit] * 3, axis=1), misfit3, NT).reshape(step_x, by, nz)
        for x in range(x0, x0 + step_x):
            total = acurl[x]
            extra = x_rim(1, x)
            if extra is not None:
                total = total + extra
            adjoint = 2.0 * anow[x] - anext[x] + total + added[x - x0]
            anext[x] = adjoint
            grad = (2.0 * VELOCITY_GAIN) * speed[x] * adjoint * curl[x]
            acurl[x] = grad

        zsend[:, x0 * by : x0 * by + block] = dot(
            cas_side, parts3(acurl[x0 : x0 + step_x].reshape(block, nz)), NT
        )
        part = x0 // step_x
        for copy in z_copies[0][part * (nyp - 1) : (part + 1) * (nyp - 1)]:
            copy.start()

    for copies in z_copies[1:]:
        for copy in copies:
            copy.start()

    adj_out = pltpu.make_async_copy(anext, adj_o, osem.at[1])
    adj_out.start()
    for x in range(bx):
        anow[x] = acurl[x] * logs[x] - 1.0
    lgrad_out = pltpu.make_async_copy(anow, lgrad_o, osem.at[2])
    lgrad_out.start()
    sample_out = pltpu.make_async_copy(mean, sample_o, osem.at[3])
    sample_out.start()
    for c in range(chunks):
        own_z(c)

    def ratio(c):
        return line_tab[0, gy, c * sub : (c + 1) * sub, :]

    def at(c, x):
        return lines[c, x * sub : (x + 1) * sub, :]

    def segment(o):
        return (
            slice((o // tiles) * rows, (o // tiles + 1) * rows),
            slice((o % tiles) * LANES, (o % tiles + 1) * LANES),
        )

    def small_copy(src, dst, send, recv, c, i):
        to = lax.rem(gx + i, nxp)
        return pltpu.make_async_remote_copy(
            src_ref=src.at[c, to],
            dst_ref=dst.at[c, gx],
            send_sem=send.at[c, i],
            recv_sem=recv.at[c, i],
            device_id={"gx": to},
            device_id_type=MESH,
        )

    m_copies, r_copies, v_copies, own_fields = [], [], [], []

    def lateral(c):
        for copy in z_copies[c]:
            copy.wait_recv()
        rows_of = [[] for _ in range(bx)]
        for j in range(pairs):
            here = [zrecv[c, p, :, LANES * j : LANES * (j + 1)] for p in range(nyp)]
            for p in range(0, nyp, 2):
                first, second = trade(here[p], here[p + 1])
                rows_of[2 * j].append(first)
                rows_of[2 * j + 1].append(second)
        block = jnp.concatenate([jnp.concatenate(row, axis=1) for row in rows_of], axis=0)
        lines[c] = dot3(block, cas_y)
        r = ratio(c)
        up = at(c, 0)
        down = at(c, bx - 1)
        for x in range(1, bx):
            up = at(c, x) + r * up
            down = at(c, bx - 1 - x) + r * down
        for o in range(nxp):
            here = segment(o)
            msend[c, o, 0:rows, :] = up[here]
            msend[c, o, rows : 2 * rows, :] = down[here]
        copies = [small_copy(msend, mrecv, ms, mr, c, i) for i in range(1, nxp)]
        for copy in copies:
            copy.start()
        mrecv[c, gx] = msend[c, gx]
        m_copies.append(copies)

    def close(c):
        for copy in m_copies[c]:
            copy.wait_recv()
        decay = seg_tab[gy, c, gx, 0]
        closure = seg_tab[gy, c, gx, 1]
        ups = [mrecv[c, d, 0:rows, :] for d in range(nxp)]
        downs = [mrecv[c, d, rows : 2 * rows, :] for d in range(nxp)]
        up, down = ups[0], downs[nxp - 1]
        for d in range(1, nxp):
            up = ups[d] + decay * up
            down = downs[nxp - 1 - d] + decay * down
        up = up * closure
        down = down * closure
        for d in range(nxp):
            rsend[c, d, 0:rows, :] = up
            up = ups[d] + decay * up
        for d in range(nxp - 1, -1, -1):
            rsend[c, d, rows : 2 * rows, :] = down
            down = downs[d] + decay * down
        copies = [small_copy(rsend, rrecv, rs, rr, c, i) for i in range(1, nxp)]
        for copy in copies:
            copy.start()
        rrecv[c, gx] = rsend[c, gx]
        r_copies.append(copies)

    def back(c):
        for copy in r_copies[c]:
            copy.wait_recv()

        def whole(first):
            return jnp.concatenate(
                [
                    jnp.concatenate(
                        [rrecv[c, i * tiles + t, first : first + rows, :] for t in range(tiles)],
                        axis=1,
                    )
                    for i in range(nxp // tiles)
                ],
                axis=0,
            )

        r = ratio(c)
        gain = line_tab[1, gy, c * sub : (c + 1) * sub, :] * prior[...]
        up, down = whole(0), whole(rows)
        ups = []
        for x in range(bx):
            up = at(c, x) + r * up
            ups.append(up)
        for x in range(bx - 1, -1, -1):
            ahead = r * down
            here = at(c, x)
            down = here + ahead
            lines[c, x * sub : (x + 1) * sub, :] = gain * (ups[x] + ahead)
        out = dot3(lines[c], cas_y)
        for j in range(pairs):
            one = out[2 * j * sub : (2 * j + 1) * sub, :]
            two = out[(2 * j + 1) * sub : (2 * j + 2) * sub, :]
            for p in range(0, nyp, 2):
                here = slice(p * by, (p + 2) * by)
                first, second = trade(one[:, here], two[:, here])
                isend[c, p, sub * j : sub * (j + 1), :] = first
                isend[c, p + 1, sub * j : sub * (j + 1), :] = second
        copies = []
        for i in range(1, nyp):
            to = lax.rem(gy + i, nyp)
            copies.append(
                pltpu.make_async_remote_copy(
                    src_ref=isend.at[c, to],
                    dst_ref=irecv.at[c, gy],
                    send_sem=vs.at[c, i],
                    recv_sem=vr.at[c, i],
                    device_id={"gy": to},
                    device_id_type=MESH,
                )
            )
        for copy in copies:
            copy.start()
        own = pltpu.make_async_copy(isend.at[c, gy], irecv.at[c, gy], vsem.at[c])
        own.start()
        own_fields.append(own)
        v_copies.append(copies)

    for stage in range(chunks + 2):
        if stage >= 2:
            back(stage - 2)
        if 1 <= stage <= chunks:
            close(stage - 1)
        if stage < chunks:
            lateral(stage)

    for c in range(chunks):
        for copy in v_copies[c]:
            copy.wait_recv()
    for own in own_fields:
        own.wait()
    for axis, side, copy in rims:

        @pl.when(jnp.logical_not(outside[axis][1 - side]))
        def _():
            copy.wait_send()

    for group in (z_copies, m_copies, r_copies, v_copies):
        for copies in group:
            for copy in copies:
                copy.wait_send()
    wave_out.wait()
    adj_out.wait()
    lgrad_out.wait()
    sample_out.wait()


def finish(
    wave,
    adjoint,
    sample_h,
    lgrad,
    field_h,
    cas_h,
    wave_o,
    adj_o,
    search_o,
    lgrad_o,
    sample,
    field,
    cas_z,
    search,
    kept,
    sem,
    out_sem,
):
    bx, by, nz = sample.shape
    pair = LANES // by
    pairs = bx // pair
    chunks, nyp, height, _ = field.shape
    sub = height // pairs
    copies = [
        pltpu.make_async_copy(field_h, field, sem.at[0]),
        pltpu.make_async_copy(cas_h, cas_z, sem.at[1]),
        pltpu.make_async_copy(sample_h, sample, sem.at[2]),
        pltpu.make_async_copy(wave, kept.at[0], sem.at[3]),
        pltpu.make_async_copy(adjoint, kept.at[1], sem.at[4]),
        pltpu.make_async_copy(lgrad, kept.at[2], sem.at[5]),
    ]
    for copy in copies:
        copy.start()
    outs = []
    for copy in copies[:3]:
        copy.wait()
    for j in range(pairs):
        spectrum = jnp.concatenate(
            [field[c, p, sub * j : sub * (j + 1), :] for p in range(nyp) for c in range(chunks)],
            axis=0,
        )
        smooth = dot3(spectrum.T, cas_z).reshape(pair, by, nz)
        here = pl.ds(pair * j, pair)
        search[here] = sample[here] + smooth
        out = pltpu.make_async_copy(search.at[here], search_o.at[here], out_sem.at[j])
        out.start()
        outs.append(out)
        if j < 3:
            copies[3 + j].wait()
            out = pltpu.make_async_copy(
                kept.at[j], (wave_o, adj_o, lgrad_o)[j], out_sem.at[pairs + j]
            )
            out.start()
            outs.append(out)
    for out in outs:
        out.wait()


def per_device(
    nxp,
    nyp,
    mean_field,
    log_scale,
    noise,
    wave_prev,
    wave_now,
    adjoint_next,
    adjoint_now,
    sources,
    receivers,
    observed,
    step_index,
    prior_scale,
):
    bx, by, nz = wave_now.shape
    chunks = max(1, min(CHUNKS, nz // nyp // 8))
    constants = tables(bx, by, nz, nxp, nyp, chunks)
    small = [
        sources.T,
        receivers.T,
        observed.reshape(1, -1),
        step_index.reshape(1, 1),
        prior_scale.reshape(1, 1),
    ] + [jnp.asarray(table) for table in constants]
    pairs = bx * by // LANES
    share = nz // nyp
    sub = share // chunks
    total_y = by * nyp
    rows = sub * (total_y // LANES) // nxp
    field = jax.ShapeDtypeStruct((bx, by, nz), F32)
    hbm = pl.BlockSpec(memory_space=pltpu.HBM)
    anywhere = pl.BlockSpec(memory_space=pl.ANY)
    dma = pltpu.SemaphoreType.DMA
    whole = pltpu.VMEM((bx, by, nz), F32)
    padded = pltpu.VMEM((bx, by + 2 * PAD, nz), F32)
    scratch = [pltpu.VMEM(a.shape, a.dtype) for a in small]
    scratch += [whole] * 6 + [padded] * 2 + [whole] * 3
    scratch += [
        pltpu.VMEM((2, 2, REACH, by, nz), F32),
        pltpu.VMEM((2, 2, REACH * bx, nz), F32),
        pltpu.VMEM((2, 2, REACH * bx, nz), F32),
        pltpu.VMEM((nz, bx * by), F32),
        pltpu.VMEM((chunks, nyp, sub, bx * by), F32),
        pltpu.VMEM((chunks, bx * sub, total_y), F32),
        pltpu.VMEM((chunks, nyp, pairs * sub, LANES), F32),
        pltpu.VMEM((chunks, nxp, 2 * rows, LANES), F32),
        pltpu.VMEM((chunks, nxp, 2 * rows, LANES), F32),
        pltpu.VMEM((chunks, nxp, 2 * rows, LANES), F32),
        pltpu.VMEM((chunks, nxp, 2 * rows, LANES), F32),
        pltpu.VMEM((bx * by, receivers.shape[0]), BF16),
        dma((7,)),
        dma((SMALL,)),
        dma((4,)),
        dma((2, 2)),
        dma((2, 2)),
        dma((2, 2)),
        dma((2, 2)),
    ]
    scratch += [dma((chunks, bx // 4, nyp))] * 2 + [dma((chunks, nxp))] * 4 + [dma((chunks, nyp))] * 2
    scratch += [dma((chunks,))]
    spread = jax.ShapeDtypeStruct((chunks, nyp, pairs * sub, LANES), F32)
    wave, adjoint, sample, lgrad, spectrum = pl.pallas_call(
        functools.partial(kernel, nxp, nyp, chunks),
        out_shape=(field,) * 4 + (spread,),
        in_specs=[hbm] * (7 + len(small)),
        out_specs=(anywhere,) * 5,
        scratch_shapes=scratch,
        compiler_params=pltpu.CompilerParams(
            collective_id=0, has_side_effects=True, vmem_limit_bytes=63 * 2**20
        ),
    )(
        mean_field, log_scale, noise, wave_prev, wave_now, adjoint_next, adjoint_now, *small
    )
    return pl.pallas_call(
        finish,
        out_shape=(field,) * 4,
        in_specs=[anywhere] * 5 + [hbm],
        out_specs=(hbm,) * 4,
        scratch_shapes=[
            whole,
            pltpu.VMEM(spread.shape, F32),
            pltpu.VMEM(small[7].shape, BF16),
            whole,
            pltpu.VMEM((3, bx, by, nz), F32),
            dma((6,)),
            dma((pairs + 3,)),
        ],
        compiler_params=pltpu.CompilerParams(vmem_limit_bytes=63 * 2**20),
    )(wave, adjoint, sample, lgrad, spectrum, small[7])


def solution(mesh):
    grid = P("gx", "gy", None)
    return jax.shard_map(
        functools.partial(per_device, mesh.shape["gx"], mesh.shape["gy"]),
        mesh=mesh,
        in_specs=(grid,) * 7 + (P(),) * 5,
        out_specs=(grid,) * 4,
        check_vma=False,
    )
```

```python
import functools
import math

import jax
import jax.numpy as jnp
import ml_dtypes
import numpy as np
from jax import lax
from jax.experimental import pallas as pl
from jax.experimental.pallas import tpu as pltpu
from jax.sharding import PartitionSpec as P

NSTEPS = 48
STENCIL_WEIGHTS = (-205.0 / 72.0, 8.0 / 5.0, -1.0 / 5.0, 8.0 / 315.0, -1.0 / 560.0)
COURANT_SQUARED = 0.08
VELOCITY_GAIN = 0.2
PULSE_FREQUENCY = 0.05
PULSE_AMPLITUDE = 20.0

REACH = 4
PAD = 8
LANES = 128
CHUNKS = 2
SMALL = 11
MESH = pl.DeviceIdType.MESH
F32 = jnp.float32
BF16 = jnp.bfloat16
NN = (((1,), (0,)), ((), ()))
NT = (((1,), (1,)), ((), ()))


def halves(table):
    high = table.astype(ml_dtypes.bfloat16)
    low = (table - high.astype(np.float64)).astype(ml_dtypes.bfloat16)
    return np.concatenate([high, low, high])


def thirds(table):
    parts = []
    for _ in range(3):
        part = table.astype(ml_dtypes.bfloat16)
        table = table - part.astype(np.float64)
        parts.append(part)
    high, mid, low = parts
    return np.concatenate([high, mid, low, high, mid, high])


def cas(length):
    index = np.arange(length)
    angle = (index[:, None] * index[None, :] % length) * (2.0 * math.pi / length)
    return np.cos(angle) + np.sin(angle)


def wave_term(length):
    return (length / 8.0) ** 2 * 4.0 * np.sin(np.arange(length) * (math.pi / length)) ** 2


def tables(bx, by, nz, nxp, nyp, chunks):
    total_x, total_y = bx * nxp, by * nyp
    along_z = np.zeros((nz, nz))
    for o in range(1, REACH + 1):
        along_z += STENCIL_WEIGHTS[o] * (np.eye(nz, k=o) + np.eye(nz, k=-o))
    face_low = np.zeros((REACH, REACH))
    face_high = np.zeros((REACH, REACH))
    for i in range(REACH):
        for h in range(REACH):
            if h >= i:
                face_low[i, h] = STENCIL_WEIGHTS[i + REACH - h]
            if h <= i:
                face_high[i, h] = STENCIL_WEIGHTS[REACH + h - i]
    faces = np.stack([np.kron(np.eye(bx), face_low), np.kron(np.eye(bx), face_high)])
    c = (total_x / 8.0) ** 2
    d = 1.0 + wave_term(nz)[:, None] + wave_term(total_y)[None, :]
    log_r = -2.0 * np.arcsinh(0.5 * np.sqrt(d / c))
    r = np.exp(log_r)
    scale = math.sqrt(total_x * total_y * nz) / 8.0 / (nz * total_y)
    scale = scale / (c * -2.0 * np.sinh(log_r))
    closure = 1.0 / -np.expm1(total_x * log_r)
    share = nz // nyp
    sub = share // chunks
    tiles = total_y // LANES
    rows = sub * tiles // nxp
    segment = np.stack([np.exp(bx * log_r), closure])
    segment = segment.reshape(2, nyp, chunks, nxp // tiles, rows, tiles, LANES)
    segment = segment.transpose(1, 2, 3, 5, 0, 4, 6).reshape(nyp, chunks, nxp, 2, rows, LANES)
    as32 = lambda a: np.ascontiguousarray(a).astype(np.float32)
    return (
        thirds(along_z),
        as32(faces),
        halves(cas(nz)),
        halves(cas(total_y)),
        as32(np.stack([r, scale]).reshape(2, nyp, share, total_y)),
        as32(segment),
    )


def split(x):
    high = x.astype(BF16)
    return high, (x - high.astype(F32)).astype(BF16)


def split3(x):
    high = x.astype(BF16)
    rest = x - high.astype(F32)
    mid = rest.astype(BF16)
    return high, mid, (rest - mid.astype(F32)).astype(BF16)


def dot(a, b, dims=NN):
    return lax.dot_general(a, b, dims, preferred_element_type=F32)


def parts6(x):
    high, mid, low = split3(x)
    return jnp.concatenate([high, high, high, mid, mid, low], axis=1)


def parts3(x):
    high, low = split(x)
    return jnp.concatenate([high, high, low], axis=1)


def dot3(x, w):
    return dot(parts3(x), w[...])


def trade(left, right):
    half = LANES // 2
    low = lax.broadcasted_iota(jnp.int32, left.shape, 1) < half
    first = jnp.where(low, left, pltpu.roll(right, half, 1))
    second = jnp.where(low, pltpu.roll(left, half, 1), right)
    return first, second


def exact(a, b):
    return lax.dot_general(a, b, NN, precision=lax.Precision.HIGHEST, preferred_element_type=F32)


def kernel(
    nxp,
    nyp,
    chunks,
    mean_h,
    scale_h,
    noise_h,
    prev_h,
    now_h,
    anext_h,
    anow_h,
    *rest,
):
    small_h, rest = rest[:SMALL], rest[SMALL:]
    (wave_o, adj_o, sample_o, lgrad_o, irecv), rest = rest[:5], rest[5:]
    small, rest = rest[:SMALL], rest[SMALL:]
    (src_row, rec_row, observed, step, prior) = small[:5]
    (along_z, faces, cas_z, cas_y, line_tab, seg_tab) = small[5:]
    (
        mean,
        logs,
        noise,
        prev,
        anext,
        anow,
        wpad,
        bpad,
        curl,
        acurl,
        speed,
        xrecv,
        ysend,
        yrecv,
        zsend,
        zrecv,
        lines,
        isend,
        msend,
        mrecv,
        rsend,
        rrecv,
        hits,
        lsem,
        tsem,
        osem,
        xs,
        xr,
        ys,
        yr,
        zs,
        zr,
        ms,
        mr,
        rs,
        rr,
        vs,
        vr,
        vsem,
    ) = rest
    bx, by, nz = mean.shape
    gx, gy = lax.axis_index("gx"), lax.axis_index("gy")
    pairs = bx * by // LANES
    pair = LANES // by
    share = nz // nyp
    sub = share // chunks
    total_y = by * nyp
    tiles = total_y // LANES
    rows = sub * tiles // nxp
    cells = bx * by
    centre = pl.ds(PAD, by)

    loads = [
        pltpu.make_async_copy(now_h, wpad.at[:, centre, :], lsem.at[0]),
        pltpu.make_async_copy(scale_h, logs, lsem.at[1]),
        pltpu.make_async_copy(noise_h, noise, lsem.at[2]),
        pltpu.make_async_copy(mean_h, mean, lsem.at[3]),
        pltpu.make_async_copy(anow_h, anow, lsem.at[4]),
        pltpu.make_async_copy(prev_h, prev, lsem.at[5]),
        pltpu.make_async_copy(anext_h, anext, lsem.at[6]),
    ]
    for load in loads:
        load.start()
    small_loads = [
        pltpu.make_async_copy(small_h[i], small[i], tsem.at[i]) for i in range(SMALL)
    ]
    for load in small_loads:
        load.start()

    for padded in (wpad, bpad):
        padded[:, 0:PAD, :] = jnp.zeros((bx, PAD, nz), F32)
        padded[:, PAD + by : by + 2 * PAD, :] = jnp.zeros((bx, PAD, nz), F32)
    outside = ((gx == 0, gx == nxp - 1), (gy == 0, gy == nyp - 1))
    for side in range(2):

        @pl.when(outside[0][side])
        def _():
            for field in range(2):
                xrecv[field, side] = jnp.zeros(xrecv.shape[2:], F32)

        @pl.when(outside[1][side])
        def _():
            for field in range(2):
                yrecv[field, side] = jnp.zeros(yrecv.shape[2:], F32)

    barrier = pltpu.get_barrier_semaphore()
    for i in range(1, nxp):
        pl.semaphore_signal(
            barrier, inc=1, device_id={"gx": lax.rem(gx + i, nxp)}, device_id_type=MESH
        )
    for i in range(1, nyp):
        pl.semaphore_signal(
            barrier, inc=1, device_id={"gy": lax.rem(gy + i, nyp)}, device_id_type=MESH
        )
    pl.semaphore_wait(barrier, nxp + nyp - 2)

    def rim_copy(axis, field, side, src):
        me, count = ((gx, nxp), (gy, nyp))[axis]
        target = lax.rem(me + (1 if side == 0 else count - 1), count)
        land, send, recv = ((xrecv, xs, xr), (yrecv, ys, yr))[axis]
        return pltpu.make_async_remote_copy(
            src_ref=src,
            dst_ref=land.at[field, side],
            send_sem=send.at[field, side],
            recv_sem=recv.at[field, side],
            device_id={("gx", "gy")[axis]: target},
            device_id_type=MESH,
        )

    def start_rim(axis, field, side, src):
        copy = rim_copy(axis, field, side, src)

        @pl.when(jnp.logical_not(outside[axis][1 - side]))
        def _():
            copy.start()

        return (axis, side, copy)

    rims = []
    rims.append(start_rim(0, 0, 0, now_h.at[pl.ds(bx - REACH, REACH)]))
    rims.append(start_rim(0, 0, 1, now_h.at[pl.ds(0, REACH)]))

    def pack_faces(field, padded):
        for x in range(bx):
            here = pl.ds(REACH * x, REACH)
            ysend[field, 0, here, :] = padded[x, PAD + by - REACH : PAD + by, :]
            ysend[field, 1, here, :] = padded[x, PAD : PAD + REACH, :]
        for side in range(2):
            rims.append(start_rim(1, field, side, ysend.at[field, side]))

    loads[0].wait()
    pack_faces(0, wpad)
    small_loads[0].wait()
    small_loads[1].wait()

    def codes(points):
        across = points[0:1, :] - gx * bx
        lateral = points[1:2, :] - gy * by
        inside = (across >= 0) & (across < bx) & (lateral >= 0) & (lateral < by)
        return jnp.where(inside, across * by + lateral, -1)

    src_code = codes(src_row)
    rec_code = codes(rec_row)

    nsrc, nrec = src_row.shape[1], rec_row.shape[1]
    src_level = lax.broadcasted_iota(jnp.int32, (nz, nsrc), 0) == src_row[2:3, :]
    src_level = src_level.astype(F32).astype(BF16)
    rec_level = lax.broadcasted_iota(jnp.int32, (nz, nrec), 0) == rec_row[2:3, :]
    rec_level = rec_level.astype(F32)
    level3 = jnp.concatenate([rec_level.astype(BF16)] * 3, axis=0)
    step_x = 4
    block = step_x * by
    for x0 in range(0, bx, step_x):
        cell = lax.broadcasted_iota(jnp.int32, (block, nrec), 0) + x0 * by
        hits[x0 * by : x0 * by + block, :] = (cell == rec_code).astype(F32).astype(BF16)

    for load in loads[1:5]:
        load.wait()

    def pointwise(x):
        turned = jnp.exp(logs[x]) * noise[x]
        sample = mean[x] + turned
        logs[x] = turned
        mean[x] = sample
        fast = COURANT_SQUARED * jnp.exp(2.0 * VELOCITY_GAIN * sample)
        speed[x] = fast
        bpad[x, centre, :] = fast * anow[x]

    for x in range(REACH):
        pointwise(x)
    rims.append(start_rim(0, 1, 1, bpad.at[pl.ds(0, REACH), centre, :]))
    for x in range(bx - REACH, bx):
        pointwise(x)
    rims.append(start_rim(0, 1, 0, bpad.at[pl.ds(bx - REACH, REACH), centre, :]))
    for x in range(REACH, bx - REACH):
        pointwise(x)
    pack_faces(1, bpad)

    def inner_laplacian(padded, out):
        for x0 in range(0, bx, REACH):
            block = padded[x0 : x0 + REACH, PAD : PAD + by, :].reshape(REACH * by, nz)
            depthwise = dot(parts6(block), along_z[...]).reshape(REACH, by, nz)
            for x in range(x0, x0 + REACH):
                total = depthwise[x - x0] + 3.0 * STENCIL_WEIGHTS[0] * padded[x, centre, :]
                for o in range(1, REACH + 1):
                    near = padded[x, PAD + o : PAD + o + by, :] + padded[x, PAD - o : PAD - o + by, :]
                    if x + o < bx:
                        near = near + padded[x + o, centre, :]
                    if x - o >= 0:
                        near = near + padded[x - o, centre, :]
                    total = total + STENCIL_WEIGHTS[o] * near
                out[x] = total

    for load in small_loads[2:]:
        load.wait()
    inner_laplacian(wpad, curl)

    def rim_terms(field, out):
        for side in range(2):
            terms = exact(faces[side], yrecv[field, side])
            first = 0 if side == 0 else by - REACH
            for x in range(bx):
                here = out[x, first : first + REACH, :]
                out[x, first : first + REACH, :] = here + terms[REACH * x : REACH * (x + 1), :]

    def x_rim(field, x):
        total = None
        for o in range(1, REACH + 1):
            if x - o < 0:
                term = STENCIL_WEIGHTS[o] * xrecv[field, 0, REACH + x - o]
                total = term if total is None else total + term
            if x + o >= bx:
                term = STENCIL_WEIGHTS[o] * xrecv[field, 1, x + o - bx]
                total = term if total is None else total + term
        return total

    def wait_rims(field_rims):
        for axis, side, copy in field_rims:

            @pl.when(jnp.logical_not(outside[axis][side]))
            def _():
                copy.wait_recv()

    inner_laplacian(bpad, acurl)
    loads[5].wait()
    loads[6].wait()

    wave_rims = rims[0:4]
    adj_rims = rims[4:8]
    wait_rims(wave_rims)
    rim_terms(0, curl)
    for x in range(bx):
        curved = curl[x]
        extra = x_rim(0, x)
        if extra is not None:
            curved = curved + extra
            curl[x] = curved
        prev[x] = 2.0 * wpad[x, centre, :] - prev[x] + speed[x] * curved

    moment = (step[...] - NSTEPS // 2).astype(F32) * (math.pi * PULSE_FREQUENCY)
    pulse = PULSE_AMPLITUDE * (1.0 - 2.0 * moment * moment) * jnp.exp(-moment * moment)
    picked = jnp.zeros((1, nrec), F32)
    for x0 in range(0, bx, step_x):
        cell = lax.broadcasted_iota(jnp.int32, (block, nsrc), 0) + x0 * by
        hit = (cell == src_code).astype(F32).astype(BF16)
        wave = prev[x0 : x0 + step_x].reshape(block, nz) + pulse * dot(hit, src_level, NT)
        prev[x0 : x0 + step_x] = wave.reshape(step_x, by, nz)
        traces = dot(jnp.concatenate(split3(wave), axis=1), level3)
        hit = hits[x0 * by : x0 * by + block, :].astype(F32)
        picked = picked + jnp.sum(
            hit * traces, axis=0, keepdims=True
        )
    wave_out = pltpu.make_async_copy(prev, wave_o, osem.at[0])
    wave_out.start()
    misfit = picked - observed[...]

    wait_rims(adj_rims)
    rim_terms(1, acurl)
    misfit3 = jnp.concatenate(split3(rec_level * misfit), axis=1)

    cas_side = jnp.concatenate([cas_z[nz * i : nz * (i + 1), :] for i in range(3)], axis=1)

    parts = bx // step_x

    def z_copy(c, i, part):
        to = lax.rem(gy + i, nyp)
        first = pl.multiple_of(to * share + c * sub, sub)
        across = pl.ds(0, cells) if part is None else pl.ds(part * block, block)
        slot = 0 if part is None else part
        return pltpu.make_async_remote_copy(
            src_ref=zsend.at[pl.ds(first, sub), across],
            dst_ref=zrecv.at[c, gy, :, across],
            send_sem=zs.at[c, slot, i],
            recv_sem=zr.at[c, slot, i],
            device_id={"gy": to},
            device_id_type=MESH,
        )

    def own_z(c):
        zrecv[c, gy] = zsend[pl.ds(pl.multiple_of(gy * share + c * sub, sub), sub), :]

    z_copies = [
        [z_copy(c, i, part) for part in (range(parts) if c == 0 else (None,)) for i in range(1, nyp)]
        for c in range(chunks)
    ]
    for x0 in range(0, bx, step_x):
        hit = hits[x0 * by : x0 * by + block, :]
        added = dot(jnp.concatenate([hit] * 3, axis=1), misfit3, NT).reshape(step_x, by, nz)
        for x in range(x0, x0 + step_x):
            total = acurl[x]
            extra = x_rim(1, x)
            if extra is not None:
                total = total + extra
            adjoint = 2.0 * anow[x] - anext[x] + total + added[x - x0]
            anext[x] = adjoint
            grad = (2.0 * VELOCITY_GAIN) * speed[x] * adjoint * curl[x]
            acurl[x] = grad

        zsend[:, x0 * by : x0 * by + block] = dot(
            cas_side, parts3(acurl[x0 : x0 + step_x].reshape(block, nz)), NT
        )
        part = x0 // step_x
        for copy in z_copies[0][part * (nyp - 1) : (part + 1) * (nyp - 1)]:
            copy.start()

    for copies in z_copies[1:]:
        for copy in copies:
            copy.start()

    adj_out = pltpu.make_async_copy(anext, adj_o, osem.at[1])
    adj_out.start()
    for x in range(bx):
        anow[x] = acurl[x] * logs[x] - 1.0
    lgrad_out = pltpu.make_async_copy(anow, lgrad_o, osem.at[2])
    lgrad_out.start()
    sample_out = pltpu.make_async_copy(mean, sample_o, osem.at[3])
    sample_out.start()
    for c in range(chunks):
        own_z(c)

    def ratio(c):
        return line_tab[0, gy, c * sub : (c + 1) * sub, :]

    def at(c, x):
        return lines[c, x * sub : (x + 1) * sub, :]

    def segment(o):
        return (
            slice((o // tiles) * rows, (o // tiles + 1) * rows),
            slice((o % tiles) * LANES, (o % tiles + 1) * LANES),
        )

    def small_copy(src, dst, send, recv, c, i):
        to = lax.rem(gx + i, nxp)
        return pltpu.make_async_remote_copy(
            src_ref=src.at[c, to],
            dst_ref=dst.at[c, gx],
            send_sem=send.at[c, i],
            recv_sem=recv.at[c, i],
            device_id={"gx": to},
            device_id_type=MESH,
        )

    m_copies, r_copies, v_copies, own_fields = [], [], [], []

    def lateral(c):
        for copy in z_copies[c]:
            copy.wait_recv()
        rows_of = [[] for _ in range(bx)]
        for j in range(pairs):
            here = [zrecv[c, p, :, LANES * j : LANES * (j + 1)] for p in range(nyp)]
            for p in range(0, nyp, 2):
                first, second = trade(here[p], here[p + 1])
                rows_of[2 * j].append(first)
                rows_of[2 * j + 1].append(second)
        block = jnp.concatenate([jnp.concatenate(row, axis=1) for row in rows_of], axis=0)
        lines[c] = dot3(block, cas_y)
        r = ratio(c)
        up = at(c, 0)
        down = at(c, bx - 1)
        for x in range(1, bx):
            up = at(c, x) + r * up
            down = at(c, bx - 1 - x) + r * down
        for o in range(nxp):
            here = segment(o)
            msend[c, o, 0:rows, :] = up[here]
            msend[c, o, rows : 2 * rows, :] = down[here]
        copies = [small_copy(msend, mrecv, ms, mr, c, i) for i in range(1, nxp)]
        for copy in copies:
            copy.start()
        mrecv[c, gx] = msend[c, gx]
        m_copies.append(copies)

    def close(c):
        for copy in m_copies[c]:
            copy.wait_recv()
        decay = seg_tab[gy, c, gx, 0]
        closure = seg_tab[gy, c, gx, 1]
        ups = [mrecv[c, d, 0:rows, :] for d in range(nxp)]
        downs = [mrecv[c, d, rows : 2 * rows, :] for d in range(nxp)]
        up, down = ups[0], downs[nxp - 1]
        for d in range(1, nxp):
            up = ups[d] + decay * up
            down = downs[nxp - 1 - d] + decay * down
        up = up * closure
        down = down * closure
        for d in range(nxp):
            rsend[c, d, 0:rows, :] = up
            up = ups[d] + decay * up
        for d in range(nxp - 1, -1, -1):
            rsend[c, d, rows : 2 * rows, :] = down
            down = downs[d] + decay * down
        copies = [small_copy(rsend, rrecv, rs, rr, c, i) for i in range(1, nxp)]
        for copy in copies:
            copy.start()
        rrecv[c, gx] = rsend[c, gx]
        r_copies.append(copies)

    def back(c):
        for copy in r_copies[c]:
            copy.wait_recv()

        def whole(first):
            return jnp.concatenate(
                [
                    jnp.concatenate(
                        [rrecv[c, i * tiles + t, first : first + rows, :] for t in range(tiles)],
                        axis=1,
                    )
                    for i in range(nxp // tiles)
                ],
                axis=0,
            )

        r = ratio(c)
        gain = line_tab[1, gy, c * sub : (c + 1) * sub, :] * prior[...]
        up, down = whole(0), whole(rows)
        ups = []
        for x in range(bx):
            up = at(c, x) + r * up
            ups.append(up)
        for x in range(bx - 1, -1, -1):
            ahead = r * down
            here = at(c, x)
            down = here + ahead
            lines[c, x * sub : (x + 1) * sub, :] = gain * (ups[x] + ahead)
        out = dot3(lines[c], cas_y)
        for j in range(pairs):
            one = out[2 * j * sub : (2 * j + 1) * sub, :]
            two = out[(2 * j + 1) * sub : (2 * j + 2) * sub, :]
            for p in range(0, nyp, 2):
                here = slice(p * by, (p + 2) * by)
                first, second = trade(one[:, here], two[:, here])
                isend[c, p, sub * j : sub * (j + 1), :] = first
                isend[c, p + 1, sub * j : sub * (j + 1), :] = second
        copies = []
        for i in range(1, nyp):
            to = lax.rem(gy + i, nyp)
            copies.append(
                pltpu.make_async_remote_copy(
                    src_ref=isend.at[c, to],
                    dst_ref=irecv.at[c, gy],
                    send_sem=vs.at[c, i],
                    recv_sem=vr.at[c, i],
                    device_id={"gy": to},
                    device_id_type=MESH,
                )
            )
        for copy in copies:
            copy.start()
        own = pltpu.make_async_copy(isend.at[c, gy], irecv.at[c, gy], vsem.at[c])
        own.start()
        own_fields.append(own)
        v_copies.append(copies)

    for stage in (lateral, close, back):
        for c in range(chunks):
            stage(c)

    for c in range(chunks):
        for copy in v_copies[c]:
            copy.wait_recv()
    for own in own_fields:
        own.wait()
    for axis, side, copy in rims:

        @pl.when(jnp.logical_not(outside[axis][1 - side]))
        def _():
            copy.wait_send()

    for group in (z_copies, m_copies, r_copies, v_copies):
        for copies in group:
            for copy in copies:
                copy.wait_send()
    wave_out.wait()
    adj_out.wait()
    lgrad_out.wait()
    sample_out.wait()


def finish(
    wave,
    adjoint,
    sample_h,
    lgrad,
    field_h,
    cas_h,
    wave_o,
    adj_o,
    search_o,
    lgrad_o,
    sample,
    field,
    cas_z,
    search,
    kept,
    sem,
    out_sem,
):
    bx, by, nz = sample.shape
    pair = LANES // by
    pairs = bx // pair
    chunks, nyp, height, _ = field.shape
    sub = height // pairs
    copies = [
        pltpu.make_async_copy(field_h, field, sem.at[0]),
        pltpu.make_async_copy(cas_h, cas_z, sem.at[1]),
        pltpu.make_async_copy(sample_h, sample, sem.at[2]),
        pltpu.make_async_copy(wave, kept.at[0], sem.at[3]),
        pltpu.make_async_copy(adjoint, kept.at[1], sem.at[4]),
        pltpu.make_async_copy(lgrad, kept.at[2], sem.at[5]),
    ]
    for copy in copies:
        copy.start()
    outs = []
    for copy in copies[:3]:
        copy.wait()
    for j in range(pairs):
        spectrum = jnp.concatenate(
            [field[c, p, sub * j : sub * (j + 1), :] for p in range(nyp) for c in range(chunks)],
            axis=0,
        )
        smooth = dot3(spectrum.T, cas_z).reshape(pair, by, nz)
        here = pl.ds(pair * j, pair)
        search[here] = sample[here] + smooth
        out = pltpu.make_async_copy(search.at[here], search_o.at[here], out_sem.at[j])
        out.start()
        outs.append(out)
        if j < 3:
            copies[3 + j].wait()
            out = pltpu.make_async_copy(
                kept.at[j], (wave_o, adj_o, lgrad_o)[j], out_sem.at[pairs + j]
            )
            out.start()
            outs.append(out)
    for out in outs:
        out.wait()


def per_device(
    nxp,
    nyp,
    mean_field,
    log_scale,
    noise,
    wave_prev,
    wave_now,
    adjoint_next,
    adjoint_now,
    sources,
    receivers,
    observed,
    step_index,
    prior_scale,
):
    bx, by, nz = wave_now.shape
    chunks = max(1, min(CHUNKS, nz // nyp // 8))
    constants = tables(bx, by, nz, nxp, nyp, chunks)
    small = [
        sources.T,
        receivers.T,
        observed.reshape(1, -1),
        step_index.reshape(1, 1),
        prior_scale.reshape(1, 1),
    ] + [jnp.asarray(table) for table in constants]
    pairs = bx * by // LANES
    share = nz // nyp
    sub = share // chunks
    total_y = by * nyp
    rows = sub * (total_y // LANES) // nxp
    field = jax.ShapeDtypeStruct((bx, by, nz), F32)
    hbm = pl.BlockSpec(memory_space=pltpu.HBM)
    anywhere = pl.BlockSpec(memory_space=pl.ANY)
    dma = pltpu.SemaphoreType.DMA
    whole = pltpu.VMEM((bx, by, nz), F32)
    padded = pltpu.VMEM((bx, by + 2 * PAD, nz), F32)
    scratch = [pltpu.VMEM(a.shape, a.dtype) for a in small]
    scratch += [whole] * 6 + [padded] * 2 + [whole] * 3
    scratch += [
        pltpu.VMEM((2, 2, REACH, by, nz), F32),
        pltpu.VMEM((2, 2, REACH * bx, nz), F32),
        pltpu.VMEM((2, 2, REACH * bx, nz), F32),
        pltpu.VMEM((nz, bx * by), F32),
        pltpu.VMEM((chunks, nyp, sub, bx * by), F32),
        pltpu.VMEM((chunks, bx * sub, total_y), F32),
        pltpu.VMEM((chunks, nyp, pairs * sub, LANES), F32),
        pltpu.VMEM((chunks, nxp, 2 * rows, LANES), F32),
        pltpu.VMEM((chunks, nxp, 2 * rows, LANES), F32),
        pltpu.VMEM((chunks, nxp, 2 * rows, LANES), F32),
        pltpu.VMEM((chunks, nxp, 2 * rows, LANES), F32),
        pltpu.VMEM((bx * by, receivers.shape[0]), BF16),
        dma((7,)),
        dma((SMALL,)),
        dma((4,)),
        dma((2, 2)),
        dma((2, 2)),
        dma((2, 2)),
        dma((2, 2)),
    ]
    scratch += [dma((chunks, bx // 4, nyp))] * 2 + [dma((chunks, nxp))] * 4 + [dma((chunks, nyp))] * 2
    scratch += [dma((chunks,))]
    spread = jax.ShapeDtypeStruct((chunks, nyp, pairs * sub, LANES), F32)
    wave, adjoint, sample, lgrad, spectrum = pl.pallas_call(
        functools.partial(kernel, nxp, nyp, chunks),
        out_shape=(field,) * 4 + (spread,),
        in_specs=[hbm] * (7 + len(small)),
        out_specs=(anywhere,) * 5,
        scratch_shapes=scratch,
        compiler_params=pltpu.CompilerParams(
            collective_id=0, has_side_effects=True, vmem_limit_bytes=63 * 2**20
        ),
    )(
        mean_field, log_scale, noise, wave_prev, wave_now, adjoint_next, adjoint_now, *small
    )
    return pl.pallas_call(
        finish,
        out_shape=(field,) * 4,
        in_specs=[anywhere] * 5 + [hbm],
        out_specs=(hbm,) * 4,
        scratch_shapes=[
            whole,
            pltpu.VMEM(spread.shape, F32),
            pltpu.VMEM(small[7].shape, BF16),
            whole,
            pltpu.VMEM((3, bx, by, nz), F32),
            dma((6,)),
            dma((pairs + 3,)),
        ],
        compiler_params=pltpu.CompilerParams(vmem_limit_bytes=63 * 2**20),
    )(wave, adjoint, sample, lgrad, spectrum, small[7])


def solution(mesh):
    grid = P("gx", "gy", None)
    return jax.shard_map(
        functools.partial(per_device, mesh.shape["gx"], mesh.shape["gy"]),
        mesh=mesh,
        in_specs=(grid,) * 7 + (P(),) * 5,
        out_specs=(grid,) * 4,
        check_vma=False,
    )
```
